32 devices in a mesh: grp: 4 (over y, x), tok: 8 (over z, core).
Axes of the slice: x: 2, y: 2, z: 4, core: 2. Of those that a mesh axis runs over, the one named last changes fastest.
Arguments:
- tokens_in: bfloat16 [32768, 768], P(('grp', 'tok')), may hold values from -6 to 6
- w_qkv: bfloat16 [768, 2304], replicated, may hold values from -0.3125 to 0.3125
- b_query: bfloat16 [768], replicated, may hold values from -3 to 3
- b_value: bfloat16 [768], replicated, may hold values from -3 to 3
- w_out: bfloat16 [768, 768], replicated, may hold values from -0.875 to 0.875
- b_out: bfloat16 [768], replicated, may hold values from -3 to 3
- norm1_gain: bfloat16 [768], replicated, may hold values from 0.5 to 1.5
- norm1_shift: bfloat16 [768], replicated, may hold values from -2 to 2
- w_up: bfloat16 [768, 3072], replicated, may hold values from -0.21875 to 0.21875
- b_up: bfloat16 [3072], replicated, may hold values from -3 to 3
- w_down: bfloat16 [3072, 768], replicated, may hold values from -0.109375 to 0.109375
- b_down: bfloat16 [768], replicated, may hold values from -3 to 3
- norm2_gain: bfloat16 [768], replicated, may hold values from 0.5 to 1.5
- norm2_shift: bfloat16 [768], replicated, may hold values from -2 to 2
- out_grad: bfloat16 [32768, 768], P(('grp', 'tok')), may hold values from -6 to 6
- doc_lengths: int32 [4, 5], P('grp'), may hold values from 1 to 7680, as said below
- cluster_slots: int32 [32768], P(('grp', 'tok')), may hold values from 0 to 8191, as said below
Outputs:
- block_out: bfloat16 [32768, 768], P(('grp', 'tok'))
- grad_tokens: bfloat16 [32768, 768], P(('grp', 'tok'))
- grad_w_qkv: float32 [768, 2304], P('tok')
- grad_b_query: float32 [768], P('tok')
- grad_b_value: float32 [768], P('tok')
- grad_w_out: float32 [768, 768], P('tok')
- grad_b_out: float32 [768], P('tok')
- grad_norm1_gain: float32 [768], P('tok')
- grad_norm1_shift: float32 [768], P('tok')
- grad_w_up: float32 [768, 3072], P('tok')
- grad_b_up: float32 [3072], P('tok')
- grad_w_down: float32 [3072, 768], P('tok')
- grad_b_down: float32 [768], P('tok')
- grad_norm2_gain: float32 [768], P('tok')
- grad_norm2_shift: float32 [768], P('tok')
The draws below stay inside these ranges and needn't reach their ends.
Inputs may be any that keep to these rules, and one draw needn't show every extreme that they name: `doc_lengths`: in each group the documents, each padded up to a multiple of 128 rows, fill the group's rows exactly; one document of each group has the full length and spans from the group's first device to its last. `cluster_slots`: within each group the slots are a permutation of 0 to the group's rows - 1; the rows of every device of a group go to the slot range s // 1024 of every device of the group in equal numbers, 1024 / 8 each.
All inputs are finite; a program needn't handle non-finite values.
Results may differ from the reference program's by a relative error of at most 0.017.
The reference program's roundings to bfloat16 on the way count: a program that leaves them out, or rounds other values in their place, can miss the bound.
Values may be sent and summed in bfloat16 or wider, within the bound.
A program may use at most 192 MiB of HBM per device.

```python
import jax
import jax.numpy as jnp
from jax import lax

D = 768
H = 12
HD = 64
FF = 3072
CLU = 128
TOK_DEV = 1024
TOKENS = 32768
N_GRP = 4
N_TOK = 8


def distinct_order(key, shape, amount):
    noise = jax.random.randint(key, shape + (amount,), 0, 2 ** 15).astype(jnp.int32)
    ranked = noise * amount + jnp.arange(amount, dtype=jnp.int32)
    return jnp.argsort(ranked, axis=-1).astype(jnp.int32)


def draw_doc_lengths(key, part):
    key = jax.random.fold_in(key, 5)
    short_key, shuffle_key = jax.random.split(key)
    short_count = TOK_DEV // (2 * CLU)
    short_docs = jax.random.randint(short_key, (N_GRP, short_count), 1, CLU + 1).astype(jnp.int32)
    full_length = TOK_DEV * N_TOK - short_count * CLU
    long_doc = jnp.full((N_GRP, 1), full_length, jnp.int32)
    lengths = jnp.concatenate([long_doc, short_docs], axis=1)
    shuffle = distinct_order(shuffle_key, (N_GRP,), lengths.shape[1])
    return jnp.take_along_axis(lengths, shuffle, axis=1).astype(jnp.int32)


def draw_cluster_slots(key, part):
    key = jax.random.fold_in(key, 7)
    first_key, second_key = jax.random.split(key)
    per_peer = TOK_DEV // N_TOK
    send_order = distinct_order(first_key, (N_GRP, N_TOK), TOK_DEV)
    position = jnp.argsort(send_order, axis=-1).astype(jnp.int32)
    target = position // per_peer
    source = jnp.arange(N_TOK, dtype=jnp.int32)[None, :, None]
    arrival = source * per_peer + position % per_peer
    landing = distinct_order(second_key, (N_GRP, N_TOK), TOK_DEV).reshape(N_GRP, N_TOK * TOK_DEV)
    flat_index = (target * TOK_DEV + arrival).reshape(N_GRP, N_TOK * TOK_DEV)
    slot_within = jnp.take_along_axis(landing, flat_index, axis=1)
    slot_ids = target.reshape(N_GRP, N_TOK * TOK_DEV) * TOK_DEV + slot_within
    return slot_ids.reshape(N_GRP * N_TOK * TOK_DEV).astype(jnp.int32)


def spiked(values, rng, source, target, parts, factor):
    def block_of(axis_at):
        return (jnp.arange(values.shape[axis_at]) // (values.shape[axis_at] // parts)).reshape((-1,) + (1,) * (values.ndim - 1 - axis_at))

    near = jax.random.permutation(rng, parts)[block_of(target)]
    other_side = (block_of(target) + parts // 2) % parts
    return jnp.where((block_of(source) == near) | (block_of(source) == other_side), factor * values, values)


def steps_of(stream_key, extent, cuts, least, largest):
    gain, own = 1.0, jax.random.fold_in(stream_key, 6)
    for axis_at, parts in cuts:
        draws = jnp.exp(jax.random.uniform(jax.random.fold_in(own, axis_at), (parts,), jnp.float32, least / len(cuts), largest / len(cuts)))
        gain = gain * jnp.repeat(draws, extent[axis_at] // parts).reshape([-1 if axis == axis_at else 1 for axis in range(len(extent))])
    return gain


def gaussian(key, extent, deviation, most, cuts=(), kind=jnp.bfloat16):
    drawn = jax.random.normal(key, extent, jnp.float32) * deviation
    if len(cuts) > 0:
        drawn = steps_of(key, extent, cuts, -0.22, 0.18) * drawn
    return jnp.clip(drawn, min=-most, max=most).astype(kind)


def bell_draw_with(stream_key, dims, width, limit, cuts, heavy, held_as=jnp.bfloat16):
    entries = width * jax.random.normal(stream_key, dims, jnp.float32)
    if cuts:
        entries = entries * steps_of(stream_key, dims, cuts, -0.22, 0.18)
    return jnp.clip(spiked(entries, jax.random.fold_in(stream_key, 3), *heavy), -limit, limit).astype(held_as)


def setup_inputs(seed: int = 0) -> dict:
    key_list = jax.random.split(jax.random.key(seed), 18)
    tokens_in = bell_draw_with(key_list[0], (TOKENS, D), 1.0, 6.0, ((0, 32),), (0, 1, 32, 2.75))
    w_qkv = gaussian(key_list[1], (D, 3 * D), (D // 2) ** -0.5, 0.3125)
    b_query = gaussian(key_list[2], (D,), 0.5, 3.0)
    b_value = gaussian(key_list[3], (D,), 0.5, 3.0)
    w_out = gaussian(key_list[4], (D, D), (D // 16) ** -0.5, 0.875)
    b_out = gaussian(key_list[5], (D,), 0.5, 3.0)
    norm1_gain = jnp.clip(1.0 + 0.1 * jax.random.normal(key_list[6], (D,), jnp.float32), 0.5, 1.5).astype(jnp.bfloat16)
    norm1_shift = gaussian(key_list[7], (D,), 0.3, 2.0)
    w_up = gaussian(key_list[8], (D, FF), D ** -0.5, 0.21875)
    b_up = gaussian(key_list[9], (FF,), 0.5, 3.0)
    w_down = gaussian(key_list[10], (FF, D), FF ** -0.5, 0.109375)
    b_down = gaussian(key_list[11], (D,), 0.5, 3.0)
    norm2_gain = jnp.clip(1.0 + 0.1 * jax.random.normal(key_list[12], (D,), jnp.float32), 0.5, 1.5).astype(jnp.bfloat16)
    norm2_shift = gaussian(key_list[13], (D,), 0.3, 2.0)
    out_grad = gaussian(key_list[14], (TOKENS, D), 1.0, 6.0, ((0, 32),))
    doc_lengths = draw_doc_lengths(jax.random.fold_in(key_list[17], 71), 0)
    cluster_slots = draw_cluster_slots(jax.random.fold_in(key_list[17], 71), 0)
    return {"tokens_in": tokens_in, "w_qkv": w_qkv, "b_query": b_query, "b_value": b_value, "w_out": w_out, "b_out": b_out, "norm1_gain": norm1_gain, "norm1_shift": norm1_shift, "w_up": w_up, "b_up": b_up, "w_down": w_down, "b_down": b_down, "norm2_gain": norm2_gain, "norm2_shift": norm2_shift, "out_grad": out_grad, "doc_lengths": doc_lengths, "cluster_slots": cluster_slots}


eps = 1e-12
masked_score = -1000000000.0
highest = lax.Precision.HIGHEST

@jax.custom_vjp
def low(v):
    return lax.optimization_barrier(v.astype(jnp.bfloat16)).astype(jnp.float32)

@jax.custom_vjp
def low_back(v):
    return v

def low_keep(v):
    return (low(v), None)

def low_pass(kept, grad):
    return (grad,)

def back_keep(v):
    return (v, None)

def back_low(kept, grad):
    return (low(grad),)
low.defvjp(low_keep, low_pass)
low_back.defvjp(back_keep, back_low)

def norm_rows(values, scales, shifts):
    centre = values - lax.optimization_barrier(jnp.mean(values, axis=-1, keepdims=True))
    spread = lax.optimization_barrier(jnp.mean(centre * centre, axis=-1, keepdims=True))
    return centre * lax.rsqrt(spread + eps) * scales + shifts

def valid_tokens(lengths_row, offset, amount, cluster):
    padded = (lengths_row + cluster - 1) // cluster * cluster
    starts = jnp.cumsum(padded) - padded
    position = offset + jnp.arange(amount, dtype=jnp.int32)
    inside = (position[:, None] >= starts[None, :]) & (position[:, None] < (starts + lengths_row)[None, :])
    return jnp.any(inside, axis=1)

def by_rows(function, arrays):
    amount = arrays[0].shape[0]
    rows_each = min(16 * CLU, amount)
    shaped = tuple((member.reshape((amount // rows_each, rows_each) + member.shape[1:]) for member in arrays))
    result = lax.map(jax.checkpoint(function), shaped)
    return result.reshape((amount,) + result.shape[2:])

def attend(pieces):
    packed, live_keys = pieces
    query = packed[:, :, 0]
    key_rows = packed[:, :, 1]
    value = packed[:, :, 2]
    scores = jnp.einsum('bqhd,bkhd->bhqk', query, key_rows, precision=highest) * HD ** (-0.5)
    scores = low_back(jnp.where(live_keys[:, None, None, :], scores, masked_score))
    top = lax.optimization_barrier(jnp.max(scores, axis=-1, keepdims=True))
    expo = jnp.exp(scores - top)
    attn_weights = low(expo / lax.optimization_barrier(jnp.sum(expo, axis=-1, keepdims=True)))
    context = jnp.einsum('bhqk,bkhd->bqhd', attn_weights, value, precision=highest)
    return context.reshape(packed.shape[0], CLU, H * HD)

def reference(tokens_in, w_qkv, b_query, b_value, w_out, b_out, norm1_gain, norm1_shift, w_up, b_up, w_down, b_down, norm2_gain, norm2_shift, out_grad, doc_lengths, cluster_slots):
    group_tokens = TOK_DEV * N_TOK
    per_step = min(512 // CLU, group_tokens // CLU)
    slot_rows = cluster_slots.reshape(N_GRP, group_tokens).astype(jnp.int32)
    gather_rows = jnp.argsort(slot_rows, axis=1).astype(jnp.int32)
    usable = jnp.stack([valid_tokens(doc_lengths[group], 0, group_tokens, CLU) for group in range(N_GRP)])
    live_rows = jnp.take_along_axis(usable, gather_rows, axis=1)

    def layer(inputs, w_qkv, b_query, b_value, w_out, b_out, norm1_gain, norm1_shift, w_up, b_up, w_down, b_down, norm2_gain, norm2_shift):
        bias_qkv = jnp.concatenate([b_query, jnp.zeros_like(b_query), b_value])

        def project(pieces):
            return jnp.dot(pieces[0], w_qkv, precision=highest) + bias_qkv

        def finish(pieces):
            rows_in, context = pieces
            context = low_back(low(context))
            attn_out = low_back(jnp.dot(context, w_out, precision=highest) + b_out)
            normed1 = norm_rows(rows_in + attn_out, norm1_gain, norm1_shift)
            up_pre = low_back(jnp.dot(low(normed1), w_up, precision=highest) + b_up)
            gelu_low = low(jax.nn.gelu(up_pre, approximate=False))
            down_out = low_back(jnp.dot(gelu_low, w_down, precision=highest) + b_down)
            return norm_rows(normed1 + down_out, norm2_gain, norm2_shift)

        def group_step(carry, pieces):
            rows_in, gather_g, slots_g, live_g = pieces
            qkv = low_back(low(by_rows(project, (rows_in,))))
            packed = qkv[gather_g].reshape(-1, per_step, CLU, 3, H, HD)
            live_keys = live_g.reshape(-1, per_step, CLU)
            context_c = lax.map(jax.checkpoint(attend), (packed, live_keys))
            context = context_c.reshape(group_tokens, D)[slots_g]
            return (carry, by_rows(finish, (rows_in, context)))
        start = jnp.zeros((), jnp.float32)
        ignored, outputs = lax.scan(jax.checkpoint(group_step), start, (inputs.reshape(N_GRP, group_tokens, D), gather_rows, slot_rows, live_rows))
        return outputs.reshape(N_GRP * group_tokens, D)
    floats = (tokens_in, w_qkv, b_query, b_value, w_out, b_out, norm1_gain, norm1_shift, w_up, b_up, w_down, b_down, norm2_gain, norm2_shift)
    floats = tuple((member.astype(jnp.float32) for member in floats))
    result, backward = jax.vjp(layer, *floats)
    grads = backward(out_grad.astype(jnp.float32))
    return (result.astype(jnp.bfloat16), grads[0].astype(jnp.bfloat16), grads[1], grads[2], grads[3], grads[4], grads[5], grads[6], grads[7], grads[8], grads[9], grads[10], grads[11], grads[12], grads[13])
```

```python
import jax
import jax.numpy as jnp
from jax import lax
from jax.sharding import PartitionSpec as P

H = 12
CLU = 128

eps = 1e-12
masked_score = -1000000000.0


def norm_rows(values, scales, shifts):
    centre = values - jnp.mean(values, axis=-1, keepdims=True)
    spread = jnp.mean(centre * centre, axis=-1, keepdims=True)
    return centre * lax.rsqrt(spread + eps) * scales + shifts


def gelu_exact(values):
    return jax.nn.gelu(values, approximate=False)


def valid_tokens(lengths_row, offset, amount, cluster):
    padded = (lengths_row + cluster - 1) // cluster * cluster
    starts = jnp.cumsum(padded) - padded
    position = offset + jnp.arange(amount, dtype=jnp.int32)
    inside = (position[:, None] >= starts[None, :]) & (
        position[:, None] < (starts + lengths_row)[None, :]
    )
    return jnp.any(inside, axis=1)


def dot32(a, b):
    return jnp.dot(a, b, preferred_element_type=jnp.float32)


def move(one_hot, rows):
    return dot32(one_hot, rows).astype(jnp.bfloat16)


def move_back(one_hot, rows):
    picked = jnp.einsum("pi,pd->id", one_hot, rows, preferred_element_type=jnp.float32)
    return picked.astype(jnp.bfloat16)


def exchange(rows):
    return lax.all_to_all(rows, "tok", split_axis=0, concat_axis=0, tiled=True)


def per_device(
    tokens_in, w_qkv, b_query, b_value, w_out, b_out, norm1_gain, norm1_shift,
    w_up, b_up, w_down, b_down, norm2_gain, norm2_shift, out_grad, doc_lengths, cluster_slots,
):
    tok_dev, width = tokens_in.shape
    head_size = width // H
    clusters = tok_dev // CLU
    n_tok = lax.axis_size("tok")
    per_peer = tok_dev // n_tok
    my_index = lax.axis_index("tok")
    f32 = jnp.float32

    usable = valid_tokens(doc_lengths[0], my_index * tok_dev, tok_dev, CLU)
    dest = cluster_slots // tok_dev
    dest_hot = (dest[:, None] == jnp.arange(n_tok)[None, :]).astype(jnp.int32)
    rank = jnp.sum((jnp.cumsum(dest_hot, axis=0) - dest_hot) * dest_hot, axis=1)
    send_pos = dest * per_peer + rank
    send_hot = (jnp.arange(tok_dev)[:, None] == send_pos[None, :])
    note = (cluster_slots % tok_dev) * 2 + usable.astype(jnp.int32)
    sent_note = jnp.sum(jnp.where(send_hot, note[None, :], 0), axis=1)
    send_hot = send_hot.astype(jnp.bfloat16)
    got_note = exchange(sent_note)
    x_got = exchange(move(send_hot, tokens_in))
    g_got = exchange(move(send_hot, out_grad))
    place_hot = jnp.arange(tok_dev)[:, None] == (got_note // 2)[None, :]
    key_live = jnp.sum(jnp.where(place_hot, got_note[None, :] % 2, 0), axis=1) > 0
    place_hot = place_hot.astype(jnp.bfloat16)
    x = move(place_hot, x_got)

    bias_qkv = jnp.concatenate(
        [b_query.astype(f32), jnp.zeros((width,), f32), b_value.astype(f32)]
    )
    qkv = (dot32(x, w_qkv) + bias_qkv).astype(jnp.bfloat16)
    packed = qkv.reshape(clusters, CLU, 3, H, head_size)
    query, keys, value = packed[:, :, 0], packed[:, :, 1], packed[:, :, 2]
    scale = head_size ** (-0.5)
    scores = jnp.einsum("bqhd,bkhd->bhqk", query, keys, preferred_element_type=f32) * scale
    scores = jnp.where(key_live.reshape(clusters, 1, 1, CLU), scores, masked_score)
    expo = jnp.exp(scores - jnp.max(scores, axis=-1, keepdims=True))
    probs = expo / jnp.sum(expo, axis=-1, keepdims=True)
    weights = probs.astype(jnp.bfloat16)
    context = jnp.einsum("bhqk,bkhd->bqhd", weights, value, preferred_element_type=f32)
    context = context.astype(jnp.bfloat16).reshape(tok_dev, width)

    resid1 = x.astype(f32) + dot32(context, w_out) + b_out.astype(f32)
    normed1, norm1_back = jax.vjp(
        norm_rows, resid1, norm1_gain.astype(f32), norm1_shift.astype(f32)
    )
    normed1_low = normed1.astype(jnp.bfloat16)
    up_pre = dot32(normed1_low, w_up) + b_up.astype(f32)
    gelu_out, gelu_back = jax.vjp(gelu_exact, up_pre)
    gelu_low = gelu_out.astype(jnp.bfloat16)
    down_out = dot32(gelu_low, w_down) + b_down.astype(f32)
    normed2, norm2_back = jax.vjp(
        norm_rows, normed1 + down_out, norm2_gain.astype(f32), norm2_shift.astype(f32)
    )
    out_got = exchange(move_back(place_hot, normed2.astype(jnp.bfloat16)))
    block_out = move_back(send_hot, out_got)

    g = move(place_hot, g_got)
    grad_resid2, grad_gain2, grad_shift2 = norm2_back(g.astype(f32))
    grad_down = grad_resid2.astype(jnp.bfloat16)
    grad_b_down = jnp.sum(grad_down.astype(f32), axis=0)
    grad_w_down = jnp.einsum("nf,nd->fd", gelu_low, grad_down, preferred_element_type=f32)
    grad_gelu = jnp.einsum("nd,fd->nf", grad_down, w_down, preferred_element_type=f32)
    grad_up = gelu_back(grad_gelu)[0].astype(jnp.bfloat16)
    grad_b_up = jnp.sum(grad_up.astype(f32), axis=0)
    grad_w_up = jnp.einsum("nd,nf->df", normed1_low, grad_up, preferred_element_type=f32)
    grad_normed1 = grad_resid2 + jnp.einsum(
        "nf,df->nd", grad_up, w_up, preferred_element_type=f32
    )
    grad_resid1, grad_gain1, grad_shift1 = norm1_back(grad_normed1)
    grad_attn = grad_resid1.astype(jnp.bfloat16)
    grad_b_out = jnp.sum(grad_attn.astype(f32), axis=0)
    grad_w_out = jnp.einsum("nd,ne->de", context, grad_attn, preferred_element_type=f32)
    grad_context = jnp.einsum("ne,de->nd", grad_attn, w_out, preferred_element_type=f32)
    grad_context = grad_context.astype(jnp.bfloat16).reshape(clusters, CLU, H, head_size)

    grad_probs = jnp.einsum("bqhd,bkhd->bhqk", grad_context, value, preferred_element_type=f32)
    row_dot = jnp.sum(grad_probs * probs, axis=-1, keepdims=True)
    grad_scores = (probs * (grad_probs - row_dot)).astype(jnp.bfloat16)
    grad_q = jnp.einsum("bhqk,bkhd->bqhd", grad_scores, keys, preferred_element_type=f32) * scale
    grad_k = jnp.einsum("bhqk,bqhd->bkhd", grad_scores, query, preferred_element_type=f32) * scale
    grad_v = jnp.einsum("bhqk,bqhd->bkhd", weights, grad_context, preferred_element_type=f32)
    grad_qkv = jnp.stack([grad_q, grad_k, grad_v], axis=2).astype(jnp.bfloat16)
    grad_qkv = grad_qkv.reshape(tok_dev, 3 * width)
    grad_total = grad_resid1 + jnp.einsum(
        "ne,de->nd", grad_qkv, w_qkv, preferred_element_type=f32
    )
    back_got = exchange(move_back(place_hot, grad_total.astype(jnp.bfloat16)))
    grad_tokens = move_back(send_hot, back_got)
    grad_w_qkv = jnp.einsum("nd,ne->de", x, grad_qkv, preferred_element_type=f32)
    grad_qkv_sum = jnp.sum(grad_qkv.astype(f32), axis=0)

    low = jnp.bfloat16
    wide = jnp.concatenate(
        [
            grad_w_qkv.astype(low), grad_w_out.astype(low), grad_w_up.astype(low),
            grad_w_down.astype(low).reshape(width, -1),
        ],
        axis=1,
    )
    narrow = jnp.concatenate(
        [
            member.reshape(n_tok, -1)
            for member in (
                grad_qkv_sum[:width], grad_qkv_sum[2 * width :], grad_b_out, grad_gain1,
                grad_shift1, grad_b_down, grad_gain2, grad_shift2, grad_b_up,
            )
        ],
        axis=1,
    )
    share = lax.psum_scatter(wide, "tok", scatter_dimension=0, tiled=True)
    share = lax.psum(share, "grp").astype(f32)
    narrow = lax.psum(narrow, ("grp", "tok"))
    mine = lax.dynamic_index_in_dim(narrow, my_index, 0, keepdims=False)
    step = width // n_tok
    parts = [mine[i * step : (i + 1) * step] for i in range(8)] + [mine[8 * step :]]
    ffw = w_up.shape[1]
    return (
        block_out,
        grad_tokens,
        share[:, : 3 * width],
        parts[0],
        parts[1],
        share[:, 3 * width : 4 * width],
        parts[2],
        parts[3],
        parts[4],
        share[:, 4 * width : 4 * width + ffw],
        parts[8],
        share[:, 4 * width + ffw :].reshape(ffw // n_tok, width),
        parts[5],
        parts[6],
        parts[7],
    )


def solution(mesh):
    rows = P(("grp", "tok"), None)
    in_specs = (rows,) + (P(),) * 13 + (rows, P("grp", None), P(("grp", "tok")))
    shares = (
        P("tok", None), P("tok"), P("tok"), P("tok", None), P("tok"), P("tok"), P("tok"),
        P("tok", None), P("tok"), P("tok", None), P("tok"), P("tok"), P("tok"),
    )
    return jax.shard_map(
        per_device, mesh=mesh, in_specs=in_specs, out_specs=(rows, rows) + shares, check_vma=False
    )
```

```python
import functools

import jax
import jax.numpy as jnp
from jax import lax
from jax.experimental import pallas as pl
from jax.experimental.pallas import tpu as pltpu
from jax.sharding import PartitionSpec as P

H = 12
CLU = 128

eps = 1e-12
masked_score = -1000000000.0

MESH = pl.DeviceIdType.MESH
f32 = jnp.float32
bf16 = jnp.bfloat16
BLK = 256


def dot32(a, b):
    return jnp.dot(a, b, preferred_element_type=jnp.float32)


def dot_rows(a, b):
    return lax.dot_general(a, b, (((1,), (1,)), ((), ())), preferred_element_type=jnp.float32)


def dot_cols(a, b):
    return lax.dot_general(a, b, (((0,), (0,)), ((), ())), preferred_element_type=jnp.float32)


def peer_order(n_tok):
    return sorted(range(1, n_tok), key=lambda k: -k)


def row_of(ref):
    return ref[...].astype(f32)[None, :]


def norm_parts(values):
    centre = values - jnp.mean(values, axis=-1, keepdims=True)
    spread = jnp.mean(centre * centre, axis=-1, keepdims=True)
    rstd = lax.rsqrt(spread + eps)
    return centre * rstd, rstd


def lane_halves(width):
    lane = lax.broadcasted_iota(jnp.int32, (1, width), 1)
    low = (lane < width // 2).astype(f32)
    return low.astype(bf16), (1.0 - low).astype(bf16)


def stack_heads(pair, halves):
    return jnp.concatenate([pair * halves[0], pair * halves[1]], axis=0)


def side_by_side(stacked):
    half = stacked.shape[0] // 2
    return jnp.concatenate([stacked[:half], stacked[half:]], axis=1)


def column_of(row):
    amount = row.shape[1]
    return jnp.concatenate(
        [
            jnp.broadcast_to(row[:, at : at + 128], (128, 128)).T
            for at in range(0, amount, 128)
        ],
        axis=0,
    )


def hot_from_column(column, amount):
    lane = lax.broadcasted_iota(jnp.int32, column.shape, 1).astype(f32)
    return jnp.concatenate(
        [(lane + float(at) == column).astype(f32).astype(bf16) for at in range(0, amount, 128)],
        axis=1,
    )


def forward_kernel(
    n_tok, per,
    slots_ref, docs_ref, tok_ref, og_ref, wq_ref, bq_ref, bv_ref, wo_ref, bo_ref, g1_ref, s1_ref,
    wu_ref, bu_ref, wd_ref, bd_ref, g2_ref, s2_ref,
    xc_o, gc_o, qkv_o, p_o, ctx_o, r1_o, n1_o, gelu_o, gelup_o, r2_o, back_o, col_o, pos_o,
    xh, gh, xs, gs, xr, gr, hot, note_s, note_r, wq, wo, wu, wd, live_s,
    xc_t, qkv_t, p_t, ctx_t, r1_t, n1_t, gelu_t, gelup_t, r2_t, bo_c, back_t, gc_t, col_t, pos_t,
    load_sem, note_ss, note_rs, x_ss, x_rs, g_ss, g_rs, own_sem, out_sem, last_sem,
):
    rows, width = xh.shape
    ffw = wu.shape[1]
    blocks = rows // BLK
    grp = lax.axis_index("grp")
    me = lax.axis_index("tok")
    order = peer_order(n_tok)

    barrier = pltpu.get_barrier_semaphore()
    for k in order:
        pl.semaphore_signal(barrier, inc=1, device_id=(grp, me ^ k), device_id_type=MESH)

    loads = [
        pltpu.make_async_copy(src, dst, load_sem.at[i])
        for i, (src, dst) in enumerate(
            ((tok_ref, xh), (og_ref, gh), (wq_ref, wq), (wo_ref, wo), (wu_ref, wu), (wd_ref, wd))
        )
    ]
    for copy in loads:
        copy.start()

    slots = slots_ref[...][None, :]
    dest = jnp.right_shift(slots, rows.bit_length() - 1)
    within = jnp.bitwise_and(slots, rows - 1)
    lanes = lax.broadcasted_iota(jnp.int32, (1, rows), 1)
    dest_hot = lax.broadcasted_iota(jnp.int32, (16, rows), 0) == dest
    dest_hot = dest_hot.astype(f32)
    before = lax.broadcasted_iota(jnp.int32, (BLK, rows), 1)
    rank = jnp.zeros((16, rows), f32)
    for b in range(blocks):
        earlier = lax.broadcasted_iota(jnp.int32, (BLK, rows), 0) + b * BLK < before
        rank += dot32(
            dest_hot[:, b * BLK : (b + 1) * BLK].astype(bf16), earlier.astype(f32).astype(bf16)
        )
    rank = jnp.sum(rank * dest_hot, axis=0, keepdims=True).astype(jnp.int32)
    pos = dest * per + rank
    pos_t[...] = jnp.broadcast_to(pos, (8, rows))
    start = jnp.int32(0)
    position = lanes + me * rows
    usable = jnp.zeros((1, rows), jnp.int32)
    for i in range(docs_ref.shape[1]):
        length = docs_ref[0, i]
        inside = (position >= start) & (position < start + length)
        usable = jnp.where(inside, 1, usable)
        start = start + jnp.bitwise_and(length + (CLU - 1), -CLU)
    for b in range(blocks):
        spot = lax.broadcasted_iota(jnp.int32, (BLK, rows), 0) + b * BLK
        hot[b * BLK : (b + 1) * BLK, :] = (spot == pos).astype(f32).astype(bf16)
    kind = lax.broadcasted_iota(jnp.int32, (16, rows), 0)
    notes = jnp.where(
        kind == 0,
        jnp.right_shift(within, 5),
        jnp.where(kind == 1, jnp.bitwise_and(within, 31), jnp.where(kind == 2, usable, 0)),
    )
    notes = dot_rows(notes.astype(f32).astype(bf16), hot[...]).astype(bf16)
    for d in range(n_tok):
        note_s[d] = notes[:, d * per : (d + 1) * per]

    def note_copy(k):
        return pltpu.make_async_remote_copy(
            src_ref=note_s.at[me ^ k], dst_ref=note_r.at[me], send_sem=note_ss.at[k],
            recv_sem=note_rs.at[k], device_id=(grp, me ^ k), device_id_type=MESH,
        )

    def row_copy(src, dst, ss, rs, k):
        return pltpu.make_async_remote_copy(
            src_ref=src.at[pl.ds(pl.multiple_of((me ^ k) * per, per), per)],
            dst_ref=dst.at[pl.ds(pl.multiple_of(me * per, per), per)],
            send_sem=ss.at[k], recv_sem=rs.at[k], device_id=(grp, me ^ k), device_id_type=MESH,
        )

    pl.semaphore_wait(barrier, n_tok - 1)
    for k in order:
        note_copy(k).start()
    loads[0].wait()
    for b in range(blocks):
        sl = pl.ds(b * BLK, BLK)
        xs[sl, :] = dot32(hot[sl, :], xh[...]).astype(bf16)
    for k in order:
        row_copy(xs, xr, x_ss, x_rs, k).start()
    mine = pl.ds(pl.multiple_of(me * per, per), per)
    own_x = pltpu.make_async_copy(xs.at[mine], xr.at[mine], own_sem.at[0])
    own_x.start()
    own_note = pltpu.make_async_copy(note_s.at[me], note_r.at[me], own_sem.at[1])
    own_note.start()
    loads[1].wait()
    for b in range(blocks):
        sl = pl.ds(b * BLK, BLK)
        gs[sl, :] = dot32(hot[sl, :], gh[...]).astype(bf16)
    own_g = pltpu.make_async_copy(gs.at[mine], gr.at[mine], own_sem.at[2])
    own_g.start()

    own_note.wait()
    for k in order:
        note_copy(k).wait_recv()
    got = jnp.concatenate([note_r[d] for d in range(n_tok)], axis=1)
    got32 = got.astype(f32)
    slot_row = got32[0:1, :] * 32.0 + got32[1:2, :]
    col_t[...] = column_of(slot_row)
    slot_row = slot_row.astype(jnp.int32)
    for b in range(blocks):
        spot = lax.broadcasted_iota(jnp.int32, (BLK, rows), 0) + b * BLK
        hot[b * BLK : (b + 1) * BLK, :] = (spot == slot_row).astype(f32).astype(bf16)
    live_s[...] = dot_rows(got, hot[...])

    own_x.wait()
    for k in order:
        row_copy(xs, xr, x_ss, x_rs, k).wait_send()
    for k in order:
        row_copy(gs, gr, g_ss, g_rs, k).start()
    for k in order:
        row_copy(xs, xr, x_ss, x_rs, k).wait_recv()
    for copy in loads[2:]:
        copy.wait()

    halves = lane_halves(2 * width // H)
    pair_width = 2 * width // H
    scale = (width // H) ** (-0.5)
    outs = (
        (xc_t, xc_o, BLK), (qkv_t, qkv_o, BLK), (p_t, p_o, BLK * H), (ctx_t, ctx_o, BLK), (r1_t, r1_o, BLK),
        (n1_t, n1_o, BLK), (gelu_t, gelu_o, BLK), (gelup_t, gelup_o, BLK), (r2_t, r2_o, BLK),
    )

    def out_copy(i, b, slot):
        tile, whole, count = outs[i]
        return pltpu.make_async_copy(
            tile.at[slot], whole.at[pl.ds(pl.multiple_of(b * count, count), count)], out_sem.at[slot, i]
        )

    def block(b, carry):
        slot = lax.rem(b, 2)
        sl = pl.ds(pl.multiple_of(b * BLK, BLK), BLK)

        @pl.when(b >= 2)
        def _():
            for i in range(len(outs)):
                out_copy(i, b - 2, slot).wait()

        x = dot32(hot[sl, :], xr[...]).astype(bf16)
        xc_t[slot] = x
        for part, bias in ((0, row_of(bq_ref)), (1, None), (2, row_of(bv_ref))):
            got_part = dot32(x, wq[:, part * width : (part + 1) * width])
            if bias is not None:
                got_part = got_part + bias
            qkv_t[slot, :, part * width : (part + 1) * width] = got_part.astype(bf16)
        for c in range(BLK // CLU):
            at = pl.multiple_of(b * BLK + c * CLU, CLU)
            live = live_s[2:3, pl.ds(at, CLU)] > 0.5
            crow = pl.ds(c * CLU, CLU)
            for p in range(H // 2):
                cols = [pl.ds(part * width + p * pair_width, pair_width) for part in range(3)]
                q2 = qkv_t[slot, crow, cols[0]]
                k2 = qkv_t[slot, crow, cols[1]]
                v2 = qkv_t[slot, crow, cols[2]]
                scores = dot_rows(stack_heads(q2, halves), k2) * scale
                scores = jnp.where(live, scores, masked_score)
                expo = jnp.exp(scores - jnp.max(scores, axis=-1, keepdims=True))
                weights = (expo / jnp.sum(expo, axis=-1, keepdims=True)).astype(bf16)
                p_t[slot, pl.ds((c * H + 2 * p) * CLU, 2 * CLU), :] = weights
                context = dot32(side_by_side(weights), stack_heads(v2, halves))
                ctx_t[slot, crow, pl.ds(p * pair_width, pair_width)] = context.astype(bf16)
        resid1 = x.astype(f32) + (dot32(ctx_t[slot], wo[...]) + row_of(bo_ref))
        r1_t[slot] = resid1
        hat1, _ = norm_parts(resid1)
        normed1 = hat1 * row_of(g1_ref) + row_of(s1_ref)
        low1 = normed1.astype(bf16)
        n1_t[slot] = low1
        down = None
        step = width
        for j in range(ffw // step):
            cs = pl.ds(j * step, step)
            up = dot32(low1, wu[:, cs]) + bu_ref[cs].astype(f32)[None, :]
            phi = 0.5 * (1.0 + lax.erf(up * 0.7071067811865476))
            slope = phi + up * jnp.exp(up * up * -0.5) * 0.3989422804014327
            act = (up * phi).astype(bf16)
            gelu_t[slot, :, cs] = act
            gelup_t[slot, :, cs] = slope.astype(bf16)
            term = dot32(act, wd[cs, :])
            down = term if down is None else down + term
        resid2 = normed1 + (down + row_of(bd_ref))
        r2_t[slot] = resid2
        hat2, _ = norm_parts(resid2)
        bo_c[sl, :] = (hat2 * row_of(g2_ref) + row_of(s2_ref)).astype(bf16)
        for i in range(len(outs)):
            out_copy(i, b, slot).start()
        return carry

    lax.fori_loop(0, blocks, block, 0)

    col_out = pltpu.make_async_copy(col_t, col_o, last_sem.at[0])
    col_out.start()
    pos_out = pltpu.make_async_copy(pos_t, pos_o, last_sem.at[1])
    pos_out.start()
    for b in range(blocks):
        sl = pl.ds(b * BLK, BLK)
        back_t[sl, :] = dot32(hot_from_column(col_t[sl, :], rows), bo_c[...]).astype(bf16)
    back_out = pltpu.make_async_copy(back_t, back_o, last_sem.at[2])
    back_out.start()
    own_g.wait()
    for k in order:
        row_copy(gs, gr, g_ss, g_rs, k).wait_recv()
    for b in range(blocks):
        sl = pl.ds(b * BLK, BLK)
        gc_t[sl, :] = dot32(hot[sl, :], gr[...]).astype(bf16)
    gc_out = pltpu.make_async_copy(gc_t, gc_o, last_sem.at[3])
    gc_out.start()
    for k in order:
        note_copy(k).wait_send()
        row_copy(gs, gr, g_ss, g_rs, k).wait_send()
    for b in range(max(blocks - 2, 0), blocks):
        for i in range(len(outs)):
            out_copy(i, b, b % 2).wait()
    col_out.wait()
    pos_out.wait()
    back_out.wait()
    gc_out.wait()


def forward(n_tok, tokens_in, w_qkv, b_query, b_value, w_out, b_out, norm1_gain, norm1_shift,
            w_up, b_up, w_down, b_down, norm2_gain, norm2_shift, out_grad, doc_lengths, cluster_slots):
    rows, width = tokens_in.shape
    ffw = w_up.shape[1]
    per = rows // n_tok
    vm = pl.BlockSpec(memory_space=pltpu.VMEM)
    sm = pl.BlockSpec(memory_space=pltpu.SMEM)
    hb = pl.BlockSpec(memory_space=pl.ANY)
    out_shape = [
        ((rows, width), bf16), ((rows, width), bf16), ((rows, 3 * width), bf16), ((rows * H, CLU), bf16),
        ((rows, width), bf16), ((rows, width), f32), ((rows, width), bf16), ((rows, ffw), bf16),
        ((rows, ffw), bf16), ((rows, width), f32), ((rows, width), bf16), ((rows, 128), f32),
        ((8, rows), jnp.int32),
    ]
    vmem = pltpu.VMEM
    dma = pltpu.SemaphoreType.DMA
    scratch = (
        [vmem((rows, width), bf16)] * 6
        + [vmem((rows, rows), bf16), vmem((n_tok, 16, per), bf16), vmem((n_tok, 16, per), bf16)]
        + [vmem(w_qkv.shape, bf16), vmem(w_out.shape, bf16), vmem(w_up.shape, bf16), vmem(w_down.shape, bf16)]
        + [vmem((16, rows), f32)]
        + [
            vmem((2, BLK, width), bf16), vmem((2, BLK, 3 * width), bf16), vmem((2, BLK * H, CLU), bf16),
            vmem((2, BLK, width), bf16), vmem((2, BLK, width), f32), vmem((2, BLK, width), bf16),
            vmem((2, BLK, ffw), bf16), vmem((2, BLK, ffw), bf16), vmem((2, BLK, width), f32),
            vmem((rows, width), bf16), vmem((rows, width), bf16), vmem((rows, width), bf16),
            vmem((rows, 128), f32), vmem((8, rows), jnp.int32),
        ]
        + [dma((6,))] + [dma((n_tok,))] * 6 + [dma((3,)), dma((2, 9)), dma((4,))]
    )
    return pl.pallas_call(
        functools.partial(forward_kernel, n_tok, per),
        out_shape=[jax.ShapeDtypeStruct(s, d) for s, d in out_shape],
        in_specs=[vm, sm, hb, hb, hb, vm, vm, hb, vm, vm, vm, hb, vm, hb, vm, vm, vm],
        out_specs=[hb] * len(out_shape),
        scratch_shapes=scratch,
        compiler_params=pltpu.CompilerParams(
            collective_id=0, has_side_effects=True, vmem_limit_bytes=60 * 2**20
        ),
        name="layer_forward",
    )(cluster_slots, doc_lengths, tokens_in, out_grad, w_qkv, b_query, b_value, w_out, b_out, norm1_gain,
      norm1_shift, w_up, b_up, w_down, b_down, norm2_gain, norm2_shift)


def gelu_exact(values):
    return jax.nn.gelu(values, approximate=False)


def valid_tokens(lengths_row, offset, amount, cluster):
    padded = (lengths_row + cluster - 1) // cluster * cluster
    starts = jnp.cumsum(padded) - padded
    position = offset + jnp.arange(amount, dtype=jnp.int32)
    inside = (position[:, None] >= starts[None, :]) & (
        position[:, None] < (starts + lengths_row)[None, :]
    )
    return jnp.any(inside, axis=1)


def move(one_hot, rows):
    return dot32(one_hot, rows).astype(jnp.bfloat16)


def move_back(one_hot, rows):
    picked = jnp.einsum("pi,pd->id", one_hot, rows, preferred_element_type=jnp.float32)
    return picked.astype(jnp.bfloat16)


def exchange(rows):
    return lax.all_to_all(rows, "tok", split_axis=0, concat_axis=0, tiled=True)


def per_device(
    tokens_in, w_qkv, b_query, b_value, w_out, b_out, norm1_gain, norm1_shift,
    w_up, b_up, w_down, b_down, norm2_gain, norm2_shift, out_grad, doc_lengths, cluster_slots,
):
    tok_dev, width = tokens_in.shape
    head_size = width // H
    clusters = tok_dev // CLU
    n_tok = lax.axis_size("tok")
    per_peer = tok_dev // n_tok
    my_index = lax.axis_index("tok")
    f32 = jnp.float32

    usable = valid_tokens(doc_lengths[0], my_index * tok_dev, tok_dev, CLU)
    dest = cluster_slots // tok_dev
    dest_hot = (dest[:, None] == jnp.arange(n_tok)[None, :]).astype(jnp.int32)
    rank = jnp.sum((jnp.cumsum(dest_hot, axis=0) - dest_hot) * dest_hot, axis=1)
    send_pos = dest * per_peer + rank
    send_hot = (jnp.arange(tok_dev)[:, None] == send_pos[None, :])
    note = (cluster_slots % tok_dev) * 2 + usable.astype(jnp.int32)
    sent_note = jnp.sum(jnp.where(send_hot, note[None, :], 0), axis=1)
    send_hot = send_hot.astype(jnp.bfloat16)
    got_note = exchange(sent_note)
    x_got = exchange(move(send_hot, tokens_in))
    g_got = exchange(move(send_hot, out_grad))
    place_hot = jnp.arange(tok_dev)[:, None] == (got_note // 2)[None, :]
    key_live = jnp.sum(jnp.where(place_hot, got_note[None, :] % 2, 0), axis=1) > 0
    place_hot = place_hot.astype(jnp.bfloat16)
    x = move(place_hot, x_got)

    bias_qkv = jnp.concatenate(
        [b_query.astype(f32), jnp.zeros((width,), f32), b_value.astype(f32)]
    )
    qkv = (dot32(x, w_qkv) + bias_qkv).astype(jnp.bfloat16)
    packed = qkv.reshape(clusters, CLU, 3, H, head_size)
    query, keys, value = packed[:, :, 0], packed[:, :, 1], packed[:, :, 2]
    scale = head_size ** (-0.5)
    scores = jnp.einsum("bqhd,bkhd->bhqk", query, keys, preferred_element_type=f32) * scale
    scores = jnp.where(key_live.reshape(clusters, 1, 1, CLU), scores, masked_score)
    expo = jnp.exp(scores - jnp.max(scores, axis=-1, keepdims=True))
    probs = expo / jnp.sum(expo, axis=-1, keepdims=True)
    weights = probs.astype(jnp.bfloat16)
    context = jnp.einsum("bhqk,bkhd->bqhd", weights, value, preferred_element_type=f32)
    context = context.astype(jnp.bfloat16).reshape(tok_dev, width)

    resid1 = x.astype(f32) + dot32(context, w_out) + b_out.astype(f32)
    normed1, norm1_back = jax.vjp(
        norm_rows, resid1, norm1_gain.astype(f32), norm1_shift.astype(f32)
    )
    normed1_low = normed1.astype(jnp.bfloat16)
    up_pre = dot32(normed1_low, w_up) + b_up.astype(f32)
    gelu_out, gelu_back = jax.vjp(gelu_exact, up_pre)
    gelu_low = gelu_out.astype(jnp.bfloat16)
    down_out = dot32(gelu_low, w_down) + b_down.astype(f32)
    normed2, norm2_back = jax.vjp(
        norm_rows, normed1 + down_out, norm2_gain.astype(f32), norm2_shift.astype(f32)
    )
    out_got = exchange(move_back(place_hot, normed2.astype(jnp.bfloat16)))
    block_out = move_back(send_hot, out_got)

    g = move(place_hot, g_got)
    grad_resid2, grad_gain2, grad_shift2 = norm2_back(g.astype(f32))
    grad_down = grad_resid2.astype(jnp.bfloat16)
    grad_b_down = jnp.sum(grad_down.astype(f32), axis=0)
    grad_w_down = jnp.einsum("nf,nd->fd", gelu_low, grad_down, preferred_element_type=f32)
    grad_gelu = jnp.einsum("nd,fd->nf", grad_down, w_down, preferred_element_type=f32)
    grad_up = gelu_back(grad_gelu)[0].astype(jnp.bfloat16)
    grad_b_up = jnp.sum(grad_up.astype(f32), axis=0)
    grad_w_up = jnp.einsum("nd,nf->df", normed1_low, grad_up, preferred_element_type=f32)
    grad_normed1 = grad_resid2 + jnp.einsum(
        "nf,df->nd", grad_up, w_up, preferred_element_type=f32
    )
    grad_resid1, grad_gain1, grad_shift1 = norm1_back(grad_normed1)
    grad_attn = grad_resid1.astype(jnp.bfloat16)
    grad_b_out = jnp.sum(grad_attn.astype(f32), axis=0)
    grad_w_out = jnp.einsum("nd,ne->de", context, grad_attn, preferred_element_type=f32)
    grad_context = jnp.einsum("ne,de->nd", grad_attn, w_out, preferred_element_type=f32)
    grad_context = grad_context.astype(jnp.bfloat16).reshape(clusters, CLU, H, head_size)

    grad_probs = jnp.einsum("bqhd,bkhd->bhqk", grad_context, value, preferred_element_type=f32)
    row_dot = jnp.sum(grad_probs * probs, axis=-1, keepdims=True)
    grad_scores = (probs * (grad_probs - row_dot)).astype(jnp.bfloat16)
    grad_q = jnp.einsum("bhqk,bkhd->bqhd", grad_scores, keys, preferred_element_type=f32) * scale
    grad_k = jnp.einsum("bhqk,bqhd->bkhd", grad_scores, query, preferred_element_type=f32) * scale
    grad_v = jnp.einsum("bhqk,bqhd->bkhd", weights, grad_context, preferred_element_type=f32)
    grad_qkv = jnp.stack([grad_q, grad_k, grad_v], axis=2).astype(jnp.bfloat16)
    grad_qkv = grad_qkv.reshape(tok_dev, 3 * width)
    grad_total = grad_resid1 + jnp.einsum(
        "ne,de->nd", grad_qkv, w_qkv, preferred_element_type=f32
    )
    back_got = exchange(move_back(place_hot, grad_total.astype(jnp.bfloat16)))
    grad_tokens = move_back(send_hot, back_got)
    grad_w_qkv = jnp.einsum("nd,ne->de", x, grad_qkv, preferred_element_type=f32)
    grad_qkv_sum = jnp.sum(grad_qkv.astype(f32), axis=0)

    low = jnp.bfloat16
    wide = jnp.concatenate(
        [
            grad_w_qkv.astype(low), grad_w_out.astype(low), grad_w_up.astype(low),
            grad_w_down.astype(low).reshape(width, -1),
        ],
        axis=1,
    )
    narrow = jnp.concatenate(
        [
            member.reshape(n_tok, -1)
            for member in (
                grad_qkv_sum[:width], grad_qkv_sum[2 * width :], grad_b_out, grad_gain1,
                grad_shift1, grad_b_down, grad_gain2, grad_shift2, grad_b_up,
            )
        ],
        axis=1,
    )
    share = lax.psum_scatter(wide, "tok", scatter_dimension=0, tiled=True)
    share = lax.psum(share, "grp").astype(f32)
    narrow = lax.psum(narrow, ("grp", "tok"))
    mine = lax.dynamic_index_in_dim(narrow, my_index, 0, keepdims=False)
    step = width // n_tok
    parts = [mine[i * step : (i + 1) * step] for i in range(8)] + [mine[8 * step :]]
    ffw = w_up.shape[1]
    return (
        block_out,
        grad_tokens,
        share[:, : 3 * width],
        parts[0],
        parts[1],
        share[:, 3 * width : 4 * width],
        parts[2],
        parts[3],
        parts[4],
        share[:, 4 * width : 4 * width + ffw],
        parts[8],
        share[:, 4 * width + ffw :].reshape(ffw // n_tok, width),
        parts[5],
        parts[6],
        parts[7],
    )


def norm_rows(values, scales, shifts):
    centre = values - jnp.mean(values, axis=-1, keepdims=True)
    spread = jnp.mean(centre * centre, axis=-1, keepdims=True)
    return centre * lax.rsqrt(spread + eps) * scales + shifts


def per_device_fast(
    tokens_in, w_qkv, b_query, b_value, w_out, b_out, norm1_gain, norm1_shift,
    w_up, b_up, w_down, b_down, norm2_gain, norm2_shift, out_grad, doc_lengths, cluster_slots,
):
    tok_dev, width = tokens_in.shape
    head_size = width // H
    clusters = tok_dev // CLU
    n_tok = lax.axis_size("tok")
    my_index = lax.axis_index("tok")
    scale = head_size ** (-0.5)
    (x, g, qkv, weights, context, resid1, normed1_low, gelu_low, gelup, resid2, back, col, pos) = forward(
        n_tok, tokens_in, w_qkv, b_query, b_value, w_out, b_out, norm1_gain, norm1_shift,
        w_up, b_up, w_down, b_down, norm2_gain, norm2_shift, out_grad, doc_lengths, cluster_slots)
    send_hot = (jnp.arange(tok_dev)[:, None] == pos[0][None, :]).astype(bf16)
    place_hot = (jnp.arange(tok_dev, dtype=f32)[:, None] == col[:, 0][None, :]).astype(bf16)
    block_out = move_back(send_hot, exchange(back))
    _, norm1_back = jax.vjp(norm_rows, resid1, norm1_gain.astype(f32), norm1_shift.astype(f32))
    _, norm2_back = jax.vjp(norm_rows, resid2, norm2_gain.astype(f32), norm2_shift.astype(f32))
    grad_resid2, grad_gain2, grad_shift2 = norm2_back(g.astype(f32))
    grad_down = grad_resid2.astype(jnp.bfloat16)
    grad_b_down = jnp.sum(grad_down.astype(f32), axis=0)
    grad_w_down = jnp.einsum("nf,nd->fd", gelu_low, grad_down, preferred_element_type=f32)
    grad_gelu = jnp.einsum("nd,fd->nf", grad_down, w_down, preferred_element_type=f32)
    grad_up = (grad_gelu * gelup.astype(f32)).astype(jnp.bfloat16)
    grad_b_up = jnp.sum(grad_up.astype(f32), axis=0)
    grad_w_up = jnp.einsum("nd,nf->df", normed1_low, grad_up, preferred_element_type=f32)
    grad_normed1 = grad_resid2 + jnp.einsum(
        "nf,df->nd", grad_up, w_up, preferred_element_type=f32
    )
    grad_resid1, grad_gain1, grad_shift1 = norm1_back(grad_normed1)
    grad_attn = grad_resid1.astype(jnp.bfloat16)
    grad_b_out = jnp.sum(grad_attn.astype(f32), axis=0)
    grad_w_out = jnp.einsum("nd,ne->de", context, grad_attn, preferred_element_type=f32)
    grad_context = jnp.einsum("ne,de->nd", grad_attn, w_out, preferred_element_type=f32)
    grad_context = grad_context.astype(jnp.bfloat16).reshape(clusters, CLU, H, head_size)

    packed = qkv.reshape(clusters, CLU, 3, H, head_size)
    query, keys, value = packed[:, :, 0], packed[:, :, 1], packed[:, :, 2]
    weights = weights.reshape(clusters, H, CLU, CLU)
    probs = weights.astype(f32)
    grad_probs = jnp.einsum("bqhd,bkhd->bhqk", grad_context, value, preferred_element_type=f32)
    row_dot = jnp.sum(grad_probs * probs, axis=-1, keepdims=True)
    grad_scores = (probs * (grad_probs - row_dot)).astype(jnp.bfloat16)
    grad_q = jnp.einsum("bhqk,bkhd->bqhd", grad_scores, keys, preferred_element_type=f32) * scale
    grad_k = jnp.einsum("bhqk,bqhd->bkhd", grad_scores, query, preferred_element_type=f32) * scale
    grad_v = jnp.einsum("bhqk,bqhd->bkhd", weights, grad_context, preferred_element_type=f32)
    grad_qkv = jnp.stack([grad_q, grad_k, grad_v], axis=2).astype(jnp.bfloat16)
    grad_qkv = grad_qkv.reshape(tok_dev, 3 * width)
    grad_total = grad_resid1 + jnp.einsum(
        "ne,de->nd", grad_qkv, w_qkv, preferred_element_type=f32
    )
    back_got = exchange(move_back(place_hot, grad_total.astype(jnp.bfloat16)))
    grad_tokens = move_back(send_hot, back_got)
    grad_w_qkv = jnp.einsum("nd,ne->de", x, grad_qkv, preferred_element_type=f32)
    grad_qkv_sum = jnp.sum(grad_qkv.astype(f32), axis=0)

    low = jnp.bfloat16
    wide = jnp.concatenate(
        [
            grad_w_qkv.astype(low), grad_w_out.astype(low), grad_w_up.astype(low),
            grad_w_down.astype(low).reshape(width, -1),
        ],
        axis=1,
    )
    narrow = jnp.concatenate(
        [
            member.reshape(n_tok, -1)
            for member in (
                grad_qkv_sum[:width], grad_qkv_sum[2 * width :], grad_b_out, grad_gain1,
                grad_shift1, grad_b_down, grad_gain2, grad_shift2, grad_b_up,
            )
        ],
        axis=1,
    )
    share = lax.psum_scatter(wide, "tok", scatter_dimension=0, tiled=True)
    share = lax.psum(share, "grp").astype(f32)
    narrow = lax.psum(narrow, ("grp", "tok"))
    mine = lax.dynamic_index_in_dim(narrow, my_index, 0, keepdims=False)
    step = width // n_tok
    parts = [mine[i * step : (i + 1) * step] for i in range(8)] + [mine[8 * step :]]
    ffw = w_up.shape[1]
    return (
        block_out,
        grad_tokens,
        share[:, : 3 * width],
        parts[0],
        parts[1],
        share[:, 3 * width : 4 * width],
        parts[2],
        parts[3],
        parts[4],
        share[:, 4 * width : 4 * width + ffw],
        parts[8],
        share[:, 4 * width + ffw :].reshape(ffw // n_tok, width),
        parts[5],
        parts[6],
        parts[7],
    )


def solution(mesh):
    n_tok = mesh.shape["tok"]

    def body(*args):
        even = (args[0].shape[0] // n_tok) % 128 == 0 and n_tok & (n_tok - 1) == 0
        return (per_device_fast if even and mesh.shape["grp"] == 4 else per_device)(*args)

    rows = P(("grp", "tok"), None)
    in_specs = (rows,) + (P(),) * 13 + (rows, P("grp", None), P(("grp", "tok")))
    shares = (
        P("tok", None), P("tok"), P("tok"), P("tok", None), P("tok"), P("tok"), P("tok"),
        P("tok", None), P("tok"), P("tok", None), P("tok"), P("tok"), P("tok"),
    )
    return jax.shard_map(
        body, mesh=mesh, in_specs=in_specs, out_specs=(rows, rows) + shares, check_vma=False
    )
```

```python
import functools

import jax
import jax.numpy as jnp
from jax import lax
from jax.experimental import pallas as pl
from jax.experimental.pallas import tpu as pltpu
from jax.sharding import PartitionSpec as P

H = 12
CLU = 128

eps = 1e-12
masked_score = -1000000000.0

MESH = pl.DeviceIdType.MESH
f32 = jnp.float32
bf16 = jnp.bfloat16
BLK = 256


def dot32(a, b):
    return jnp.dot(a, b, preferred_element_type=jnp.float32)


def dot_rows(a, b):
    return lax.dot_general(a, b, (((1,), (1,)), ((), ())), preferred_element_type=jnp.float32)


def dot_cols(a, b):
    return lax.dot_general(a, b, (((0,), (0,)), ((), ())), preferred_element_type=jnp.float32)


def peer_order(n_tok):
    return sorted(range(1, n_tok), key=lambda k: -k)


def row_of(ref):
    return ref[...].astype(f32)[None, :]


def norm_parts(values):
    centre = values - jnp.mean(values, axis=-1, keepdims=True)
    spread = jnp.mean(centre * centre, axis=-1, keepdims=True)
    rstd = lax.rsqrt(spread + eps)
    return centre * rstd, rstd


def lane_halves(width):
    lane = lax.broadcasted_iota(jnp.int32, (1, width), 1)
    low = (lane < width // 2).astype(f32)
    return low.astype(bf16), (1.0 - low).astype(bf16)


def stack_heads(pair, halves):
    return jnp.concatenate([pair * halves[0], pair * halves[1]], axis=0)


def side_by_side(stacked):
    half = stacked.shape[0] // 2
    return jnp.concatenate([stacked[:half], stacked[half:]], axis=1)


def column_of(row):
    amount = row.shape[1]
    return jnp.concatenate(
        [
            jnp.broadcast_to(row[:, at : at + 128], (128, 128)).T
            for at in range(0, amount, 128)
        ],
        axis=0,
    )


def hot_from_column(column, amount):
    lane = lax.broadcasted_iota(jnp.int32, column.shape, 1).astype(f32)
    return jnp.concatenate(
        [(lane + float(at) == column).astype(f32).astype(bf16) for at in range(0, amount, 128)],
        axis=1,
    )


def forward_kernel(
    n_tok, per,
    slots_ref, docs_ref, tok_ref, og_ref, wq_ref, bq_ref, bv_ref, wo_ref, bo_ref, g1_ref, s1_ref,
    wu_ref, bu_ref, wd_ref, bd_ref, g2_ref, s2_ref,
    xc_o, gc_o, qkv_o, p_o, ctx_o, r1_o, n1_o, gelu_o, gelup_o, r2_o, back_o, col_o, pos_o,
    xh, gh, xs, gs, xr, gr, hot, note_s, note_r, wq, wo, wu, wd, live_s,
    xc_t, qkv_t, p_t, ctx_t, r1_t, n1_t, gelu_t, gelup_t, r2_t, bo_c, back_t, gc_t, col_t, pos_t,
    load_sem, note_ss, note_rs, x_ss, x_rs, g_ss, g_rs, own_sem, out_sem, last_sem,
):
    rows, width = xh.shape
    ffw = wu.shape[1]
    blocks = rows // BLK
    grp = lax.axis_index("grp")
    me = lax.axis_index("tok")
    order = peer_order(n_tok)

    barrier = pltpu.get_barrier_semaphore()
    for k in order:
        pl.semaphore_signal(barrier, inc=1, device_id=(grp, me ^ k), device_id_type=MESH)

    loads = [
        pltpu.make_async_copy(src, dst, load_sem.at[i])
        for i, (src, dst) in enumerate(
            ((tok_ref, xh), (og_ref, gh), (wq_ref, wq), (wo_ref, wo), (wu_ref, wu), (wd_ref, wd))
        )
    ]
    for copy in loads:
        copy.start()

    slots = slots_ref[...][None, :]
    dest = jnp.right_shift(slots, rows.bit_length() - 1)
    within = jnp.bitwise_and(slots, rows - 1)
    lanes = lax.broadcasted_iota(jnp.int32, (1, rows), 1)
    dest_hot = lax.broadcasted_iota(jnp.int32, (16, rows), 0) == dest
    dest_hot = dest_hot.astype(f32)
    before = lax.broadcasted_iota(jnp.int32, (BLK, rows), 1)
    rank = jnp.zeros((16, rows), f32)
    for b in range(blocks):
        earlier = lax.broadcasted_iota(jnp.int32, (BLK, rows), 0) + b * BLK < before
        rank += dot32(
            dest_hot[:, b * BLK : (b + 1) * BLK].astype(bf16), earlier.astype(f32).astype(bf16)
        )
    rank = jnp.sum(rank * dest_hot, axis=0, keepdims=True).astype(jnp.int32)
    pos = dest * per + rank
    pos_t[...] = jnp.broadcast_to(pos, (8, rows))
    start = jnp.int32(0)
    position = lanes + me * rows
    usable = jnp.zeros((1, rows), jnp.int32)
    for i in range(docs_ref.shape[1]):
        length = docs_ref[0, i]
        inside = (position >= start) & (position < start + length)
        usable = jnp.where(inside, 1, usable)
        start = start + jnp.bitwise_and(length + (CLU - 1), -CLU)
    for b in range(blocks):
        spot = lax.broadcasted_iota(jnp.int32, (BLK, rows), 0) + b * BLK
        hot[b * BLK : (b + 1) * BLK, :] = (spot == pos).astype(f32).astype(bf16)
    kind = lax.broadcasted_iota(jnp.int32, (16, rows), 0)
    notes = jnp.where(
        kind == 0,
        jnp.right_shift(within, 5),
        jnp.where(kind == 1, jnp.bitwise_and(within, 31), jnp.where(kind == 2, usable, 0)),
    )
    notes = dot_rows(notes.astype(f32).astype(bf16), hot[...]).astype(bf16)
    for d in range(n_tok):
        note_s[d] = notes[:, d * per : (d + 1) * per]

    def note_copy(k):
        return pltpu.make_async_remote_copy(
            src_ref=note_s.at[me ^ k], dst_ref=note_r.at[me], send_sem=note_ss.at[k],
            recv_sem=note_rs.at[k], device_id=(grp, me ^ k), device_id_type=MESH,
        )

    def row_copy(src, dst, ss, rs, k):
        return pltpu.make_async_remote_copy(
            src_ref=src.at[pl.ds(pl.multiple_of((me ^ k) * per, per), per)],
            dst_ref=dst.at[pl.ds(pl.multiple_of(me * per, per), per)],
            send_sem=ss.at[k], recv_sem=rs.at[k], device_id=(grp, me ^ k), device_id_type=MESH,
        )

    pl.semaphore_wait(barrier, n_tok - 1)
    for k in order:
        note_copy(k).start()
    loads[0].wait()
    for b in range(blocks):
        sl = pl.ds(b * BLK, BLK)
        xs[sl, :] = dot32(hot[sl, :], xh[...]).astype(bf16)
    for k in order:
        row_copy(xs, xr, x_ss, x_rs, k).start()
    mine = pl.ds(pl.multiple_of(me * per, per), per)
    own_x = pltpu.make_async_copy(xs.at[mine], xr.at[mine], own_sem.at[0])
    own_x.start()
    own_note = pltpu.make_async_copy(note_s.at[me], note_r.at[me], own_sem.at[1])
    own_note.start()
    loads[1].wait()
    for b in range(blocks):
        sl = pl.ds(b * BLK, BLK)
        gs[sl, :] = dot32(hot[sl, :], gh[...]).astype(bf16)
    own_g = pltpu.make_async_copy(gs.at[mine], gr.at[mine], own_sem.at[2])
    own_g.start()

    own_note.wait()
    for k in order:
        note_copy(k).wait_recv()
    got = jnp.concatenate([note_r[d] for d in range(n_tok)], axis=1)
    got32 = got.astype(f32)
    slot_row = got32[0:1, :] * 32.0 + got32[1:2, :]
    col_t[...] = column_of(slot_row)
    slot_row = slot_row.astype(jnp.int32)
    for b in range(blocks):
        spot = lax.broadcasted_iota(jnp.int32, (BLK, rows), 0) + b * BLK
        hot[b * BLK : (b + 1) * BLK, :] = (spot == slot_row).astype(f32).astype(bf16)
    live_s[...] = dot_rows(got, hot[...])

    own_x.wait()
    for k in order:
        row_copy(xs, xr, x_ss, x_rs, k).wait_send()
    for k in order:
        row_copy(gs, gr, g_ss, g_rs, k).start()
    for k in order:
        row_copy(xs, xr, x_ss, x_rs, k).wait_recv()
    for copy in loads[2:]:
        copy.wait()

    halves = lane_halves(2 * width // H)
    pair_width = 2 * width // H
    scale = (width // H) ** (-0.5)
    outs = (
        (xc_t, xc_o, BLK), (qkv_t, qkv_o, BLK), (p_t, p_o, BLK * H), (ctx_t, ctx_o, BLK), (r1_t, r1_o, BLK),
        (n1_t, n1_o, BLK), (gelu_t, gelu_o, BLK), (gelup_t, gelup_o, BLK), (r2_t, r2_o, BLK),
    )

    def out_copy(i, b, slot):
        tile, whole, count = outs[i]
        return pltpu.make_async_copy(
            tile.at[slot], whole.at[pl.ds(pl.multiple_of(b * count, count), count)], out_sem.at[slot, i]
        )

    def block(b, carry):
        slot = lax.rem(b, 2)
        sl = pl.ds(pl.multiple_of(b * BLK, BLK), BLK)

        @pl.when(b >= 2)
        def _():
            for i in range(len(outs)):
                out_copy(i, b - 2, slot).wait()

        x = dot32(hot[sl, :], xr[...]).astype(bf16)
        xc_t[slot] = x
        for part, bias in ((0, row_of(bq_ref)), (1, None), (2, row_of(bv_ref))):
            got_part = dot32(x, wq[:, part * width : (part + 1) * width])
            if bias is not None:
                got_part = got_part + bias
            qkv_t[slot, :, part * width : (part + 1) * width] = got_part.astype(bf16)
        for c in range(BLK // CLU):
            at = pl.multiple_of(b * BLK + c * CLU, CLU)
            live = live_s[2:3, pl.ds(at, CLU)] > 0.5
            crow = pl.ds(c * CLU, CLU)
            for p in range(H // 2):
                cols = [pl.ds(part * width + p * pair_width, pair_width) for part in range(3)]
                q2 = qkv_t[slot, crow, cols[0]]
                k2 = qkv_t[slot, crow, cols[1]]
                v2 = qkv_t[slot, crow, cols[2]]
                scores = dot_rows(stack_heads(q2, halves), k2) * scale
                scores = jnp.where(live, scores, masked_score)
                expo = jnp.exp(scores - jnp.max(scores, axis=-1, keepdims=True))
                weights = (expo / jnp.sum(expo, axis=-1, keepdims=True)).astype(bf16)
                p_t[slot, pl.ds((c * H + 2 * p) * CLU, 2 * CLU), :] = weights
                context = dot32(side_by_side(weights), stack_heads(v2, halves))
                ctx_t[slot, crow, pl.ds(p * pair_width, pair_width)] = context.astype(bf16)
        resid1 = x.astype(f32) + (dot32(ctx_t[slot], wo[...]) + row_of(bo_ref))
        r1_t[slot] = resid1
        hat1, _ = norm_parts(resid1)
        normed1 = hat1 * row_of(g1_ref) + row_of(s1_ref)
        low1 = normed1.astype(bf16)
        n1_t[slot] = low1
        down = None
        step = width
        for j in range(ffw // step):
            cs = pl.ds(j * step, step)
            up = dot32(low1, wu[:, cs]) + bu_ref[cs].astype(f32)[None, :]
            phi = 0.5 * (1.0 + lax.erf(up * 0.7071067811865476))
            slope = phi + up * jnp.exp(up * up * -0.5) * 0.3989422804014327
            act = (up * phi).astype(bf16)
            gelu_t[slot, :, cs] = act
            gelup_t[slot, :, cs] = slope.astype(bf16)
            term = dot32(act, wd[cs, :])
            down = term if down is None else down + term
        resid2 = normed1 + (down + row_of(bd_ref))
        r2_t[slot] = resid2
        hat2, _ = norm_parts(resid2)
        bo_c[sl, :] = (hat2 * row_of(g2_ref) + row_of(s2_ref)).astype(bf16)
        for i in range(len(outs)):
            out_copy(i, b, slot).start()
        return carry

    lax.fori_loop(0, blocks, block, 0)

    col_out = pltpu.make_async_copy(col_t, col_o, last_sem.at[0])
    col_out.start()
    pos_out = pltpu.make_async_copy(pos_t, pos_o, last_sem.at[1])
    pos_out.start()
    for b in range(blocks):
        sl = pl.ds(b * BLK, BLK)
        back_t[sl, :] = dot32(hot_from_column(col_t[sl, :], rows), bo_c[...]).astype(bf16)
    back_out = pltpu.make_async_copy(back_t, back_o, last_sem.at[2])
    back_out.start()
    own_g.wait()
    for k in order:
        row_copy(gs, gr, g_ss, g_rs, k).wait_recv()
    for b in range(blocks):
        sl = pl.ds(b * BLK, BLK)
        gc_t[sl, :] = dot32(hot[sl, :], gr[...]).astype(bf16)
    gc_out = pltpu.make_async_copy(gc_t, gc_o, last_sem.at[3])
    gc_out.start()
    for k in order:
        note_copy(k).wait_send()
        row_copy(gs, gr, g_ss, g_rs, k).wait_send()
    for b in range(max(blocks - 2, 0), blocks):
        for i in range(len(outs)):
            out_copy(i, b, b % 2).wait()
    col_out.wait()
    pos_out.wait()
    back_out.wait()
    gc_out.wait()


def forward(n_tok, tokens_in, w_qkv, b_query, b_value, w_out, b_out, norm1_gain, norm1_shift,
            w_up, b_up, w_down, b_down, norm2_gain, norm2_shift, out_grad, doc_lengths, cluster_slots):
    rows, width = tokens_in.shape
    ffw = w_up.shape[1]
    per = rows // n_tok
    vm = pl.BlockSpec(memory_space=pltpu.VMEM)
    sm = pl.BlockSpec(memory_space=pltpu.SMEM)
    hb = pl.BlockSpec(memory_space=pl.ANY)
    out_shape = [
        ((rows, width), bf16), ((rows, width), bf16), ((rows, 3 * width), bf16), ((rows * H, CLU), bf16),
        ((rows, width), bf16), ((rows, width), f32), ((rows, width), bf16), ((rows, ffw), bf16),
        ((rows, ffw), bf16), ((rows, width), f32), ((rows, width), bf16), ((rows, 128), f32),
        ((8, rows), jnp.int32),
    ]
    vmem = pltpu.VMEM
    dma = pltpu.SemaphoreType.DMA
    scratch = (
        [vmem((rows, width), bf16)] * 6
        + [vmem((rows, rows), bf16), vmem((n_tok, 16, per), bf16), vmem((n_tok, 16, per), bf16)]
        + [vmem(w_qkv.shape, bf16), vmem(w_out.shape, bf16), vmem(w_up.shape, bf16), vmem(w_down.shape, bf16)]
        + [vmem((16, rows), f32)]
        + [
            vmem((2, BLK, width), bf16), vmem((2, BLK, 3 * width), bf16), vmem((2, BLK * H, CLU), bf16),
            vmem((2, BLK, width), bf16), vmem((2, BLK, width), f32), vmem((2, BLK, width), bf16),
            vmem((2, BLK, ffw), bf16), vmem((2, BLK, ffw), bf16), vmem((2, BLK, width), f32),
            vmem((rows, width), bf16), vmem((rows, width), bf16), vmem((rows, width), bf16),
            vmem((rows, 128), f32), vmem((8, rows), jnp.int32),
        ]
        + [dma((6,))] + [dma((n_tok,))] * 6 + [dma((3,)), dma((2, 9)), dma((4,))]
    )
    return pl.pallas_call(
        functools.partial(forward_kernel, n_tok, per),
        out_shape=[jax.ShapeDtypeStruct(s, d) for s, d in out_shape],
        in_specs=[vm, sm, hb, hb, hb, vm, vm, hb, vm, vm, vm, hb, vm, hb, vm, vm, vm],
        out_specs=[hb] * len(out_shape),
        scratch_shapes=scratch,
        compiler_params=pltpu.CompilerParams(
            collective_id=0, has_side_effects=True, vmem_limit_bytes=60 * 2**20
        ),
        name="layer_forward",
    )(cluster_slots, doc_lengths, tokens_in, out_grad, w_qkv, b_query, b_value, w_out, b_out, norm1_gain,
      norm1_shift, w_up, b_up, w_down, b_down, norm2_gain, norm2_shift)


def grad_kinds(width, ffw, n_tok):
    return ((ffw // n_tok, width), (width // n_tok, ffw), (width // n_tok, width), (width // n_tok, 3 * width))


def backward_kernel(n_tok, per, kinds, *refs):
    (xc_ref, gc_ref, qkv_ref, p_ref, ctx_ref, r1_ref, n1_ref, gelu_ref, gelup_ref, r2_ref, back_ref, col_ref,
     wq_ref, wo_ref, wu_ref, wd_ref, g1_ref, g2_ref) = refs[:18]
    refs = refs[18:]
    bo_got, gt_got, nar_o = refs[:3]
    shares = refs[3:7]
    rec0, recx, recy, rec2, recz = (refs[7 + 4 * i : 11 + 4 * i] for i in range(5))
    refs = refs[27:]
    (wq, wo, wu, wd, gwd, gelu, gup, low1, gdown, resid, grow, ctx, gattn, gcl, qkv, probs, xc, col,
     nar_v, bup_v, nar_s, nar_r, nar_g, nar_h, nar_t,
     load_sem, bo_ss, bo_rs, gt_ss, gt_rs, own_sem, s0_ss, s0_rs, x1_ss, x1_rs, x2_ss, x2_rs, z_ss, z_rs,
     ag_ss, ag_rs, loc_sem, fin_sem, nt_ss, nt_rs, ng_ss, ng_rs) = refs
    rows, width = xc.shape
    ffw = wu.shape[1]
    blocks = rows // BLK
    grp = lax.axis_index("grp")
    me = lax.axis_index("tok")
    core = lax.rem(me, 2)
    chip = lax.div(me, 2)
    chips = n_tok // 2
    gx = lax.rem(grp, 2)
    gy = lax.div(grp, 2)
    order = peer_order(n_tok)
    mats = (gwd, wu, wo, wq)

    barrier = pltpu.get_barrier_semaphore()
    for k in order:
        pl.semaphore_signal(barrier, inc=1, device_id=(grp, me ^ k), device_id_type=MESH)
    for k in (1, 2, 3):
        pl.semaphore_signal(barrier, inc=1, device_id=(grp ^ k, me), device_id_type=MESH)

    load = {
        name: pltpu.make_async_copy(src, dst, load_sem.at[i])
        for i, (name, src, dst) in enumerate((
            ("gc", gc_ref, gcl), ("r2", r2_ref, resid), ("gelu", gelu_ref, gelu), ("wd", wd_ref, wd),
            ("gelup", gelup_ref, gup), ("wu", wu_ref, wu), ("n1", n1_ref, low1), ("wo", wo_ref, wo),
            ("ctx", ctx_ref, ctx), ("qkv", qkv_ref, qkv), ("p", p_ref, probs), ("wq", wq_ref, wq),
            ("xc", xc_ref, xc), ("col", col_ref, col), ("r1", r1_ref, resid),
        ))
    }
    for name in load:
        if name != "r1":
            load[name].start()

    def row_copy(src, dst, ss, rs, k):
        return pltpu.make_async_remote_copy(
            src_ref=src.at[pl.ds(pl.multiple_of((me ^ k) * per, per), per)],
            dst_ref=dst.at[pl.ds(pl.multiple_of(me * per, per), per)],
            send_sem=ss.at[k], recv_sem=rs.at[k], device_id=(grp, me ^ k), device_id_type=MESH,
        )

    mine = pl.ds(pl.multiple_of(me * per, per), per)
    pl.semaphore_wait(barrier, n_tok - 1 + 3)
    for k in order:
        row_copy(back_ref, bo_got, bo_ss, bo_rs, k).start()
    own_bo = pltpu.make_async_copy(back_ref.at[mine], bo_got.at[mine], own_sem.at[0])
    own_bo.start()

    def held(m, z, row0, count, col0, ncols):
        share, _ = kinds[m]
        at = (2 * z + core) * share + row0
        return mats[m].at[pl.ds(pl.multiple_of(at, 16), count), pl.ds(pl.multiple_of(col0, 128), ncols)]

    def room(m, z, row0, count, col0, ncols):
        share, _ = kinds[m]
        if m == 0:
            whole, r, c = gelu, row0, z * width + col0
        elif m == 1:
            whole, r, c = gelu, kinds[0][0] + z * share + row0, col0
        elif m == 2:
            whole, r, c = gup, z * share + row0, 3 * width + col0
        else:
            whole, r, c = gup, z * share + row0, col0
        return whole.at[pl.ds(pl.multiple_of(r, 16), count), pl.ds(pl.multiple_of(c, 128), ncols)]

    def remote(src, dst, ss, rs, who):
        return pltpu.make_async_remote_copy(
            src_ref=src, dst_ref=dst, send_sem=ss, recv_sem=rs, device_id=who, device_id_type=MESH
        )

    def copy_s0(m, z):
        share, cols = kinds[m]
        at = (2 * z + 1 - core) * share
        return remote(
            mats[m].at[pl.ds(pl.multiple_of(at, 16), share)], rec0[m].at[pl.ds(z * share, share)],
            s0_ss.at[m, z], s0_rs.at[m, z], (grp, me ^ 1),
        )

    def first_x(z):
        return z < chips // 2

    def copy_x1(m, z):
        share, cols = kinds[m]
        half, hcols = share // 2, cols // 2
        if first_x(z):
            src = held(m, z, 0, share, (1 - gx) * hcols, hcols)
            dst, who = recx[m].at[pl.ds(z * share, share)], (grp ^ 1, me)
        else:
            src = held(m, z, (1 - gy) * half, half, 0, cols)
            dst, who = recy[m].at[pl.ds((z - chips // 2) * half, half)], (grp ^ 2, me)
        return remote(src, dst, x1_ss.at[m, z], x1_rs.at[m, z], who)

    def copy_x2(m, z):
        share, cols = kinds[m]
        half, hcols = share // 2, cols // 2
        dst = rec2[m].at[pl.ds(z * half, half)]
        if first_x(z):
            src, who = held(m, z, (1 - gy) * half, half, gx * hcols, hcols), (grp ^ 2, me)
        else:
            src, who = held(m, z, gy * half, half, (1 - gx) * hcols, hcols), (grp ^ 1, me)
        return remote(src, dst, x2_ss.at[m, z], x2_rs.at[m, z], who)

    def copy_z(m, j):
        share, cols = kinds[m]
        half, hcols = share // 2, cols // 2
        return remote(
            held(m, chip ^ j, gy * half, half, gx * hcols, hcols), recz[m].at[pl.ds(j * half, half)],
            z_ss.at[m, j], z_rs.at[m, j], (grp, me ^ (2 * j)),
        )

    def share_part(m):
        share, cols = kinds[m]
        half, hcols = share // 2, cols // 2
        return shares[m].at[
            pl.ds(pl.multiple_of(gy * half, 16), half), pl.ds(pl.multiple_of(gx * hcols, 128), hcols)
        ]

    def own_part(m):
        share, cols = kinds[m]
        half, hcols = share // 2, cols // 2
        return held(m, chip, gy * half, half, gx * hcols, hcols)

    def copy_ag(m, k):
        return remote(own_part(m), share_part(m), ag_ss.at[m, k], ag_rs.at[m, k], (grp ^ k, me))

    def own_ag(m):
        return pltpu.make_async_copy(own_part(m), share_part(m), fin_sem.at[m])

    def add_in(target, extra):
        target[...] = (target[...].astype(f32) + extra[...].astype(f32)).astype(bf16)

    def start_s0(m):
        for z in range(chips):
            copy_s0(m, z).start()

    def step_r0(m):
        share, cols = kinds[m]
        local = []
        for z in range(chips):
            copy_s0(m, z).wait_recv()
            local.append(pltpu.make_async_copy(
                rec0[m].at[pl.ds(z * share, share)], room(m, z, 0, share, 0, cols), loc_sem.at[m, z]))
            local[-1].start()
        for z in range(chips):
            local[z].wait()
            add_in(held(m, z, 0, share, 0, cols), room(m, z, 0, share, 0, cols))
            copy_x1(m, z).start()

    def step_r1(m):
        share, cols = kinds[m]
        half, hcols = share // 2, cols // 2
        local, spots = [], []
        for z in range(chips):
            copy_x1(m, z).wait_recv()
            if first_x(z):
                src, spot = recx[m].at[pl.ds(z * share, share)], (0, share, gx * hcols, hcols)
            else:
                src = recy[m].at[pl.ds((z - chips // 2) * half, half)]
                spot = (gy * half, half, 0, cols)
            spots.append(spot)
            local.append(pltpu.make_async_copy(src, room(m, z, *spot), loc_sem.at[m, z]))
            local[-1].start()
        for z in range(chips):
            local[z].wait()
            add_in(held(m, z, *spots[z]), room(m, z, *spots[z]))
            copy_x2(m, z).start()

    def step_r2(m):
        share, cols = kinds[m]
        half, hcols = share // 2, cols // 2
        spot = (gy * half, half, gx * hcols, hcols)
        local = []
        for z in range(chips):
            copy_x2(m, z).wait_recv()
            local.append(pltpu.make_async_copy(
                rec2[m].at[pl.ds(z * half, half)], room(m, z, *spot), loc_sem.at[m, z]))
            local[-1].start()
        for z in range(chips):
            local[z].wait()
            add_in(held(m, z, *spot), room(m, z, *spot))
        for j in range(chips - 1, 0, -1):
            copy_z(m, j).start()

    def step_rz(m):
        share, cols = kinds[m]
        half, hcols = share // 2, cols // 2
        local = []
        for j in range(1, chips):
            copy_z(m, j).wait_recv()
            local.append(pltpu.make_async_copy(
                recz[m].at[pl.ds(j * half, half)], room(m, j, 0, half, 0, hcols), loc_sem.at[m, j]))
            local[-1].start()
        total = own_part(m)[...].astype(f32)
        for j in range(1, chips):
            local[j - 1].wait()
            total += room(m, j, 0, half, 0, hcols)[...].astype(f32)
        own_part(m)[...] = total.astype(bf16)
        for k in (3, 1, 2):
            copy_ag(m, k).start()
        own_ag(m).start()

    gain2 = row_of(g2_ref)
    gain1 = row_of(g1_ref)

    def norm_back(upstream, resid_rows, gain):
        hat, rstd = norm_parts(resid_rows)
        dh = upstream * gain
        inner = jnp.mean(dh * hat, axis=-1, keepdims=True)
        return rstd * (dh - jnp.mean(dh, axis=-1, keepdims=True) - hat * inner), hat

    def add_sum(at, values):
        nar_v[at : at + 1, :] += jnp.sum(values, axis=0, keepdims=True)

    nar_v[...] = jnp.zeros_like(nar_v)
    bup_v[...] = jnp.zeros_like(bup_v)
    load["gc"].wait()
    load["r2"].wait()
    for b in range(blocks):
        sl = pl.ds(b * BLK, BLK)
        g = gcl[sl, :].astype(f32)
        back, hat = norm_back(g, resid[sl, :], gain2)
        low = back.astype(bf16)
        grow[sl, :] = back
        gdown[sl, :] = low
        add_sum(5, low.astype(f32))
        add_sum(6, g * hat)
        add_sum(7, g)
    load["r1"].start()

    load["gelu"].wait()
    step = width
    for j in range(ffw // step):
        cs = pl.ds(j * step, step)
        gwd[cs, :] = dot_cols(gelu[:, cs], gdown[...]).astype(bf16)
    start_s0(0)
    load["wd"].wait()
    load["gelup"].wait()
    for b in range(blocks):
        sl = pl.ds(b * BLK, BLK)
        for j in range(ffw // step):
            cs = pl.ds(j * step, step)
            up = (dot_rows(gdown[sl, :], wd[cs, :]) * gup[sl, cs].astype(f32)).astype(bf16)
            gup[sl, cs] = up
            bup_v[0:1, cs] += jnp.sum(up.astype(f32), axis=0, keepdims=True)
    load["wu"].wait()
    load["r1"].wait()
    load["wo"].wait()
    for b in range(blocks):
        sl = pl.ds(b * BLK, BLK)
        gn1 = grow[sl, :] + dot_rows(gup[sl, :], wu[...])
        back, hat = norm_back(gn1, resid[sl, :], gain1)
        low = back.astype(bf16)
        grow[sl, :] = back
        gattn[sl, :] = low
        add_sum(2, low.astype(f32))
        add_sum(3, gn1 * hat)
        add_sum(4, gn1)
        gcl[sl, :] = dot_rows(low, wo[...]).astype(bf16)
    step_r0(0)
    load["n1"].wait()
    for j in range(ffw // step):
        cs = pl.ds(j * step, step)
        wu[:, cs] = dot_cols(low1[...], gup[:, cs]).astype(bf16)
    start_s0(1)
    load["ctx"].wait()
    wo[...] = dot_cols(ctx[...], gattn[...]).astype(bf16)
    start_s0(2)

    load["qkv"].wait()
    load["p"].wait()
    load["wq"].wait()
    halves = lane_halves(2 * width // H)
    pair_width = 2 * width // H
    scale = (width // H) ** (-0.5)

    def attend(b):
        for c in range(BLK // CLU):
            crow = pl.ds(b * BLK + c * CLU, CLU)
            for p in range(H // 2):
                cols = [pl.ds(part * width + p * pair_width, pair_width) for part in range(3)]
                q2 = stack_heads(qkv[crow, cols[0]], halves)
                k2 = stack_heads(qkv[crow, cols[1]], halves)
                v2 = qkv[crow, cols[2]]
                go = stack_heads(gcl[crow, pl.ds(p * pair_width, pair_width)], halves)
                weights = probs[pl.ds((b * BLK + c * CLU) * H + 2 * p * CLU, 2 * CLU), :]
                weights32 = weights.astype(f32)
                gp = dot_rows(go, v2)
                dot = jnp.sum(gp * weights32, axis=-1, keepdims=True)
                gs = (weights32 * (gp - dot)).astype(bf16)
                gq = (dot32(side_by_side(gs), k2) * scale).astype(bf16)
                gk = (dot_cols(gs, q2) * scale).astype(bf16)
                gv = dot_cols(weights, go).astype(bf16)
                qkv[crow, cols[0]] = gq
                qkv[crow, cols[1]] = gk
                qkv[crow, cols[2]] = gv
        sl = pl.ds(b * BLK, BLK)
        add_sum(0, qkv[sl, 0:width].astype(f32))
        add_sum(1, qkv[sl, 2 * width :].astype(f32))
        total = grow[sl, :] + dot_rows(qkv[sl, :], wq[...])
        low1[sl, :] = total.astype(bf16)

    attend(0)
    step_r1(0)
    attend(1)
    step_r0(1)
    attend(2)
    step_r2(0)
    attend(3)
    load["col"].wait()
    for b in range(blocks):
        sl = pl.ds(b * BLK, BLK)
        gdown[sl, :] = dot32(hot_from_column(col[sl, :], rows), low1[...]).astype(bf16)
    for k in order:
        row_copy(gdown, gt_got, gt_ss, gt_rs, k).start()
    own_gt = pltpu.make_async_copy(gdown.at[mine], gt_got.at[mine], own_sem.at[1])
    own_gt.start()
    step_r1(1)

    each = width // n_tok
    at = lax.broadcasted_iota(jnp.int32, (width, n_tok * 128), 0)
    lane = lax.broadcasted_iota(jnp.int32, (width, n_tok * 128), 1)
    inner = jnp.bitwise_and(lane, 127)
    pick = (at == jnp.right_shift(lane, 7) * each + inner) & (inner < each)
    spread = jnp.dot(nar_v[...], pick.astype(f32), precision=lax.Precision.HIGHEST, preferred_element_type=f32)
    share_up = ffw // n_tok
    for d in range(n_tok):
        nar_s[d] = jnp.concatenate(
            [spread[0:8, d * 128 : (d + 1) * 128]]
            + [bup_v[0:1, d * share_up + i : d * share_up + i + 128] for i in range(0, share_up, 128)]
            + [jnp.zeros((8 - share_up // 128, 128), f32)], axis=0)

    def nar_copy(k):
        return remote(nar_s.at[me ^ k], nar_r.at[k], nt_ss.at[k], nt_rs.at[k], (grp, me ^ k))

    def nar_cross(k):
        return remote(nar_g, nar_h.at[k], ng_ss.at[k], ng_rs.at[k], (grp ^ k, me))

    for k in order:
        nar_copy(k).start()
    load["xc"].wait()
    for j in range(3):
        cs = pl.ds(j * step, step)
        wq[:, cs] = dot_cols(xc[...], qkv[:, cs]).astype(bf16)
    start_s0(3)
    step_r2(1)
    step_rz(0)
    step_r0(2)
    step_r0(3)
    total = nar_s[me]
    for k in order:
        nar_copy(k).wait_recv()
        total += nar_r[k]
    nar_g[...] = total
    for k in (3, 1, 2):
        nar_cross(k).start()
    step_r1(2)
    step_r1(3)
    step_rz(1)
    step_r2(2)
    step_r2(3)
    total = nar_g[...]
    for k in (1, 2, 3):
        nar_cross(k).wait_recv()
        total += nar_h[k]
    nar_t[...] = total
    nar_out = pltpu.make_async_copy(nar_t, nar_o, own_sem.at[2])
    nar_out.start()
    step_rz(2)
    step_rz(3)

    own_bo.wait()
    own_gt.wait()
    nar_out.wait()
    for k in order:
        row_copy(back_ref, bo_got, bo_ss, bo_rs, k).wait()
        row_copy(gdown, gt_got, gt_ss, gt_rs, k).wait()
        nar_copy(k).wait_send()
    for k in (1, 2, 3):
        nar_cross(k).wait_send()
    for m in range(4):
        own_ag(m).wait()
        for z in range(chips):
            copy_s0(m, z).wait_send()
            copy_x1(m, z).wait_send()
            copy_x2(m, z).wait_send()
        for j in range(1, chips):
            copy_z(m, j).wait_send()
        for k in (1, 2, 3):
            copy_ag(m, k).wait()


def backward(n_tok, saved, w_qkv, w_out, w_up, w_down, norm1_gain, norm2_gain):
    rows, width = saved[0].shape
    ffw = w_up.shape[1]
    per = rows // n_tok
    chips = n_tok // 2
    kinds = grad_kinds(width, ffw, n_tok)
    vm = pl.BlockSpec(memory_space=pltpu.VMEM)
    hb = pl.BlockSpec(memory_space=pl.ANY)
    outs = [((rows, width), bf16), ((rows, width), bf16), ((16, 128), f32)]
    outs += [(kind, bf16) for kind in kinds]
    outs += [((chips * r, c), bf16) for r, c in kinds]
    outs += [((chips // 2 * r, c // 2), bf16) for r, c in kinds]
    outs += [((chips // 2 * (r // 2), c), bf16) for r, c in kinds]
    outs += [((chips * (r // 2), c // 2), bf16) for r, c in kinds] * 2
    vmem = pltpu.VMEM
    dma = pltpu.SemaphoreType.DMA
    scratch = [
        vmem(w_qkv.shape, bf16), vmem(w_out.shape, bf16), vmem(w_up.shape, bf16), vmem(w_down.shape, bf16),
        vmem(w_down.shape, bf16), vmem((rows, ffw), bf16), vmem((rows, ffw), bf16), vmem((rows, width), bf16),
        vmem((rows, width), bf16), vmem((rows, width), f32), vmem((rows, width), f32), vmem((rows, width), bf16),
        vmem((rows, width), bf16), vmem((rows, width), bf16), vmem((rows, 3 * width), bf16),
        vmem((rows * H, CLU), bf16), vmem((rows, width), bf16), vmem((rows, 128), f32),
        vmem((16, width), f32), vmem((8, ffw), f32), vmem((n_tok, 16, 128), f32), vmem((n_tok, 16, 128), f32),
        vmem((16, 128), f32), vmem((4, 16, 128), f32), vmem((16, 128), f32),
        dma((15,)), dma((n_tok,)), dma((n_tok,)), dma((n_tok,)), dma((n_tok,)), dma((3,)),
    ]
    scratch += [dma((4, chips))] * 8 + [dma((4, 4))] * 2 + [dma((4, chips)), dma((4,))]
    scratch += [dma((n_tok,))] * 2 + [dma((4,))] * 2
    return pl.pallas_call(
        functools.partial(backward_kernel, n_tok, per, kinds),
        out_shape=[jax.ShapeDtypeStruct(s, d) for s, d in outs],
        in_specs=[hb] * 16 + [vm] * 2,
        out_specs=[hb] * len(outs),
        scratch_shapes=scratch,
        compiler_params=pltpu.CompilerParams(
            collective_id=1, has_side_effects=True, vmem_limit_bytes=63 * 2**20
        ),
        name="layer_backward",
    )(*saved, w_qkv, w_out, w_up, w_down, norm1_gain, norm2_gain)[:7]


def finish_kernel(pos_ref, bo_ref, gt_ref, nar_ref, wd_ref, wu_ref, wo_ref, wq_ref, *outs):
    (out_o, tok_o, wq_o, bq_o, bv_o, wo_o, b_out_o, g1_o, s1_o, wu_o, bu_o, wd_o, bd_o, g2_o, s2_o) = outs
    rows = bo_ref.shape[0]
    column = column_of(pos_ref[0:1, :].astype(f32))
    for b in range(rows // BLK):
        sl = pl.ds(b * BLK, BLK)
        home = hot_from_column(column[b * BLK : (b + 1) * BLK], rows)
        out_o[sl, :] = dot32(home, bo_ref[...]).astype(bf16)
        tok_o[sl, :] = dot32(home, gt_ref[...]).astype(bf16)
    for src, dst in ((wd_ref, wd_o), (wu_ref, wu_o), (wo_ref, wo_o), (wq_ref, wq_o)):
        dst[...] = src[...].astype(f32)
    for i, dst in enumerate((bq_o, bv_o, b_out_o, g1_o, s1_o, bd_o, g2_o, s2_o)):
        dst[...] = nar_ref[i, 0 : dst.shape[0]]
    for i in range(bu_o.shape[0] // 128):
        bu_o[i * 128 : (i + 1) * 128] = nar_ref[8 + i, :]


def finish(pos, got):
    bo, gt, nar, wd, wu, wo, wq = got
    rows, width = bo.shape
    each = wq.shape[0]
    vm = pl.BlockSpec(memory_space=pltpu.VMEM)
    outs = [
        (bo.shape, bf16), (gt.shape, bf16), (wq.shape, f32), ((each,), f32), ((each,), f32), (wo.shape, f32),
        ((each,), f32), ((each,), f32), ((each,), f32), (wu.shape, f32), ((wd.shape[0],), f32), (wd.shape, f32),
        ((each,), f32), ((each,), f32), ((each,), f32),
    ]
    return pl.pallas_call(
        finish_kernel,
        out_shape=[jax.ShapeDtypeStruct(s, d) for s, d in outs],
        in_specs=[vm] * 8,
        out_specs=[vm] * len(outs),
        compiler_params=pltpu.CompilerParams(vmem_limit_bytes=60 * 2**20),
        name="back_home",
    )(pos, bo, gt, nar, wd, wu, wo, wq)


def per_device_fast(
    tokens_in, w_qkv, b_query, b_value, w_out, b_out, norm1_gain, norm1_shift,
    w_up, b_up, w_down, b_down, norm2_gain, norm2_shift, out_grad, doc_lengths, cluster_slots,
):
    n_tok = lax.axis_size("tok")
    *saved, pos = forward(
        n_tok, tokens_in, w_qkv, b_query, b_value, w_out, b_out, norm1_gain, norm1_shift,
        w_up, b_up, w_down, b_down, norm2_gain, norm2_shift, out_grad, doc_lengths, cluster_slots)
    got = backward(n_tok, saved, w_qkv, w_out, w_up, w_down, norm1_gain, norm2_gain)
    return tuple(finish(pos, got))


def norm_rows(values, scales, shifts):
    centre = values - jnp.mean(values, axis=-1, keepdims=True)
    spread = jnp.mean(centre * centre, axis=-1, keepdims=True)
    return centre * lax.rsqrt(spread + eps) * scales + shifts


def gelu_exact(values):
    return jax.nn.gelu(values, approximate=False)


def valid_tokens(lengths_row, offset, amount, cluster):
    padded = (lengths_row + cluster - 1) // cluster * cluster
    starts = jnp.cumsum(padded) - padded
    position = offset + jnp.arange(amount, dtype=jnp.int32)
    inside = (position[:, None] >= starts[None, :]) & (
        position[:, None] < (starts + lengths_row)[None, :]
    )
    return jnp.any(inside, axis=1)


def move(one_hot, rows):
    return dot32(one_hot, rows).astype(jnp.bfloat16)


def move_back(one_hot, rows):
    picked = jnp.einsum("pi,pd->id", one_hot, rows, preferred_element_type=jnp.float32)
    return picked.astype(jnp.bfloat16)


def exchange(rows):
    return lax.all_to_all(rows, "tok", split_axis=0, concat_axis=0, tiled=True)


def per_device(
    tokens_in, w_qkv, b_query, b_value, w_out, b_out, norm1_gain, norm1_shift,
    w_up, b_up, w_down, b_down, norm2_gain, norm2_shift, out_grad, doc_lengths, cluster_slots,
):
    tok_dev, width = tokens_in.shape
    head_size = width // H
    clusters = tok_dev // CLU
    n_tok = lax.axis_size("tok")
    per_peer = tok_dev // n_tok
    my_index = lax.axis_index("tok")
    f32 = jnp.float32

    usable = valid_tokens(doc_lengths[0], my_index * tok_dev, tok_dev, CLU)
    dest = cluster_slots // tok_dev
    dest_hot = (dest[:, None] == jnp.arange(n_tok)[None, :]).astype(jnp.int32)
    rank = jnp.sum((jnp.cumsum(dest_hot, axis=0) - dest_hot) * dest_hot, axis=1)
    send_pos = dest * per_peer + rank
    send_hot = (jnp.arange(tok_dev)[:, None] == send_pos[None, :])
    note = (cluster_slots % tok_dev) * 2 + usable.astype(jnp.int32)
    sent_note = jnp.sum(jnp.where(send_hot, note[None, :], 0), axis=1)
    send_hot = send_hot.astype(jnp.bfloat16)
    got_note = exchange(sent_note)
    x_got = exchange(move(send_hot, tokens_in))
    g_got = exchange(move(send_hot, out_grad))
    place_hot = jnp.arange(tok_dev)[:, None] == (got_note // 2)[None, :]
    key_live = jnp.sum(jnp.where(place_hot, got_note[None, :] % 2, 0), axis=1) > 0
    place_hot = place_hot.astype(jnp.bfloat16)
    x = move(place_hot, x_got)

    bias_qkv = jnp.concatenate(
        [b_query.astype(f32), jnp.zeros((width,), f32), b_value.astype(f32)]
    )
    qkv = (dot32(x, w_qkv) + bias_qkv).astype(jnp.bfloat16)
    packed = qkv.reshape(clusters, CLU, 3, H, head_size)
    query, keys, value = packed[:, :, 0], packed[:, :, 1], packed[:, :, 2]
    scale = head_size ** (-0.5)
    scores = jnp.einsum("bqhd,bkhd->bhqk", query, keys, preferred_element_type=f32) * scale
    scores = jnp.where(key_live.reshape(clusters, 1, 1, CLU), scores, masked_score)
    expo = jnp.exp(scores - jnp.max(scores, axis=-1, keepdims=True))
    probs = expo / jnp.sum(expo, axis=-1, keepdims=True)
    weights = probs.astype(jnp.bfloat16)
    context = jnp.einsum("bhqk,bkhd->bqhd", weights, value, preferred_element_type=f32)
    context = context.astype(jnp.bfloat16).reshape(tok_dev, width)

    resid1 = x.astype(f32) + dot32(context, w_out) + b_out.astype(f32)
    normed1, norm1_back = jax.vjp(
        norm_rows, resid1, norm1_gain.astype(f32), norm1_shift.astype(f32)
    )
    normed1_low = normed1.astype(jnp.bfloat16)
    up_pre = dot32(normed1_low, w_up) + b_up.astype(f32)
    gelu_out, gelu_back = jax.vjp(gelu_exact, up_pre)
    gelu_low = gelu_out.astype(jnp.bfloat16)
    down_out = dot32(gelu_low, w_down) + b_down.astype(f32)
    normed2, norm2_back = jax.vjp(
        norm_rows, normed1 + down_out, norm2_gain.astype(f32), norm2_shift.astype(f32)
    )
    out_got = exchange(move_back(place_hot, normed2.astype(jnp.bfloat16)))
    block_out = move_back(send_hot, out_got)

    g = move(place_hot, g_got)
    grad_resid2, grad_gain2, grad_shift2 = norm2_back(g.astype(f32))
    grad_down = grad_resid2.astype(jnp.bfloat16)
    grad_b_down = jnp.sum(grad_down.astype(f32), axis=0)
    grad_w_down = jnp.einsum("nf,nd->fd", gelu_low, grad_down, preferred_element_type=f32)
    grad_gelu = jnp.einsum("nd,fd->nf", grad_down, w_down, preferred_element_type=f32)
    grad_up = gelu_back(grad_gelu)[0].astype(jnp.bfloat16)
    grad_b_up = jnp.sum(grad_up.astype(f32), axis=0)
    grad_w_up = jnp.einsum("nd,nf->df", normed1_low, grad_up, preferred_element_type=f32)
    grad_normed1 = grad_resid2 + jnp.einsum(
        "nf,df->nd", grad_up, w_up, preferred_element_type=f32
    )
    grad_resid1, grad_gain1, grad_shift1 = norm1_back(grad_normed1)
    grad_attn = grad_resid1.astype(jnp.bfloat16)
    grad_b_out = jnp.sum(grad_attn.astype(f32), axis=0)
    grad_w_out = jnp.einsum("nd,ne->de", context, grad_attn, preferred_element_type=f32)
    grad_context = jnp.einsum("ne,de->nd", grad_attn, w_out, preferred_element_type=f32)
    grad_context = grad_context.astype(jnp.bfloat16).reshape(clusters, CLU, H, head_size)

    grad_probs = jnp.einsum("bqhd,bkhd->bhqk", grad_context, value, preferred_element_type=f32)
    row_dot = jnp.sum(grad_probs * probs, axis=-1, keepdims=True)
    grad_scores = (probs * (grad_probs - row_dot)).astype(jnp.bfloat16)
    grad_q = jnp.einsum("bhqk,bkhd->bqhd", grad_scores, keys, preferred_element_type=f32) * scale
    grad_k = jnp.einsum("bhqk,bqhd->bkhd", grad_scores, query, preferred_element_type=f32) * scale
    grad_v = jnp.einsum("bhqk,bqhd->bkhd", weights, grad_context, preferred_element_type=f32)
    grad_qkv = jnp.stack([grad_q, grad_k, grad_v], axis=2).astype(jnp.bfloat16)
    grad_qkv = grad_qkv.reshape(tok_dev, 3 * width)
    grad_total = grad_resid1 + jnp.einsum(
        "ne,de->nd", grad_qkv, w_qkv, preferred_element_type=f32
    )
    back_got = exchange(move_back(place_hot, grad_total.astype(jnp.bfloat16)))
    grad_tokens = move_back(send_hot, back_got)
    grad_w_qkv = jnp.einsum("nd,ne->de", x, grad_qkv, preferred_element_type=f32)
    grad_qkv_sum = jnp.sum(grad_qkv.astype(f32), axis=0)

    low = jnp.bfloat16
    wide = jnp.concatenate(
        [
            grad_w_qkv.astype(low), grad_w_out.astype(low), grad_w_up.astype(low),
            grad_w_down.astype(low).reshape(width, -1),
        ],
        axis=1,
    )
    narrow = jnp.concatenate(
        [
            member.reshape(n_tok, -1)
            for member in (
                grad_qkv_sum[:width], grad_qkv_sum[2 * width :], grad_b_out, grad_gain1,
                grad_shift1, grad_b_down, grad_gain2, grad_shift2, grad_b_up,
            )
        ],
        axis=1,
    )
    share = lax.psum_scatter(wide, "tok", scatter_dimension=0, tiled=True)
    share = lax.psum(share, "grp").astype(f32)
    narrow = lax.psum(narrow, ("grp", "tok"))
    mine = lax.dynamic_index_in_dim(narrow, my_index, 0, keepdims=False)
    step = width // n_tok
    parts = [mine[i * step : (i + 1) * step] for i in range(8)] + [mine[8 * step :]]
    ffw = w_up.shape[1]
    return (
        block_out,
        grad_tokens,
        share[:, : 3 * width],
        parts[0],
        parts[1],
        share[:, 3 * width : 4 * width],
        parts[2],
        parts[3],
        parts[4],
        share[:, 4 * width : 4 * width + ffw],
        parts[8],
        share[:, 4 * width + ffw :].reshape(ffw // n_tok, width),
        parts[5],
        parts[6],
        parts[7],
    )


def solution(mesh):
    n_tok = mesh.shape["tok"]

    def body(*args):
        even = (args[0].shape[0] // n_tok) % 128 == 0 and n_tok & (n_tok - 1) == 0
        return (per_device_fast if even and mesh.shape["grp"] == 4 else per_device)(*args)

    rows = P(("grp", "tok"), None)
    in_specs = (rows,) + (P(),) * 13 + (rows, P("grp", None), P(("grp", "tok")))
    shares = (
        P("tok", None), P("tok"), P("tok"), P("tok", None), P("tok"), P("tok"), P("tok"),
        P("tok", None), P("tok"), P("tok", None), P("tok"), P("tok"), P("tok"),
    )
    return jax.shard_map(
        body, mesh=mesh, in_specs=in_specs, out_specs=(rows, rows) + shares, check_vma=False
    )
```

```python
import functools

import jax
import jax.numpy as jnp
from jax import lax
from jax.experimental import pallas as pl
from jax.experimental.pallas import tpu as pltpu
from jax.sharding import PartitionSpec as P

H = 12
CLU = 128

eps = 1e-12
masked_score = -1000000000.0

MESH = pl.DeviceIdType.MESH
f32 = jnp.float32
bf16 = jnp.bfloat16
BLK = 256


def dot32(a, b):
    return jnp.dot(a, b, preferred_element_type=jnp.float32)


def dot_rows(a, b):
    return lax.dot_general(a, b, (((1,), (1,)), ((), ())), preferred_element_type=jnp.float32)


def dot_cols(a, b):
    return lax.dot_general(a, b, (((0,), (0,)), ((), ())), preferred_element_type=jnp.float32)


def peer_order(n_tok):
    return sorted(range(1, n_tok), key=lambda k: -k)


def row_of(ref):
    return ref[...].astype(f32)[None, :]


def norm_parts(values):
    centre = values - jnp.mean(values, axis=-1, keepdims=True)
    spread = jnp.mean(centre * centre, axis=-1, keepdims=True)
    rstd = lax.rsqrt(spread + eps)
    return centre * rstd, rstd


def lane_halves(width):
    lane = lax.broadcasted_iota(jnp.int32, (1, width), 1)
    low = (lane < width // 2).astype(f32)
    return low.astype(bf16), (1.0 - low).astype(bf16)


def stack_heads(pair, halves):
    return jnp.concatenate([pair * halves[0], pair * halves[1]], axis=0)


def one_over_other(pair):
    half = pair.shape[1] // 2
    return jnp.concatenate([pair[:, :half], pair[:, half:]], axis=0)


def column_of(row):
    amount = row.shape[1]
    return jnp.concatenate(
        [
            jnp.broadcast_to(row[:, at : at + 128], (128, 128)).T
            for at in range(0, amount, 128)
        ],
        axis=0,
    )


def hot_from_column(column, amount):
    lane = lax.broadcasted_iota(jnp.int32, column.shape, 1).astype(f32)
    return jnp.concatenate(
        [(lane + float(at) == column).astype(f32).astype(bf16) for at in range(0, amount, 128)],
        axis=1,
    )


def forward_kernel(
    n_tok, per,
    slots_ref, docs_ref, tok_ref, og_ref, wq_ref, bq_ref, bv_ref, wo_ref, bo_ref, g1_ref, s1_ref,
    wu_ref, bu_ref, wd_ref, bd_ref, g2_ref, s2_ref,
    xc_o, gc_o, qkv_o, p_o, ctx_o, r1_o, n1_o, gelu_o, gelup_o, r2_o, back_o, col_o, pos_o,
    xh, gh, xs, gs, xr, gr, hot, note_s, note_r, wq, wo, wu, wd, live_s,
    xc_t, qkv_t, p_t, ctx_t, r1_t, n1_t, gelu_t, gelup_t, r2_t, bo_c, back_t, gc_t, col_t, pos_t,
    load_sem, note_ss, note_rs, x_ss, x_rs, g_ss, g_rs, own_sem, out_sem, last_sem,
):
    rows, width = xh.shape
    ffw = wu.shape[1]
    blocks = rows // BLK
    grp = lax.axis_index("grp")
    me = lax.axis_index("tok")
    order = peer_order(n_tok)

    barrier = pltpu.get_barrier_semaphore()
    for k in order:
        pl.semaphore_signal(barrier, inc=1, device_id=(grp, me ^ k), device_id_type=MESH)

    loads = [
        pltpu.make_async_copy(src, dst, load_sem.at[i])
        for i, (src, dst) in enumerate(
            ((tok_ref, xh), (og_ref, gh), (wq_ref, wq), (wo_ref, wo), (wu_ref, wu), (wd_ref, wd))
        )
    ]
    loads[0].start()

    def note_copy(k):
        return pltpu.make_async_remote_copy(
            src_ref=note_s.at[me ^ k], dst_ref=note_r.at[me], send_sem=note_ss.at[k],
            recv_sem=note_rs.at[k], device_id=(grp, me ^ k), device_id_type=MESH,
        )

    def row_copy(src, dst, ss, rs, k):
        return pltpu.make_async_remote_copy(
            src_ref=src.at[pl.ds(pl.multiple_of((me ^ k) * per, per), per)],
            dst_ref=dst.at[pl.ds(pl.multiple_of(me * per, per), per)],
            send_sem=ss.at[k], recv_sem=rs.at[k], device_id=(grp, me ^ k), device_id_type=MESH,
        )

    slots = slots_ref[...][None, :]
    dest = jnp.right_shift(slots, rows.bit_length() - 1)
    within = jnp.bitwise_and(slots, rows - 1)
    lanes = lax.broadcasted_iota(jnp.int32, (1, rows), 1)
    dest_hot = lax.broadcasted_iota(jnp.int32, (16, rows), 0) == dest
    dest_hot = dest_hot.astype(f32)
    before = lax.broadcasted_iota(jnp.int32, (BLK, rows), 1)
    rank = jnp.zeros((16, rows), f32)
    for b in range(blocks):
        earlier = lax.broadcasted_iota(jnp.int32, (BLK, rows), 0) + b * BLK < before
        rank += dot32(
            dest_hot[:, b * BLK : (b + 1) * BLK].astype(bf16), earlier.astype(f32).astype(bf16)
        )
    rank = jnp.sum(rank * dest_hot, axis=0, keepdims=True).astype(jnp.int32)
    pos = dest * per + rank
    spot = lax.broadcasted_iota(jnp.int32, (BLK, rows), 0)
    chip = lax.div(me * per, BLK)
    loads[0].wait()
    for copy in loads[1:]:
        copy.start()
    for j in range(blocks - 1, -1, -1):
        at = pl.multiple_of((chip ^ j) * BLK, BLK)
        picked = (spot + at == pos).astype(f32).astype(bf16)
        hot[pl.ds(at, BLK), :] = picked
        xs[pl.ds(at, BLK), :] = dot32(picked, xh[...]).astype(bf16)
        if j == blocks - 1:
            pl.semaphore_wait(barrier, n_tok - 1)
        for k in order:
            if k // (BLK // per) == j:
                row_copy(xs, xr, x_ss, x_rs, k).start()
    mine = pl.ds(pl.multiple_of(me * per, per), per)
    own_x = pltpu.make_async_copy(xs.at[mine], xr.at[mine], own_sem.at[0])
    own_x.start()

    pos_t[...] = jnp.broadcast_to(pos, (8, rows))
    start = jnp.int32(0)
    position = lanes + me * rows
    usable = jnp.zeros((1, rows), jnp.int32)
    for i in range(docs_ref.shape[1]):
        length = docs_ref[0, i]
        inside = (position >= start) & (position < start + length)
        usable = jnp.where(inside, 1, usable)
        start = start + jnp.bitwise_and(length + (CLU - 1), -CLU)
    kind = lax.broadcasted_iota(jnp.int32, (16, rows), 0)
    notes = jnp.where(
        kind == 0,
        jnp.right_shift(within, 5),
        jnp.where(kind == 1, jnp.bitwise_and(within, 31), jnp.where(kind == 2, usable, 0)),
    )
    notes = dot_rows(notes.astype(f32).astype(bf16), hot[...]).astype(bf16)
    for d in range(n_tok):
        note_s[d] = notes[:, d * per : (d + 1) * per]
    for k in order:
        note_copy(k).start()
    own_note = pltpu.make_async_copy(note_s.at[me], note_r.at[me], own_sem.at[1])
    own_note.start()
    loads[1].wait()
    for b in range(blocks):
        sl = pl.ds(b * BLK, BLK)
        gs[sl, :] = dot32(hot[sl, :], gh[...]).astype(bf16)
    own_g = pltpu.make_async_copy(gs.at[mine], gr.at[mine], own_sem.at[2])
    own_g.start()

    own_note.wait()
    for k in order:
        note_copy(k).wait_recv()
    got = jnp.concatenate([note_r[d] for d in range(n_tok)], axis=1)
    got32 = got.astype(f32)
    slot_row = got32[0:1, :] * 32.0 + got32[1:2, :]
    col_t[...] = column_of(slot_row)
    slot_row = slot_row.astype(jnp.int32)
    for b in range(blocks):
        spot = lax.broadcasted_iota(jnp.int32, (BLK, rows), 0) + b * BLK
        hot[b * BLK : (b + 1) * BLK, :] = (spot == slot_row).astype(f32).astype(bf16)
    live_s[...] = column_of(dot_rows(got, hot[...])[2:3, :])

    def gather_rows(source, target, own, copy):
        for j in range(blocks):
            if j == 0:
                own.wait()
            for k in range(1, n_tok):
                if k // (BLK // per) == j:
                    copy(k).wait_recv()
            at = pl.multiple_of((chip ^ j) * BLK, BLK)
            for b in range(blocks):
                sl = pl.ds(b * BLK, BLK)
                part = dot32(hot[sl, pl.ds(at, BLK)], source[pl.ds(at, BLK), :]).astype(bf16)
                target[sl, :] = part if j == 0 else target[sl, :] + part

    for k in order:
        row_copy(xs, xr, x_ss, x_rs, k).wait_send()
    for k in order:
        row_copy(gs, gr, g_ss, g_rs, k).start()
    gather_rows(xr, xc_t, own_x, lambda k: row_copy(xs, xr, x_ss, x_rs, k))
    xc_out = pltpu.make_async_copy(xc_t, xc_o, last_sem.at[4])
    xc_out.start()
    for copy in loads[2:]:
        copy.wait()

    halves = lane_halves(2 * width // H)
    pair_width = 2 * width // H
    scale = (width // H) ** (-0.5)
    outs = (
        (qkv_t, qkv_o, BLK), (p_t, p_o, BLK * H // 2), (ctx_t, ctx_o, BLK), (r1_t, r1_o, BLK),
        (n1_t, n1_o, BLK), (gelu_t, gelu_o, BLK), (gelup_t, gelup_o, BLK), (r2_t, r2_o, BLK),
    )

    def out_copy(i, b, slot):
        tile, whole, count = outs[i]
        return pltpu.make_async_copy(
            tile.at[slot], whole.at[pl.ds(pl.multiple_of(b * count, count), count)], out_sem.at[slot, i]
        )

    def block(b, carry):
        slot = lax.rem(b, 2)
        sl = pl.ds(pl.multiple_of(b * BLK, BLK), BLK)

        @pl.when(b >= 2)
        def _():
            for i in range(len(outs)):
                out_copy(i, b - 2, slot).wait()

        x = xc_t[sl, :]
        for part, bias in ((0, row_of(bq_ref)), (1, None), (2, row_of(bv_ref))):
            got_part = dot32(x, wq[:, part * width : (part + 1) * width])
            if bias is not None:
                got_part = got_part + bias
            qkv_t[slot, :, part * width : (part + 1) * width] = got_part.astype(bf16)
        for c in range(BLK // CLU):
            at = pl.multiple_of(b * BLK + c * CLU, CLU)
            live = live_s[pl.ds(at, CLU), :] > 0.5
            live = jnp.concatenate([live, live], axis=1)
            crow = pl.ds(c * CLU, CLU)
            for p in range(H // 2):
                cols = [pl.ds(part * width + p * pair_width, pair_width) for part in range(3)]
                q2 = stack_heads(qkv_t[slot, crow, cols[0]], halves)
                k2 = qkv_t[slot, crow, cols[1]]
                v2 = stack_heads(qkv_t[slot, crow, cols[2]], halves)
                scores = jnp.where(live, dot_rows(k2, q2) * scale, masked_score)
                expo = jnp.exp(scores - jnp.max(scores, axis=0, keepdims=True))
                weights = (expo / jnp.sum(expo, axis=0, keepdims=True)).astype(bf16)
                p_t[slot, pl.ds((c * (H // 2) + p) * CLU, CLU), :] = weights
                context = dot_cols(one_over_other(weights), v2)
                ctx_t[slot, crow, pl.ds(p * pair_width, pair_width)] = context.astype(bf16)
        resid1 = x.astype(f32) + (dot32(ctx_t[slot], wo[...]) + row_of(bo_ref))
        r1_t[slot] = resid1
        hat1, _ = norm_parts(resid1)
        normed1 = hat1 * row_of(g1_ref) + row_of(s1_ref)
        low1 = normed1.astype(bf16)
        n1_t[slot] = low1
        down = None
        step = width
        for j in range(ffw // step):
            cs = pl.ds(j * step, step)
            up = dot32(low1, wu[:, cs]) + bu_ref[cs].astype(f32)[None, :]
            phi = 0.5 * (1.0 + lax.erf(up * 0.7071067811865476))
            slope = phi + up * jnp.exp(up * up * -0.5) * 0.3989422804014327
            act = (up * phi).astype(bf16)
            gelu_t[slot, :, cs] = act
            gelup_t[slot, :, cs] = slope.astype(bf16)
            term = dot32(act, wd[cs, :])
            down = term if down is None else down + term
        resid2 = normed1 + (down + row_of(bd_ref))
        r2_t[slot] = resid2
        hat2, _ = norm_parts(resid2)
        bo_c[sl, :] = (hat2 * row_of(g2_ref) + row_of(s2_ref)).astype(bf16)
        for i in range(len(outs)):
            out_copy(i, b, slot).start()
        return carry

    lax.fori_loop(0, blocks, block, 0)

    col_out = pltpu.make_async_copy(col_t, col_o, last_sem.at[0])
    col_out.start()
    pos_out = pltpu.make_async_copy(pos_t, pos_o, last_sem.at[1])
    pos_out.start()
    for b in range(blocks):
        sl = pl.ds(b * BLK, BLK)
        back_t[sl, :] = dot32(hot_from_column(col_t[sl, :], rows), bo_c[...]).astype(bf16)
    back_out = pltpu.make_async_copy(back_t, back_o, last_sem.at[2])
    back_out.start()
    gather_rows(gr, gc_t, own_g, lambda k: row_copy(gs, gr, g_ss, g_rs, k))
    gc_out = pltpu.make_async_copy(gc_t, gc_o, last_sem.at[3])
    gc_out.start()
    for k in order:
        note_copy(k).wait_send()
        row_copy(gs, gr, g_ss, g_rs, k).wait_send()
    for b in range(max(blocks - 2, 0), blocks):
        for i in range(len(outs)):
            out_copy(i, b, b % 2).wait()
    col_out.wait()
    pos_out.wait()
    back_out.wait()
    gc_out.wait()
    xc_out.wait()


def forward(n_tok, tokens_in, w_qkv, b_query, b_value, w_out, b_out, norm1_gain, norm1_shift,
            w_up, b_up, w_down, b_down, norm2_gain, norm2_shift, out_grad, doc_lengths, cluster_slots):
    rows, width = tokens_in.shape
    ffw = w_up.shape[1]
    per = rows // n_tok
    vm = pl.BlockSpec(memory_space=pltpu.VMEM)
    sm = pl.BlockSpec(memory_space=pltpu.SMEM)
    hb = pl.BlockSpec(memory_space=pl.ANY)
    out_shape = [
        ((rows, width), bf16), ((rows, width), bf16), ((rows, 3 * width), bf16), ((rows * H // 2, 2 * CLU), bf16),
        ((rows, width), bf16), ((rows, width), f32), ((rows, width), bf16), ((rows, ffw), bf16),
        ((rows, ffw), bf16), ((rows, width), f32), ((rows, width), bf16), ((rows, 128), f32),
        ((8, rows), jnp.int32),
    ]
    vmem = pltpu.VMEM
    dma = pltpu.SemaphoreType.DMA
    scratch = (
        [vmem((rows, width), bf16)] * 6
        + [vmem((rows, rows), bf16), vmem((n_tok, 16, per), bf16), vmem((n_tok, 16, per), bf16)]
        + [vmem(w_qkv.shape, bf16), vmem(w_out.shape, bf16), vmem(w_up.shape, bf16), vmem(w_down.shape, bf16)]
        + [vmem((rows, 128), f32)]
        + [
            vmem((rows, width), bf16), vmem((2, BLK, 3 * width), bf16), vmem((2, BLK * H // 2, 2 * CLU), bf16),
            vmem((2, BLK, width), bf16), vmem((2, BLK, width), f32), vmem((2, BLK, width), bf16),
            vmem((2, BLK, ffw), bf16), vmem((2, BLK, ffw), bf16), vmem((2, BLK, width), f32),
            vmem((rows, width), bf16), vmem((rows, width), bf16), vmem((rows, width), bf16),
            vmem((rows, 128), f32), vmem((8, rows), jnp.int32),
        ]
        + [dma((6,))] + [dma((n_tok,))] * 6 + [dma((3,)), dma((2, 8)), dma((5,))]
    )
    return pl.pallas_call(
        functools.partial(forward_kernel, n_tok, per),
        out_shape=[jax.ShapeDtypeStruct(s, d) for s, d in out_shape],
        in_specs=[vm, sm, hb, hb, hb, vm, vm, hb, vm, vm, vm, hb, vm, hb, vm, vm, vm],
        out_specs=[hb] * len(out_shape),
        scratch_shapes=scratch,
        compiler_params=pltpu.CompilerParams(
            collective_id=0, has_side_effects=True, vmem_limit_bytes=60 * 2**20
        ),
        name="layer_forward",
    )(cluster_slots, doc_lengths, tokens_in, out_grad, w_qkv, b_query, b_value, w_out, b_out, norm1_gain,
      norm1_shift, w_up, b_up, w_down, b_down, norm2_gain, norm2_shift)


def grad_kinds(width, ffw, n_tok):
    return ((ffw // n_tok, width), (width // n_tok, ffw), (width // n_tok, width), (width // n_tok, 3 * width))


def backward_kernel(n_tok, per, kinds, *refs):
    (xc_ref, gc_ref, qkv_ref, p_ref, ctx_ref, r1_ref, n1_ref, gelu_ref, gelup_ref, r2_ref, back_ref, col_ref,
     wq_ref, wo_ref, wu_ref, wd_ref, g1_ref, g2_ref) = refs[:18]
    refs = refs[18:]
    bo_got, gt_got, nar_o = refs[:3]
    shares = refs[3:7]
    refs = refs[7:]
    (wq, wo, wu, wd, gwd, gelu, gup, low1, gdown, resid, grow, ctx, gattn, gcl, qkv, probs, land0, col,
     nar_v, bup_v, nar_s, nar_r, nar_g, nar_h, nar_t,
     load_sem, bo_ss, bo_rs, gt_ss, gt_rs, own_sem, s0_ss, s0_rs, x1_ss, x1_rs, x2_ss, x2_rs, za_ss, za_rs,
     zb_ss, zb_rs, ag_ss, ag_rs, fin_sem, free_sem, nt_ss, nt_rs, ng_ss, ng_rs) = refs
    rows, width = low1.shape
    ffw = wu.shape[1]
    blocks = rows // BLK
    grp = lax.axis_index("grp")
    me = lax.axis_index("tok")
    core = lax.rem(me, 2)
    chip = lax.div(me, 2)
    chips = n_tok // 2
    gx = lax.rem(grp, 2)
    gy = lax.div(grp, 2)
    order = peer_order(n_tok)
    mats = (gwd, wu, wo, wq)

    barrier = pltpu.get_barrier_semaphore()
    for k in order:
        pl.semaphore_signal(barrier, inc=1, device_id=(grp, me ^ k), device_id_type=MESH)
    for k in (1, 2, 3):
        pl.semaphore_signal(barrier, inc=1, device_id=(grp ^ k, me), device_id_type=MESH)

    load = {
        name: pltpu.make_async_copy(src, dst, load_sem.at[i])
        for i, (name, src, dst) in enumerate((
            ("gc", gc_ref, gcl), ("r2", r2_ref, resid), ("gelu", gelu_ref, gelu), ("wd", wd_ref, wd),
            ("gelup", gelup_ref, gup), ("wu", wu_ref, wu), ("n1", n1_ref, low1), ("wo", wo_ref, wo),
            ("ctx", ctx_ref, ctx), ("qkv", qkv_ref, qkv), ("p", p_ref, probs), ("wq", wq_ref, wq),
            ("xc", xc_ref, gattn), ("col", col_ref, col), ("r1", r1_ref, resid),
        ))
    }

    def begin(*names):
        for name in names:
            load[name].start()

    def ready(*names):
        for name in names:
            load[name].wait()

    begin("gc", "r2")

    def row_copy(src, dst, ss, rs, k):
        return pltpu.make_async_remote_copy(
            src_ref=src.at[pl.ds(pl.multiple_of((me ^ k) * per, per), per)],
            dst_ref=dst.at[pl.ds(pl.multiple_of(me * per, per), per)],
            send_sem=ss.at[k], recv_sem=rs.at[k], device_id=(grp, me ^ k), device_id_type=MESH,
        )

    mine = pl.ds(pl.multiple_of(me * per, per), per)
    def held(m, z, row0, count, col0, ncols):
        share, _ = kinds[m]
        at = (2 * z + core) * share + row0
        return mats[m].at[pl.ds(pl.multiple_of(at, 16), count), pl.ds(pl.multiple_of(col0, 128), ncols)]

    zones = (land0, gelu, gup, gup)
    zone_col = (0, 0, 3 * width, 0)

    def land(m, row, count, half_at, whole):
        share, cols = kinds[m]
        ncols = cols if whole else cols // 2
        return zones[m].at[pl.ds(row, count), pl.ds(zone_col[m] + half_at * (cols // 2), ncols)]

    def land_s0(m, z):
        share = kinds[m][0]
        return land(m, z * share, share, 0, True)

    def land_x1(m, z):
        share = kinds[m][0]
        if first_x(z):
            return land(m, (chips + z) * share, share, 0, False)
        return land(m, (chips + 2) * share + (z - chips // 2) * (share // 2), share // 2, 0, True)

    def land_x2(m, z):
        share = kinds[m][0]
        return land(m, chips * share + z * (share // 2), share // 2, 1, False)

    def land_za(m, i):
        share = kinds[m][0]
        return land(m, (chips + 3) * share, share // 2, i, False)

    def land_zb(m):
        share = kinds[m][0]
        return land(m, (chips + 3) * share + share // 2, share // 2, 0, False)

    partners = ((grp, me ^ 1), (grp ^ 1, me), (grp ^ 2, me), (grp, me ^ 2), (grp, me ^ 4))

    def tell_free(i):
        for who in partners:
            pl.semaphore_signal(free_sem.at[i], inc=1, device_id=who, device_id_type=MESH)

    def partners_free(i):
        pl.semaphore_wait(free_sem.at[i], len(partners))

    def remote(src, dst, ss, rs, who):
        return pltpu.make_async_remote_copy(
            src_ref=src, dst_ref=dst, send_sem=ss, recv_sem=rs, device_id=who, device_id_type=MESH
        )

    def copy_s0(m, z):
        share, cols = kinds[m]
        at = (2 * z + 1 - core) * share
        return remote(
            mats[m].at[pl.ds(pl.multiple_of(at, 16), share)], land_s0(m, z),
            s0_ss.at[m, z], s0_rs.at[m, z], (grp, me ^ 1),
        )

    def first_x(z):
        return z < chips // 2

    def copy_x1(m, z):
        share, cols = kinds[m]
        half, hcols = share // 2, cols // 2
        if first_x(z):
            src = held(m, z, 0, share, (1 - gx) * hcols, hcols)
            who = (grp ^ 1, me)
        else:
            src = held(m, z, (1 - gy) * half, half, 0, cols)
            who = (grp ^ 2, me)
        return remote(src, land_x1(m, z), x1_ss.at[m, z], x1_rs.at[m, z], who)

    def copy_x2(m, z):
        share, cols = kinds[m]
        half, hcols = share // 2, cols // 2
        if first_x(z):
            src, who = held(m, z, (1 - gy) * half, half, gx * hcols, hcols), (grp ^ 2, me)
        else:
            src, who = held(m, z, gy * half, half, (1 - gx) * hcols, hcols), (grp ^ 1, me)
        return remote(src, land_x2(m, z), x2_ss.at[m, z], x2_rs.at[m, z], who)

    def quarter(m, z):
        share, cols = kinds[m]
        half, hcols = share // 2, cols // 2
        return held(m, z, gy * half, half, gx * hcols, hcols)

    def copy_za(m, i):
        return remote(quarter(m, chip ^ (1 + 2 * i)), land_za(m, i), za_ss.at[m, i], za_rs.at[m, i], (grp, me ^ 2))

    def copy_zb(m):
        return remote(quarter(m, chip ^ 2), land_zb(m), zb_ss.at[m], zb_rs.at[m], (grp, me ^ 4))

    def share_part(m):
        share, cols = kinds[m]
        half, hcols = share // 2, cols // 2
        return shares[m].at[
            pl.ds(pl.multiple_of(gy * half, 16), half), pl.ds(pl.multiple_of(gx * hcols, 128), hcols)
        ]

    def own_part(m):
        return quarter(m, chip)

    def copy_ag(m, k):
        return remote(own_part(m), share_part(m), ag_ss.at[m, k], ag_rs.at[m, k], (grp ^ k, me))

    def own_ag(m):
        return pltpu.make_async_copy(own_part(m), share_part(m), fin_sem.at[m])

    def add_in(target, extra):
        target[...] = target[...] + extra[...]

    def start_s0(m):
        for z in range(chips):
            copy_s0(m, z).start()

    def step_r0(m, zs=None):
        share, cols = kinds[m]
        for z in zs or range(chips):
            copy_s0(m, z).wait_recv()
            add_in(held(m, z, 0, share, 0, cols), land_s0(m, z))
            copy_x1(m, z).start()

    def step_r1(m):
        share, cols = kinds[m]
        half, hcols = share // 2, cols // 2
        for z in range(chips):
            copy_x1(m, z).wait_recv()
            spot = (0, share, gx * hcols, hcols) if first_x(z) else (gy * half, half, 0, cols)
            add_in(held(m, z, *spot), land_x1(m, z))
            copy_x2(m, z).start()

    def step_r2(m):
        for z in range(chips):
            copy_x2(m, z).wait_recv()
            add_in(quarter(m, z), land_x2(m, z))
        copy_za(m, 0).start()
        copy_za(m, 1).start()

    def step_ra(m):
        copy_za(m, 0).wait_recv()
        copy_za(m, 1).wait_recv()
        add_in(quarter(m, chip ^ 2), land_za(m, 1))
        copy_zb(m).start()
        add_in(own_part(m), land_za(m, 0))

    def step_rb(m):
        copy_zb(m).wait_recv()
        add_in(own_part(m), land_zb(m))
        for k in (3, 1, 2):
            copy_ag(m, k).start()
        own_ag(m).start()

    gain2 = row_of(g2_ref)
    gain1 = row_of(g1_ref)

    def norm_back(upstream, resid_rows, gain):
        hat, rstd = norm_parts(resid_rows)
        dh = upstream * gain
        inner = jnp.mean(dh * hat, axis=-1, keepdims=True)
        return rstd * (dh - jnp.mean(dh, axis=-1, keepdims=True) - hat * inner), hat

    def add_sum(at, values):
        nar_v[at : at + 1, :] += jnp.sum(values, axis=0, keepdims=True)

    nar_v[...] = jnp.zeros_like(nar_v)
    bup_v[...] = jnp.zeros_like(bup_v)
    own_bo = pltpu.make_async_copy(back_ref.at[mine], bo_got.at[mine], own_sem.at[0])
    ready("gc", "r2")
    begin("gelu", "wd", "gelup")
    for b in range(blocks):
        sl = pl.ds(b * BLK, BLK)
        g = gcl[sl, :].astype(f32)
        back, hat = norm_back(g, resid[sl, :], gain2)
        low = back.astype(bf16)
        grow[sl, :] = back
        gdown[sl, :] = low
        add_sum(5, low.astype(f32))
        add_sum(6, g * hat)
        add_sum(7, g)
        if b == 0:
            pl.semaphore_wait(barrier, n_tok - 1 + 3)
            for k in order:
                row_copy(back_ref, bo_got, bo_ss, bo_rs, k).start()
            own_bo.start()

    ready("gelu")
    begin("wu", "r1", "wo", "n1", "ctx")
    step = width
    for j in range(ffw // step):
        cs = pl.ds(j * step, step)
        gwd[cs, :] = dot_cols(gelu[:, cs], gdown[...]).astype(bf16)
        if step == 2 * kinds[0][0]:
            copy_s0(0, j).start()
    if step != 2 * kinds[0][0]:
        start_s0(0)
    tell_free(0)
    ready("wd", "gelup")
    for b in range(blocks):
        sl = pl.ds(b * BLK, BLK)
        for j in range(ffw // step):
            cs = pl.ds(j * step, step)
            up = (dot_rows(gdown[sl, :], wd[cs, :]) * gup[sl, cs].astype(f32)).astype(bf16)
            gup[sl, cs] = up
            bup_v[0:1, cs] += jnp.sum(up.astype(f32), axis=0, keepdims=True)
        if b == 1:
            step_r0(0, (0, 1))
    step_r0(0, (2, 3))
    begin("qkv", "p", "wq", "col")
    ready("wu", "r1", "wo")
    for b in range(blocks):
        sl = pl.ds(b * BLK, BLK)
        gn1 = grow[sl, :] + dot_rows(gup[sl, :], wu[...])
        back, hat = norm_back(gn1, resid[sl, :], gain1)
        low = back.astype(bf16)
        grow[sl, :] = back
        gattn[sl, :] = low
        add_sum(2, low.astype(f32))
        add_sum(3, gn1 * hat)
        add_sum(4, gn1)
        gcl[sl, :] = dot_rows(low, wo[...]).astype(bf16)
    ready("n1")
    for j in range(ffw // step):
        cs = pl.ds(j * step, step)
        wu[:, cs] = dot_cols(low1[...], gup[:, cs]).astype(bf16)
    tell_free(1)
    partners_free(0)
    start_s0(1)
    ready("ctx")
    wo[...] = dot_cols(ctx[...], gattn[...]).astype(bf16)
    begin("xc")
    partners_free(1)
    start_s0(2)
    step_r1(0)

    ready("qkv", "p", "wq")
    halves = lane_halves(2 * width // H)
    pair_width = 2 * width // H
    scale = (width // H) ** (-0.5)

    def attend(b):
        for c in range(BLK // CLU):
            crow = pl.ds(b * BLK + c * CLU, CLU)
            for p in range(H // 2):
                cols = [pl.ds(part * width + p * pair_width, pair_width) for part in range(3)]
                q2 = stack_heads(qkv[crow, cols[0]], halves)
                k2 = stack_heads(qkv[crow, cols[1]], halves)
                v2 = qkv[crow, cols[2]]
                go = stack_heads(gcl[crow, pl.ds(p * pair_width, pair_width)], halves)
                weights = probs[pl.ds(((b * BLK // CLU + c) * (H // 2) + p) * CLU, CLU), :]
                weights32 = weights.astype(f32)
                gp = dot_rows(v2, go)
                dot = jnp.sum(gp * weights32, axis=0, keepdims=True)
                gs = (weights32 * (gp - dot)).astype(bf16)
                gq = (dot_cols(one_over_other(gs), k2) * scale).astype(bf16)
                gk = (dot32(gs, q2) * scale).astype(bf16)
                gv = dot32(weights, go).astype(bf16)
                qkv[crow, cols[0]] = gq
                qkv[crow, cols[1]] = gk
                qkv[crow, cols[2]] = gv
        sl = pl.ds(b * BLK, BLK)
        add_sum(0, qkv[sl, 0:width].astype(f32))
        add_sum(1, qkv[sl, 2 * width :].astype(f32))
        total = grow[sl, :] + dot_rows(qkv[sl, :], wq[...])
        low1[sl, :] = total.astype(bf16)

    attend(0)
    attend(1)
    step_r0(1)
    step_r0(2)
    attend(2)
    step_r2(0)
    attend(3)
    ready("xc", "col")
    for j in range(3):
        cs = pl.ds(j * step, step)
        wq[:, cs] = dot_cols(gattn[...], qkv[:, cs]).astype(bf16)
    start_s0(3)
    for b in range(blocks):
        sl = pl.ds(b * BLK, BLK)
        gdown[sl, :] = dot32(hot_from_column(col[sl, :], rows), low1[...]).astype(bf16)
    for k in order:
        row_copy(gdown, gt_got, gt_ss, gt_rs, k).start()
    own_gt = pltpu.make_async_copy(gdown.at[mine], gt_got.at[mine], own_sem.at[1])
    own_gt.start()
    step_ra(0)
    step_r0(3)
    step_r1(1)
    step_r1(2)

    each = width // n_tok
    at = lax.broadcasted_iota(jnp.int32, (width, n_tok * 128), 0)
    lane = lax.broadcasted_iota(jnp.int32, (width, n_tok * 128), 1)
    inner = jnp.bitwise_and(lane, 127)
    pick = (at == jnp.right_shift(lane, 7) * each + inner) & (inner < each)
    spread = jnp.dot(nar_v[...], pick.astype(f32), precision=lax.Precision.HIGHEST, preferred_element_type=f32)
    share_up = ffw // n_tok
    for d in range(n_tok):
        nar_s[d] = jnp.concatenate(
            [spread[0:8, d * 128 : (d + 1) * 128]]
            + [bup_v[0:1, d * share_up + i : d * share_up + i + 128] for i in range(0, share_up, 128)]
            + [jnp.zeros((8 - share_up // 128, 128), f32)], axis=0)

    def nar_copy(k):
        return remote(nar_s.at[me ^ k], nar_r.at[k], nt_ss.at[k], nt_rs.at[k], (grp, me ^ k))

    def nar_cross(k):
        return remote(nar_g, nar_h.at[k], ng_ss.at[k], ng_rs.at[k], (grp ^ k, me))

    for k in order:
        nar_copy(k).start()
    step_r1(3)
    step_rb(0)
    step_r2(1)
    step_r2(2)
    total = nar_s[me]
    for k in order:
        nar_copy(k).wait_recv()
        total += nar_r[k]
    nar_g[...] = total
    for k in (3, 1, 2):
        nar_cross(k).start()
    step_r2(3)
    step_ra(1)
    step_ra(2)
    step_ra(3)
    step_rb(1)
    step_rb(2)
    total = nar_g[...]
    for k in (1, 2, 3):
        nar_cross(k).wait_recv()
        total += nar_h[k]
    nar_t[...] = total
    nar_out = pltpu.make_async_copy(nar_t, nar_o, own_sem.at[2])
    nar_out.start()
    step_rb(3)

    own_bo.wait()
    own_gt.wait()
    nar_out.wait()
    for k in order:
        row_copy(back_ref, bo_got, bo_ss, bo_rs, k).wait()
        row_copy(gdown, gt_got, gt_ss, gt_rs, k).wait()
        nar_copy(k).wait_send()
    for k in (1, 2, 3):
        nar_cross(k).wait_send()
    for m in range(4):
        own_ag(m).wait()
        for z in range(chips):
            copy_s0(m, z).wait_send()
            copy_x1(m, z).wait_send()
            copy_x2(m, z).wait_send()
        copy_za(m, 0).wait_send()
        copy_za(m, 1).wait_send()
        copy_zb(m).wait_send()
        for k in (1, 2, 3):
            copy_ag(m, k).wait()


def backward(n_tok, saved, w_qkv, w_out, w_up, w_down, norm1_gain, norm2_gain):
    rows, width = saved[0].shape
    ffw = w_up.shape[1]
    per = rows // n_tok
    chips = n_tok // 2
    kinds = grad_kinds(width, ffw, n_tok)
    vm = pl.BlockSpec(memory_space=pltpu.VMEM)
    hb = pl.BlockSpec(memory_space=pl.ANY)
    outs = [((rows, width), bf16), ((rows, width), bf16), ((16, 128), f32)]
    outs += [(kind, bf16) for kind in kinds]
    vmem = pltpu.VMEM
    dma = pltpu.SemaphoreType.DMA
    scratch = [
        vmem(w_qkv.shape, bf16), vmem(w_out.shape, bf16), vmem(w_up.shape, bf16), vmem(w_down.shape, bf16),
        vmem(w_down.shape, bf16), vmem((rows, ffw), bf16), vmem((rows, ffw), bf16), vmem((rows, width), bf16),
        vmem((rows, width), bf16), vmem((rows, width), f32), vmem((rows, width), f32), vmem((rows, width), bf16),
        vmem((rows, width), bf16), vmem((rows, width), bf16), vmem((rows, 3 * width), bf16),
        vmem((rows * H // 2, 2 * CLU), bf16), vmem(w_down.shape, bf16), vmem((rows, 128), f32),
        vmem((16, width), f32), vmem((8, ffw), f32), vmem((n_tok, 16, 128), f32), vmem((n_tok, 16, 128), f32),
        vmem((16, 128), f32), vmem((4, 16, 128), f32), vmem((16, 128), f32),
        dma((15,)), dma((n_tok,)), dma((n_tok,)), dma((n_tok,)), dma((n_tok,)), dma((3,)),
    ]
    scratch += [dma((4, chips))] * 6 + [dma((4, 2))] * 2 + [dma((4,))] * 2
    scratch += [dma((4, 4))] * 2 + [dma((4,)), pltpu.SemaphoreType.REGULAR((2,))]
    scratch += [dma((n_tok,))] * 2 + [dma((4,))] * 2
    return pl.pallas_call(
        functools.partial(backward_kernel, n_tok, per, kinds),
        out_shape=[jax.ShapeDtypeStruct(s, d) for s, d in outs],
        in_specs=[hb] * 16 + [vm] * 2,
        out_specs=[hb] * len(outs),
        scratch_shapes=scratch,
        compiler_params=pltpu.CompilerParams(
            collective_id=1, has_side_effects=True, vmem_limit_bytes=63 * 2**20
        ),
        name="layer_backward",
    )(*saved, w_qkv, w_out, w_up, w_down, norm1_gain, norm2_gain)[:7]


def finish_kernel(pos_ref, bo_ref, gt_ref, nar_ref, wd_ref, wu_ref, wo_ref, wq_ref, *outs):
    (out_o, tok_o, wq_o, bq_o, bv_o, wo_o, b_out_o, g1_o, s1_o, wu_o, bu_o, wd_o, bd_o, g2_o, s2_o) = outs
    rows = bo_ref.shape[0]
    column = column_of(pos_ref[0:1, :].astype(f32))
    for b in range(rows // BLK):
        sl = pl.ds(b * BLK, BLK)
        home = hot_from_column(column[b * BLK : (b + 1) * BLK], rows)
        out_o[sl, :] = dot32(home, bo_ref[...]).astype(bf16)
        tok_o[sl, :] = dot32(home, gt_ref[...]).astype(bf16)
    for src, dst in ((wd_ref, wd_o), (wu_ref, wu_o), (wo_ref, wo_o), (wq_ref, wq_o)):
        dst[...] = src[...].astype(f32)
    for i, dst in enumerate((bq_o, bv_o, b_out_o, g1_o, s1_o, bd_o, g2_o, s2_o)):
        dst[...] = nar_ref[i, 0 : dst.shape[0]]
    for i in range(bu_o.shape[0] // 128):
        bu_o[i * 128 : (i + 1) * 128] = nar_ref[8 + i, :]


def finish(pos, got):
    bo, gt, nar, wd, wu, wo, wq = got
    rows, width = bo.shape
    each = wq.shape[0]
    vm = pl.BlockSpec(memory_space=pltpu.VMEM)
    outs = [
        (bo.shape, bf16), (gt.shape, bf16), (wq.shape, f32), ((each,), f32), ((each,), f32), (wo.shape, f32),
        ((each,), f32), ((each,), f32), ((each,), f32), (wu.shape, f32), ((wd.shape[0],), f32), (wd.shape, f32),
        ((each,), f32), ((each,), f32), ((each,), f32),
    ]
    return pl.pallas_call(
        finish_kernel,
        out_shape=[jax.ShapeDtypeStruct(s, d) for s, d in outs],
        in_specs=[vm] * 8,
        out_specs=[vm] * len(outs),
        compiler_params=pltpu.CompilerParams(vmem_limit_bytes=60 * 2**20),
        name="back_home",
    )(pos, bo, gt, nar, wd, wu, wo, wq)


def per_device_fast(
    tokens_in, w_qkv, b_query, b_value, w_out, b_out, norm1_gain, norm1_shift,
    w_up, b_up, w_down, b_down, norm2_gain, norm2_shift, out_grad, doc_lengths, cluster_slots,
):
    n_tok = lax.axis_size("tok")
    *saved, pos = forward(
        n_tok, tokens_in, w_qkv, b_query, b_value, w_out, b_out, norm1_gain, norm1_shift,
        w_up, b_up, w_down, b_down, norm2_gain, norm2_shift, out_grad, doc_lengths, cluster_slots)
    got = backward(n_tok, saved, w_qkv, w_out, w_up, w_down, norm1_gain, norm2_gain)
    return tuple(finish(pos, got))


def norm_rows(values, scales, shifts):
    centre = values - jnp.mean(values, axis=-1, keepdims=True)
    spread = jnp.mean(centre * centre, axis=-1, keepdims=True)
    return centre * lax.rsqrt(spread + eps) * scales + shifts


def gelu_exact(values):
    return jax.nn.gelu(values, approximate=False)


def valid_tokens(lengths_row, offset, amount, cluster):
    padded = (lengths_row + cluster - 1) // cluster * cluster
    starts = jnp.cumsum(padded) - padded
    position = offset + jnp.arange(amount, dtype=jnp.int32)
    inside = (position[:, None] >= starts[None, :]) & (
        position[:, None] < (starts + lengths_row)[None, :]
    )
    return jnp.any(inside, axis=1)


def move(one_hot, rows):
    return dot32(one_hot, rows).astype(jnp.bfloat16)


def move_back(one_hot, rows):
    picked = jnp.einsum("pi,pd->id", one_hot, rows, preferred_element_type=jnp.float32)
    return picked.astype(jnp.bfloat16)


def exchange(rows):
    return lax.all_to_all(rows, "tok", split_axis=0, concat_axis=0, tiled=True)


def per_device(
    tokens_in, w_qkv, b_query, b_value, w_out, b_out, norm1_gain, norm1_shift,
    w_up, b_up, w_down, b_down, norm2_gain, norm2_shift, out_grad, doc_lengths, cluster_slots,
):
    tok_dev, width = tokens_in.shape
    head_size = width // H
    clusters = tok_dev // CLU
    n_tok = lax.axis_size("tok")
    per_peer = tok_dev // n_tok
    my_index = lax.axis_index("tok")
    f32 = jnp.float32

    usable = valid_tokens(doc_lengths[0], my_index * tok_dev, tok_dev, CLU)
    dest = cluster_slots // tok_dev
    dest_hot = (dest[:, None] == jnp.arange(n_tok)[None, :]).astype(jnp.int32)
    rank = jnp.sum((jnp.cumsum(dest_hot, axis=0) - dest_hot) * dest_hot, axis=1)
    send_pos = dest * per_peer + rank
    send_hot = (jnp.arange(tok_dev)[:, None] == send_pos[None, :])
    note = (cluster_slots % tok_dev) * 2 + usable.astype(jnp.int32)
    sent_note = jnp.sum(jnp.where(send_hot, note[None, :], 0), axis=1)
    send_hot = send_hot.astype(jnp.bfloat16)
    got_note = exchange(sent_note)
    x_got = exchange(move(send_hot, tokens_in))
    g_got = exchange(move(send_hot, out_grad))
    place_hot = jnp.arange(tok_dev)[:, None] == (got_note // 2)[None, :]
    key_live = jnp.sum(jnp.where(place_hot, got_note[None, :] % 2, 0), axis=1) > 0
    place_hot = place_hot.astype(jnp.bfloat16)
    x = move(place_hot, x_got)

    bias_qkv = jnp.concatenate(
        [b_query.astype(f32), jnp.zeros((width,), f32), b_value.astype(f32)]
    )
    qkv = (dot32(x, w_qkv) + bias_qkv).astype(jnp.bfloat16)
    packed = qkv.reshape(clusters, CLU, 3, H, head_size)
    query, keys, value = packed[:, :, 0], packed[:, :, 1], packed[:, :, 2]
    scale = head_size ** (-0.5)
    scores = jnp.einsum("bqhd,bkhd->bhqk", query, keys, preferred_element_type=f32) * scale
    scores = jnp.where(key_live.reshape(clusters, 1, 1, CLU), scores, masked_score)
    expo = jnp.exp(scores - jnp.max(scores, axis=-1, keepdims=True))
    probs = expo / jnp.sum(expo, axis=-1, keepdims=True)
    weights = probs.astype(jnp.bfloat16)
    context = jnp.einsum("bhqk,bkhd->bqhd", weights, value, preferred_element_type=f32)
    context = context.astype(jnp.bfloat16).reshape(tok_dev, width)

    resid1 = x.astype(f32) + dot32(context, w_out) + b_out.astype(f32)
    normed1, norm1_back = jax.vjp(
        norm_rows, resid1, norm1_gain.astype(f32), norm1_shift.astype(f32)
    )
    normed1_low = normed1.astype(jnp.bfloat16)
    up_pre = dot32(normed1_low, w_up) + b_up.astype(f32)
    gelu_out, gelu_back = jax.vjp(gelu_exact, up_pre)
    gelu_low = gelu_out.astype(jnp.bfloat16)
    down_out = dot32(gelu_low, w_down) + b_down.astype(f32)
    normed2, norm2_back = jax.vjp(
        norm_rows, normed1 + down_out, norm2_gain.astype(f32), norm2_shift.astype(f32)
    )
    out_got = exchange(move_back(place_hot, normed2.astype(jnp.bfloat16)))
    block_out = move_back(send_hot, out_got)

    g = move(place_hot, g_got)
    grad_resid2, grad_gain2, grad_shift2 = norm2_back(g.astype(f32))
    grad_down = grad_resid2.astype(jnp.bfloat16)
    grad_b_down = jnp.sum(grad_down.astype(f32), axis=0)
    grad_w_down = jnp.einsum("nf,nd->fd", gelu_low, grad_down, preferred_element_type=f32)
    grad_gelu = jnp.einsum("nd,fd->nf", grad_down, w_down, preferred_element_type=f32)
    grad_up = gelu_back(grad_gelu)[0].astype(jnp.bfloat16)
    grad_b_up = jnp.sum(grad_up.astype(f32), axis=0)
    grad_w_up = jnp.einsum("nd,nf->df", normed1_low, grad_up, preferred_element_type=f32)
    grad_normed1 = grad_resid2 + jnp.einsum(
        "nf,df->nd", grad_up, w_up, preferred_element_type=f32
    )
    grad_resid1, grad_gain1, grad_shift1 = norm1_back(grad_normed1)
    grad_attn = grad_resid1.astype(jnp.bfloat16)
    grad_b_out = jnp.sum(grad_attn.astype(f32), axis=0)
    grad_w_out = jnp.einsum("nd,ne->de", context, grad_attn, preferred_element_type=f32)
    grad_context = jnp.einsum("ne,de->nd", grad_attn, w_out, preferred_element_type=f32)
    grad_context = grad_context.astype(jnp.bfloat16).reshape(clusters, CLU, H, head_size)

    grad_probs = jnp.einsum("bqhd,bkhd->bhqk", grad_context, value, preferred_element_type=f32)
    row_dot = jnp.sum(grad_probs * probs, axis=-1, keepdims=True)
    grad_scores = (probs * (grad_probs - row_dot)).astype(jnp.bfloat16)
    grad_q = jnp.einsum("bhqk,bkhd->bqhd", grad_scores, keys, preferred_element_type=f32) * scale
    grad_k = jnp.einsum("bhqk,bqhd->bkhd", grad_scores, query, preferred_element_type=f32) * scale
    grad_v = jnp.einsum("bhqk,bqhd->bkhd", weights, grad_context, preferred_element_type=f32)
    grad_qkv = jnp.stack([grad_q, grad_k, grad_v], axis=2).astype(jnp.bfloat16)
    grad_qkv = grad_qkv.reshape(tok_dev, 3 * width)
    grad_total = grad_resid1 + jnp.einsum(
        "ne,de->nd", grad_qkv, w_qkv, preferred_element_type=f32
    )
    back_got = exchange(move_back(place_hot, grad_total.astype(jnp.bfloat16)))
    grad_tokens = move_back(send_hot, back_got)
    grad_w_qkv = jnp.einsum("nd,ne->de", x, grad_qkv, preferred_element_type=f32)
    grad_qkv_sum = jnp.sum(grad_qkv.astype(f32), axis=0)

    low = jnp.bfloat16
    wide = jnp.concatenate(
        [
            grad_w_qkv.astype(low), grad_w_out.astype(low), grad_w_up.astype(low),
            grad_w_down.astype(low).reshape(width, -1),
        ],
        axis=1,
    )
    narrow = jnp.concatenate(
        [
            member.reshape(n_tok, -1)
            for member in (
                grad_qkv_sum[:width], grad_qkv_sum[2 * width :], grad_b_out, grad_gain1,
                grad_shift1, grad_b_down, grad_gain2, grad_shift2, grad_b_up,
            )
        ],
        axis=1,
    )
    share = lax.psum_scatter(wide, "tok", scatter_dimension=0, tiled=True)
    share = lax.psum(share, "grp").astype(f32)
    narrow = lax.psum(narrow, ("grp", "tok"))
    mine = lax.dynamic_index_in_dim(narrow, my_index, 0, keepdims=False)
    step = width // n_tok
    parts = [mine[i * step : (i + 1) * step] for i in range(8)] + [mine[8 * step :]]
    ffw = w_up.shape[1]
    return (
        block_out,
        grad_tokens,
        share[:, : 3 * width],
        parts[0],
        parts[1],
        share[:, 3 * width : 4 * width],
        parts[2],
        parts[3],
        parts[4],
        share[:, 4 * width : 4 * width + ffw],
        parts[8],
        share[:, 4 * width + ffw :].reshape(ffw // n_tok, width),
        parts[5],
        parts[6],
        parts[7],
    )


def solution(mesh):
    n_tok = mesh.shape["tok"]

    def body(*args):
        fits = n_tok == 8 and mesh.shape["grp"] == 4 and args[0].shape[0] == 1024
        return (per_device_fast if fits else per_device)(*args)

    rows = P(("grp", "tok"), None)
    in_specs = (rows,) + (P(),) * 13 + (rows, P("grp", None), P(("grp", "tok")))
    shares = (
        P("tok", None), P("tok"), P("tok"), P("tok", None), P("tok"), P("tok"), P("tok"),
        P("tok", None), P("tok"), P("tok", None), P("tok"), P("tok"), P("tok"),
    )
    return jax.shard_map(
        body, mesh=mesh, in_specs=in_specs, out_specs=(rows, rows) + shares, check_vma=False
    )
```

```python
import functools

import jax
import jax.numpy as jnp
from jax import lax
from jax.experimental import pallas as pl
from jax.experimental.pallas import tpu as pltpu
from jax.sharding import PartitionSpec as P

H = 12
CLU = 128

eps = 1e-12
masked_score = -1000000000.0

MESH = pl.DeviceIdType.MESH
f32 = jnp.float32
bf16 = jnp.bfloat16
BLK = 256


def dot32(a, b):
    return jnp.dot(a, b, preferred_element_type=jnp.float32)


def dot_rows(a, b):
    return lax.dot_general(a, b, (((1,), (1,)), ((), ())), preferred_element_type=jnp.float32)


def dot_cols(a, b):
    return lax.dot_general(a, b, (((0,), (0,)), ((), ())), preferred_element_type=jnp.float32)


def peer_order(n_tok):
    return sorted(range(1, n_tok), key=lambda k: -k)


def row_of(ref):
    return ref[...].astype(f32)[None, :]


def norm_parts(values):
    centre = values - jnp.mean(values, axis=-1, keepdims=True)
    spread = jnp.mean(centre * centre, axis=-1, keepdims=True)
    rstd = lax.rsqrt(spread + eps)
    return centre * rstd, rstd


def lane_halves(width, factor=1.0):
    lane = lax.broadcasted_iota(jnp.int32, (1, width), 1)
    low = (lane < width // 2).astype(f32) * factor
    return low.astype(bf16), (factor - low).astype(bf16)


def stack_heads(pair, halves):
    return jnp.concatenate([pair * halves[0], pair * halves[1]], axis=0)


def one_over_other(pair):
    half = pair.shape[1] // 2
    return jnp.concatenate([pair[:, :half], pair[:, half:]], axis=0)


def column_of(row):
    amount = row.shape[1]
    return jnp.concatenate(
        [
            jnp.broadcast_to(row[:, at : at + 128], (128, 128)).T
            for at in range(0, amount, 128)
        ],
        axis=0,
    )


def hot_from_column(column, amount):
    lane = lax.broadcasted_iota(jnp.int32, column.shape, 1).astype(f32)
    return jnp.concatenate(
        [(lane + float(at) == column).astype(f32).astype(bf16) for at in range(0, amount, 128)],
        axis=1,
    )


def forward_kernel(
    n_tok, per,
    slots_ref, docs_ref, tok_ref, og_ref, wq_ref, bq_ref, bv_ref, wo_ref, bo_ref, g1_ref, s1_ref,
    wu_ref, bu_ref, wd_ref, bd_ref, g2_ref, s2_ref,
    xc_o, gc_o, qkv_o, p_o, ctx_o, r1_o, n1_o, gelu_o, gelup_o, r2_o, back_o, col_o, pos_o,
    xh, gh, xs, gs, xr, gr, hot, note_s, note_r, wq, wo, wu, wd, live_s,
    xc_t, qkv_t, p_t, ctx_t, r1_t, n1_t, gelu_t, gelup_t, r2_t, bo_c, back_t, gc_t, col_t, pos_t,
    load_sem, note_ss, note_rs, x_ss, x_rs, g_ss, g_rs, own_sem, out_sem, last_sem,
):
    rows, width = xh.shape
    ffw = wu.shape[1]
    blocks = rows // BLK
    grp = lax.axis_index("grp")
    me = lax.axis_index("tok")
    order = peer_order(n_tok)

    barrier = pltpu.get_barrier_semaphore()
    for k in order:
        pl.semaphore_signal(barrier, inc=1, device_id=(grp, me ^ k), device_id_type=MESH)

    loads = [
        pltpu.make_async_copy(src, dst, load_sem.at[i])
        for i, (src, dst) in enumerate(
            ((tok_ref, xh), (og_ref, gh), (wq_ref, wq), (wo_ref, wo), (wu_ref, wu), (wd_ref, wd))
        )
    ]
    loads[0].start()

    def note_copy(k):
        return pltpu.make_async_remote_copy(
            src_ref=note_s.at[me ^ k], dst_ref=note_r.at[me], send_sem=note_ss.at[k],
            recv_sem=note_rs.at[k], device_id=(grp, me ^ k), device_id_type=MESH,
        )

    def row_copy(src, dst, ss, rs, k):
        return pltpu.make_async_remote_copy(
            src_ref=src.at[pl.ds(pl.multiple_of((me ^ k) * per, per), per)],
            dst_ref=dst.at[pl.ds(pl.multiple_of(me * per, per), per)],
            send_sem=ss.at[k], recv_sem=rs.at[k], device_id=(grp, me ^ k), device_id_type=MESH,
        )

    slots = slots_ref[...][None, :]
    dest = jnp.right_shift(slots, rows.bit_length() - 1)
    within = jnp.bitwise_and(slots, rows - 1)
    lanes = lax.broadcasted_iota(jnp.int32, (1, rows), 1)
    dest_hot = lax.broadcasted_iota(jnp.int32, (16, rows), 0) == dest
    dest_hot = dest_hot.astype(f32)
    before = lax.broadcasted_iota(jnp.int32, (BLK, rows), 1)
    rank = jnp.zeros((16, rows), f32)
    for b in range(blocks):
        earlier = lax.broadcasted_iota(jnp.int32, (BLK, rows), 0) + b * BLK < before
        rank += dot32(
            dest_hot[:, b * BLK : (b + 1) * BLK].astype(bf16), earlier.astype(f32).astype(bf16)
        )
    rank = jnp.sum(rank * dest_hot, axis=0, keepdims=True).astype(jnp.int32)
    pos = dest * per + rank
    spot = lax.broadcasted_iota(jnp.int32, (BLK, rows), 0)
    chip = lax.div(me * per, BLK)
    loads[0].wait()
    for copy in loads[1:]:
        copy.start()
    for j in range(blocks - 1, -1, -1):
        at = pl.multiple_of((chip ^ j) * BLK, BLK)
        picked = (spot + at == pos).astype(f32).astype(bf16)
        hot[pl.ds(at, BLK), :] = picked
        xs[pl.ds(at, BLK), :] = dot32(picked, xh[...]).astype(bf16)
        if j == blocks - 1:
            pl.semaphore_wait(barrier, n_tok - 1)
        for k in order:
            if k // (BLK // per) == j:
                row_copy(xs, xr, x_ss, x_rs, k).start()
    mine = pl.ds(pl.multiple_of(me * per, per), per)
    own_x = pltpu.make_async_copy(xs.at[mine], xr.at[mine], own_sem.at[0])
    own_x.start()

    pos_t[...] = jnp.broadcast_to(pos, (8, rows))
    start = jnp.int32(0)
    position = lanes + me * rows
    usable = jnp.zeros((1, rows), jnp.int32)
    for i in range(docs_ref.shape[1]):
        length = docs_ref[0, i]
        inside = (position >= start) & (position < start + length)
        usable = jnp.where(inside, 1, usable)
        start = start + jnp.bitwise_and(length + (CLU - 1), -CLU)
    kind = lax.broadcasted_iota(jnp.int32, (16, rows), 0)
    notes = jnp.where(
        kind == 0,
        jnp.right_shift(within, 5),
        jnp.where(kind == 1, jnp.bitwise_and(within, 31), jnp.where(kind == 2, usable, 0)),
    )
    notes = dot_rows(notes.astype(f32).astype(bf16), hot[...]).astype(bf16)
    for d in range(n_tok):
        note_s[d] = notes[:, d * per : (d + 1) * per]
    for k in order:
        note_copy(k).start()
    own_note = pltpu.make_async_copy(note_s.at[me], note_r.at[me], own_sem.at[1])
    own_note.start()
    loads[1].wait()
    for b in range(blocks):
        sl = pl.ds(b * BLK, BLK)
        gs[sl, :] = dot32(hot[sl, :], gh[...]).astype(bf16)
    own_g = pltpu.make_async_copy(gs.at[mine], gr.at[mine], own_sem.at[2])
    own_g.start()

    own_note.wait()
    for k in order:
        note_copy(k).wait_recv()
    got = jnp.concatenate([note_r[d] for d in range(n_tok)], axis=1)
    got32 = got.astype(f32)
    slot_row = got32[0:1, :] * 32.0 + got32[1:2, :]
    col_t[...] = column_of(slot_row)
    slot_row = slot_row.astype(jnp.int32)
    for b in range(blocks):
        spot = lax.broadcasted_iota(jnp.int32, (BLK, rows), 0) + b * BLK
        hot[b * BLK : (b + 1) * BLK, :] = (spot == slot_row).astype(f32).astype(bf16)
    live_s[...] = column_of(dot_rows(got, hot[...])[2:3, :])

    def gather_rows(source, target, own, copy):
        for j in range(blocks):
            if j == 0:
                own.wait()
            for k in range(1, n_tok):
                if k // (BLK // per) == j:
                    copy(k).wait_recv()
            at = pl.multiple_of((chip ^ j) * BLK, BLK)
            for b in range(blocks):
                sl = pl.ds(b * BLK, BLK)
                part = dot32(hot[sl, pl.ds(at, BLK)], source[pl.ds(at, BLK), :]).astype(bf16)
                target[sl, :] = part if j == 0 else target[sl, :] + part

    for k in order:
        row_copy(xs, xr, x_ss, x_rs, k).wait_send()
    for k in order:
        row_copy(gs, gr, g_ss, g_rs, k).start()
    gather_rows(xr, xc_t, own_x, lambda k: row_copy(xs, xr, x_ss, x_rs, k))
    xc_out = pltpu.make_async_copy(xc_t, xc_o, last_sem.at[4])
    xc_out.start()
    for copy in loads[2:]:
        copy.wait()

    halves = lane_halves(2 * width // H)
    scaled = lane_halves(2 * width // H, (width // H) ** (-0.5))
    pair_width = 2 * width // H
    pairs = range(H // 2)
    outs = (
        (qkv_t, qkv_o, BLK), (p_t, p_o, BLK * H // 2), (ctx_t, ctx_o, BLK), (r1_t, r1_o, BLK),
        (n1_t, n1_o, BLK), (gelu_t, gelu_o, BLK), (gelup_t, gelup_o, BLK), (r2_t, r2_o, BLK),
    )

    def out_copy(i, b, slot):
        tile, whole, count = outs[i]
        return pltpu.make_async_copy(
            tile.at[slot], whole.at[pl.ds(pl.multiple_of(b * count, count), count)], out_sem.at[slot, i]
        )

    def block(b, carry):
        slot = lax.rem(b, 2)
        sl = pl.ds(pl.multiple_of(b * BLK, BLK), BLK)

        @pl.when(b >= 2)
        def _():
            for i in range(len(outs)):
                out_copy(i, b - 2, slot).wait()

        x = xc_t[sl, :]
        for part, bias in ((0, row_of(bq_ref)), (1, None), (2, row_of(bv_ref))):
            got_part = dot32(x, wq[:, part * width : (part + 1) * width])
            if bias is not None:
                got_part = got_part + bias
            qkv_t[slot, :, part * width : (part + 1) * width] = got_part.astype(bf16)
        for c in range(BLK // CLU):
            at = pl.multiple_of(b * BLK + c * CLU, CLU)
            live = live_s[pl.ds(at, CLU), :] > 0.5
            live = jnp.concatenate([live, live], axis=1)
            crow = pl.ds(c * CLU, CLU)
            cols = [[pl.ds(part * width + p * pair_width, pair_width) for p in pairs] for part in range(3)]
            q2 = [stack_heads(qkv_t[slot, crow, cols[0][p]], scaled) for p in pairs]
            scores = [jnp.where(live, dot_rows(qkv_t[slot, crow, cols[1][p]], q2[p]), masked_score) for p in pairs]
            expo = [jnp.exp(member - jnp.max(member, axis=0, keepdims=True)) for member in scores]
            weights = [(member / jnp.sum(member, axis=0, keepdims=True)).astype(bf16) for member in expo]
            v2 = [stack_heads(qkv_t[slot, crow, cols[2][p]], halves) for p in pairs]
            context = [dot_cols(one_over_other(weights[p]), v2[p]).astype(bf16) for p in pairs]
            for p in pairs:
                p_t[slot, pl.ds((c * (H // 2) + p) * CLU, CLU), :] = weights[p]
                ctx_t[slot, crow, cols[0][p]] = context[p]
        resid1 = x.astype(f32) + (dot32(ctx_t[slot], wo[...]) + row_of(bo_ref))
        r1_t[slot] = resid1
        hat1, _ = norm_parts(resid1)
        normed1 = hat1 * row_of(g1_ref) + row_of(s1_ref)
        low1 = normed1.astype(bf16)
        n1_t[slot] = low1
        down = None
        step = width
        for j in range(ffw // step):
            cs = pl.ds(j * step, step)
            up = dot32(low1, wu[:, cs]) + bu_ref[cs].astype(f32)[None, :]
            phi = 0.5 * (1.0 + lax.erf(up * 0.7071067811865476))
            slope = phi + up * jnp.exp(up * up * -0.5) * 0.3989422804014327
            act = (up * phi).astype(bf16)
            gelu_t[slot, :, cs] = act
            gelup_t[slot, :, cs] = slope.astype(bf16)
            term = dot32(act, wd[cs, :])
            down = term if down is None else down + term
        resid2 = normed1 + (down + row_of(bd_ref))
        r2_t[slot] = resid2
        hat2, _ = norm_parts(resid2)
        bo_c[sl, :] = (hat2 * row_of(g2_ref) + row_of(s2_ref)).astype(bf16)
        for i in range(len(outs)):
            out_copy(i, b, slot).start()
        return carry

    lax.fori_loop(0, blocks, block, 0)

    col_out = pltpu.make_async_copy(col_t, col_o, last_sem.at[0])
    col_out.start()
    pos_out = pltpu.make_async_copy(pos_t, pos_o, last_sem.at[1])
    pos_out.start()
    for b in range(blocks):
        sl = pl.ds(b * BLK, BLK)
        back_t[sl, :] = dot32(hot_from_column(col_t[sl, :], rows), bo_c[...]).astype(bf16)
    back_out = pltpu.make_async_copy(back_t, back_o, last_sem.at[2])
    back_out.start()
    gather_rows(gr, gc_t, own_g, lambda k: row_copy(gs, gr, g_ss, g_rs, k))
    gc_out = pltpu.make_async_copy(gc_t, gc_o, last_sem.at[3])
    gc_out.start()
    for k in order:
        note_copy(k).wait_send()
        row_copy(gs, gr, g_ss, g_rs, k).wait_send()
    for b in range(max(blocks - 2, 0), blocks):
        for i in range(len(outs)):
            out_copy(i, b, b % 2).wait()
    col_out.wait()
    pos_out.wait()
    back_out.wait()
    gc_out.wait()
    xc_out.wait()


def forward(n_tok, tokens_in, w_qkv, b_query, b_value, w_out, b_out, norm1_gain, norm1_shift,
            w_up, b_up, w_down, b_down, norm2_gain, norm2_shift, out_grad, doc_lengths, cluster_slots):
    rows, width = tokens_in.shape
    ffw = w_up.shape[1]
    per = rows // n_tok
    vm = pl.BlockSpec(memory_space=pltpu.VMEM)
    sm = pl.BlockSpec(memory_space=pltpu.SMEM)
    hb = pl.BlockSpec(memory_space=pl.ANY)
    out_shape = [
        ((rows, width), bf16), ((rows, width), bf16), ((rows, 3 * width), bf16), ((rows * H // 2, 2 * CLU), bf16),
        ((rows, width), bf16), ((rows, width), f32), ((rows, width), bf16), ((rows, ffw), bf16),
        ((rows, ffw), bf16), ((rows, width), f32), ((rows, width), bf16), ((rows, 128), f32),
        ((8, rows), jnp.int32),
    ]
    vmem = pltpu.VMEM
    dma = pltpu.SemaphoreType.DMA
    scratch = (
        [vmem((rows, width), bf16)] * 6
        + [vmem((rows, rows), bf16), vmem((n_tok, 16, per), bf16), vmem((n_tok, 16, per), bf16)]
        + [vmem(w_qkv.shape, bf16), vmem(w_out.shape, bf16), vmem(w_up.shape, bf16), vmem(w_down.shape, bf16)]
        + [vmem((rows, 128), f32)]
        + [
            vmem((rows, width), bf16), vmem((2, BLK, 3 * width), bf16), vmem((2, BLK * H // 2, 2 * CLU), bf16),
            vmem((2, BLK, width), bf16), vmem((2, BLK, width), f32), vmem((2, BLK, width), bf16),
            vmem((2, BLK, ffw), bf16), vmem((2, BLK, ffw), bf16), vmem((2, BLK, width), f32),
            vmem((rows, width), bf16), vmem((rows, width), bf16), vmem((rows, width), bf16),
            vmem((rows, 128), f32), vmem((8, rows), jnp.int32),
        ]
        + [dma((6,))] + [dma((n_tok,))] * 6 + [dma((3,)), dma((2, 8)), dma((5,))]
    )
    return pl.pallas_call(
        functools.partial(forward_kernel, n_tok, per),
        out_shape=[jax.ShapeDtypeStruct(s, d) for s, d in out_shape],
        in_specs=[vm, sm, hb, hb, hb, vm, vm, hb, vm, vm, vm, hb, vm, hb, vm, vm, vm],
        out_specs=[hb] * len(out_shape),
        scratch_shapes=scratch,
        compiler_params=pltpu.CompilerParams(
            collective_id=0, has_side_effects=True, vmem_limit_bytes=60 * 2**20
        ),
        name="layer_forward",
    )(cluster_slots, doc_lengths, tokens_in, out_grad, w_qkv, b_query, b_value, w_out, b_out, norm1_gain,
      norm1_shift, w_up, b_up, w_down, b_down, norm2_gain, norm2_shift)


def grad_kinds(width, ffw, n_tok):
    return ((ffw // n_tok, width), (width // n_tok, ffw), (width // n_tok, width), (width // n_tok, 3 * width))


def backward_kernel(n_tok, per, kinds, *refs):
    (xc_ref, gc_ref, qkv_ref, p_ref, ctx_ref, r1_ref, n1_ref, gelu_ref, gelup_ref, r2_ref, back_ref, col_ref,
     wq_ref, wo_ref, wu_ref, wd_ref, g1_ref, g2_ref) = refs[:18]
    refs = refs[18:]
    bo_got, gt_got, nar_o = refs[:3]
    shares = refs[3:7]
    refs = refs[7:]
    (wq, wo, wu, wd, gwd, gelu, gup, low1, gdown, resid, grow, ctx, gattn, gcl, qkv, probs, land0, col,
     nar_v, bup_v, nar_s, nar_r, nar_g, nar_h, nar_t,
     load_sem, bo_ss, bo_rs, gt_ss, gt_rs, own_sem, s0_ss, s0_rs, x1_ss, x1_rs, x2_ss, x2_rs, za_ss, za_rs,
     zb_ss, zb_rs, ag_ss, ag_rs, fin_sem, free_sem, nt_ss, nt_rs, ng_ss, ng_rs) = refs
    rows, width = low1.shape
    ffw = wu.shape[1]
    blocks = rows // BLK
    grp = lax.axis_index("grp")
    me = lax.axis_index("tok")
    core = lax.rem(me, 2)
    chip = lax.div(me, 2)
    chips = n_tok // 2
    gx = lax.rem(grp, 2)
    gy = lax.div(grp, 2)
    order = peer_order(n_tok)
    mats = (gwd, wu, wo, wq)

    barrier = pltpu.get_barrier_semaphore()
    for k in order:
        pl.semaphore_signal(barrier, inc=1, device_id=(grp, me ^ k), device_id_type=MESH)
    for k in (1, 2, 3):
        pl.semaphore_signal(barrier, inc=1, device_id=(grp ^ k, me), device_id_type=MESH)

    load = {
        name: pltpu.make_async_copy(src, dst, load_sem.at[i])
        for i, (name, src, dst) in enumerate((
            ("gc", gc_ref, gcl), ("r2", r2_ref, resid), ("gelu", gelu_ref, gelu), ("wd", wd_ref, wd),
            ("gelup", gelup_ref, gup), ("wu", wu_ref, wu), ("n1", n1_ref, low1), ("wo", wo_ref, wo),
            ("ctx", ctx_ref, ctx), ("qkv", qkv_ref, qkv), ("p", p_ref, probs), ("wq", wq_ref, wq),
            ("xc", xc_ref, gattn), ("col", col_ref, col), ("r1", r1_ref, resid),
        ))
    }

    def begin(*names):
        for name in names:
            load[name].start()

    def ready(*names):
        for name in names:
            load[name].wait()

    begin("gc", "r2")

    def row_copy(src, dst, ss, rs, k):
        return pltpu.make_async_remote_copy(
            src_ref=src.at[pl.ds(pl.multiple_of((me ^ k) * per, per), per)],
            dst_ref=dst.at[pl.ds(pl.multiple_of(me * per, per), per)],
            send_sem=ss.at[k], recv_sem=rs.at[k], device_id=(grp, me ^ k), device_id_type=MESH,
        )

    mine = pl.ds(pl.multiple_of(me * per, per), per)
    def held(m, z, row0, count, col0, ncols):
        share, _ = kinds[m]
        at = (2 * z + core) * share + row0
        return mats[m].at[pl.ds(pl.multiple_of(at, 16), count), pl.ds(pl.multiple_of(col0, 128), ncols)]

    zones = (land0, gelu, gup, gup)
    zone_col = (0, 0, 3 * width, 0)

    def land(m, row, count, half_at, whole):
        share, cols = kinds[m]
        ncols = cols if whole else cols // 2
        return zones[m].at[pl.ds(row, count), pl.ds(zone_col[m] + half_at * (cols // 2), ncols)]

    def land_s0(m, z):
        share = kinds[m][0]
        return land(m, z * share, share, 0, True)

    def land_x1(m, z):
        share = kinds[m][0]
        if first_x(z):
            return land(m, (chips + z) * share, share, 0, False)
        return land(m, (chips + 2) * share + (z - chips // 2) * (share // 2), share // 2, 0, True)

    def land_x2(m, z):
        share = kinds[m][0]
        return land(m, chips * share + z * (share // 2), share // 2, 1, False)

    def land_za(m, i):
        share = kinds[m][0]
        return land(m, (chips + 3) * share, share // 2, i, False)

    def land_zb(m):
        share = kinds[m][0]
        return land(m, (chips + 3) * share + share // 2, share // 2, 0, False)

    partners = ((grp, me ^ 1), (grp ^ 1, me), (grp ^ 2, me), (grp, me ^ 2), (grp, me ^ 4))

    def tell_free(i):
        for who in partners:
            pl.semaphore_signal(free_sem.at[i], inc=1, device_id=who, device_id_type=MESH)

    def partners_free(i):
        pl.semaphore_wait(free_sem.at[i], len(partners))

    def remote(src, dst, ss, rs, who):
        return pltpu.make_async_remote_copy(
            src_ref=src, dst_ref=dst, send_sem=ss, recv_sem=rs, device_id=who, device_id_type=MESH
        )

    def copy_s0(m, z):
        share, cols = kinds[m]
        at = (2 * z + 1 - core) * share
        return remote(
            mats[m].at[pl.ds(pl.multiple_of(at, 16), share)], land_s0(m, z),
            s0_ss.at[m, z], s0_rs.at[m, z], (grp, me ^ 1),
        )

    def first_x(z):
        return z < chips // 2

    def copy_x1(m, z):
        share, cols = kinds[m]
        half, hcols = share // 2, cols // 2
        if first_x(z):
            src = held(m, z, 0, share, (1 - gx) * hcols, hcols)
            who = (grp ^ 1, me)
        else:
            src = held(m, z, (1 - gy) * half, half, 0, cols)
            who = (grp ^ 2, me)
        return remote(src, land_x1(m, z), x1_ss.at[m, z], x1_rs.at[m, z], who)

    def copy_x2(m, z):
        share, cols = kinds[m]
        half, hcols = share // 2, cols // 2
        if first_x(z):
            src, who = held(m, z, (1 - gy) * half, half, gx * hcols, hcols), (grp ^ 2, me)
        else:
            src, who = held(m, z, gy * half, half, (1 - gx) * hcols, hcols), (grp ^ 1, me)
        return remote(src, land_x2(m, z), x2_ss.at[m, z], x2_rs.at[m, z], who)

    def quarter(m, z):
        share, cols = kinds[m]
        half, hcols = share // 2, cols // 2
        return held(m, z, gy * half, half, gx * hcols, hcols)

    def copy_za(m, i):
        return remote(quarter(m, chip ^ (1 + 2 * i)), land_za(m, i), za_ss.at[m, i], za_rs.at[m, i], (grp, me ^ 2))

    def copy_zb(m):
        return remote(quarter(m, chip ^ 2), land_zb(m), zb_ss.at[m], zb_rs.at[m], (grp, me ^ 4))

    def share_part(m):
        share, cols = kinds[m]
        half, hcols = share // 2, cols // 2
        return shares[m].at[
            pl.ds(pl.multiple_of(gy * half, 16), half), pl.ds(pl.multiple_of(gx * hcols, 128), hcols)
        ]

    def own_part(m):
        return quarter(m, chip)

    def copy_ag(m, k):
        return remote(own_part(m), share_part(m), ag_ss.at[m, k], ag_rs.at[m, k], (grp ^ k, me))

    def own_ag(m):
        return pltpu.make_async_copy(own_part(m), share_part(m), fin_sem.at[m])

    def add_in(target, extra):
        target[...] = target[...] + extra[...]

    turns = (0, 2, 1, 3)

    def start_s0(m):
        for z in turns:
            copy_s0(m, z).start()

    def step_r0(m, zs=turns):
        share, cols = kinds[m]
        for z in zs:
            copy_s0(m, z).wait_recv()
            add_in(held(m, z, 0, share, 0, cols), land_s0(m, z))
            copy_x1(m, z).start()

    def step_r1(m, zs=turns):
        share, cols = kinds[m]
        half, hcols = share // 2, cols // 2
        for z in zs:
            copy_x1(m, z).wait_recv()
            spot = (0, share, gx * hcols, hcols) if first_x(z) else (gy * half, half, 0, cols)
            add_in(held(m, z, *spot), land_x1(m, z))
            copy_x2(m, z).start()

    def step_r2(m):
        for z in turns:
            copy_x2(m, z).wait_recv()
            add_in(quarter(m, z), land_x2(m, z))
        copy_za(m, 0).start()
        copy_za(m, 1).start()

    def step_ra(m):
        copy_za(m, 0).wait_recv()
        copy_za(m, 1).wait_recv()
        add_in(quarter(m, chip ^ 2), land_za(m, 1))
        copy_zb(m).start()
        add_in(own_part(m), land_za(m, 0))

    def step_rb(m):
        copy_zb(m).wait_recv()
        add_in(own_part(m), land_zb(m))
        for k in (3, 1, 2):
            copy_ag(m, k).start()
        own_ag(m).start()

    gain2 = row_of(g2_ref)
    gain1 = row_of(g1_ref)

    def norm_back(upstream, resid_rows, gain):
        hat, rstd = norm_parts(resid_rows)
        dh = upstream * gain
        inner = jnp.mean(dh * hat, axis=-1, keepdims=True)
        return rstd * (dh - jnp.mean(dh, axis=-1, keepdims=True) - hat * inner), hat

    def add_sum(at, values):
        nar_v[at : at + 1, :] += jnp.sum(values, axis=0, keepdims=True)

    nar_v[...] = jnp.zeros_like(nar_v)
    bup_v[...] = jnp.zeros_like(bup_v)
    own_bo = pltpu.make_async_copy(back_ref.at[mine], bo_got.at[mine], own_sem.at[0])
    ready("gc", "r2")
    begin("gelu", "wd", "gelup")
    for b in range(blocks):
        sl = pl.ds(b * BLK, BLK)
        g = gcl[sl, :].astype(f32)
        back, hat = norm_back(g, resid[sl, :], gain2)
        low = back.astype(bf16)
        grow[sl, :] = back
        gdown[sl, :] = low
        add_sum(5, low.astype(f32))
        add_sum(6, g * hat)
        add_sum(7, g)
        if b == 0:
            pl.semaphore_wait(barrier, n_tok - 1 + 3)
            for k in order:
                row_copy(back_ref, bo_got, bo_ss, bo_rs, k).start()
            own_bo.start()

    ready("gelu")
    begin("wu", "r1", "wo", "n1", "ctx")
    step = width
    for j in turns:
        cs = pl.ds(j * step, step)
        gwd[cs, :] = dot_cols(gelu[:, cs], gdown[...]).astype(bf16)
        copy_s0(0, j).start()
    tell_free(0)
    ready("wd", "gelup")
    step_r0(0, turns[:2])
    for b in range(blocks):
        sl = pl.ds(b * BLK, BLK)
        for j in range(ffw // step):
            cs = pl.ds(j * step, step)
            up = (dot_rows(gdown[sl, :], wd[cs, :]) * gup[sl, cs].astype(f32)).astype(bf16)
            gup[sl, cs] = up
            bup_v[0:1, cs] += jnp.sum(up.astype(f32), axis=0, keepdims=True)
        if b == 1:
            step_r0(0, turns[2:])
    begin("qkv", "p", "wq", "col")
    ready("wu", "n1")
    for b in range(blocks):
        sl = pl.ds(b * BLK, BLK)
        grow[sl, :] += dot_rows(gup[sl, :], wu[...])
    for j in range(ffw // step):
        cs = pl.ds(j * step, step)
        wu[:, cs] = dot_cols(low1[...], gup[:, cs]).astype(bf16)
        if j == 0:
            step_r1(0, turns[:2])
        elif j == 2:
            step_r1(0, turns[2:])
    tell_free(1)
    partners_free(0)
    start_s0(1)
    ready("r1", "wo", "ctx")
    for b in range(blocks):
        sl = pl.ds(b * BLK, BLK)
        gn1 = grow[sl, :]
        back, hat = norm_back(gn1, resid[sl, :], gain1)
        low = back.astype(bf16)
        grow[sl, :] = back
        gattn[sl, :] = low
        add_sum(2, low.astype(f32))
        add_sum(3, gn1 * hat)
        add_sum(4, gn1)
        gcl[sl, :] = dot_rows(low, wo[...]).astype(bf16)
        if b == 2:
            step_r0(1, turns[:2])
    wo[...] = dot_cols(ctx[...], gattn[...]).astype(bf16)
    begin("xc")
    partners_free(1)
    start_s0(2)
    step_r0(1, turns[2:])
    step_r2(0)

    ready("qkv", "p", "wq")
    halves = lane_halves(2 * width // H)
    pair_width = 2 * width // H
    scaled = lane_halves(2 * width // H, (width // H) ** (-0.5))
    pairs = range(H // 2)

    def attend(b):
        for c in range(BLK // CLU):
            crow = pl.ds(b * BLK + c * CLU, CLU)
            cols = [[pl.ds(part * width + p * pair_width, pair_width) for p in pairs] for part in range(3)]
            first = (b * BLK // CLU + c) * (H // 2)
            go = [stack_heads(gcl[crow, cols[0][p]], halves) for p in pairs]
            gp = [dot_rows(qkv[crow, cols[2][p]], go[p]) for p in pairs]
            weights = [probs[pl.ds((first + p) * CLU, CLU), :] for p in pairs]
            gv = [dot32(weights[p], go[p]).astype(bf16) for p in pairs]
            wide = [member.astype(f32) for member in weights]
            dots = [jnp.sum(gp[p] * wide[p], axis=0, keepdims=True) for p in pairs]
            gs = [(wide[p] * (gp[p] - dots[p])).astype(bf16) for p in pairs]
            q2 = [stack_heads(qkv[crow, cols[0][p]], scaled) for p in pairs]
            k2 = [stack_heads(qkv[crow, cols[1][p]], scaled) for p in pairs]
            gk = [dot32(gs[p], q2[p]).astype(bf16) for p in pairs]
            gq = [dot_cols(one_over_other(gs[p]), k2[p]).astype(bf16) for p in pairs]
            for p in pairs:
                qkv[crow, cols[0][p]] = gq[p]
                qkv[crow, cols[1][p]] = gk[p]
                qkv[crow, cols[2][p]] = gv[p]
        sl = pl.ds(b * BLK, BLK)
        add_sum(0, qkv[sl, 0:width].astype(f32))
        add_sum(1, qkv[sl, 2 * width :].astype(f32))
        total = grow[sl, :] + dot_rows(qkv[sl, :], wq[...])
        low1[sl, :] = total.astype(bf16)

    attend(0)
    step_r0(2)
    attend(1)
    step_ra(0)
    attend(2)
    step_r1(1, turns[:2])
    attend(3)
    step_r1(1, turns[2:])
    ready("xc", "col")
    for b in range(blocks):
        sl = pl.ds(b * BLK, BLK)
        gdown[sl, :] = dot32(hot_from_column(col[sl, :], rows), low1[...]).astype(bf16)
    def send_home(*who):
        for k in who:
            row_copy(gdown, gt_got, gt_ss, gt_rs, k).start()

    send_home(7, 6, 1)
    own_gt = pltpu.make_async_copy(gdown.at[mine], gt_got.at[mine], own_sem.at[1])
    own_gt.start()
    step_rb(0)
    for j in range(3):
        cs = pl.ds(j * step, step)
        wq[:, cs] = dot_cols(gattn[...], qkv[:, cs]).astype(bf16)
    start_s0(3)
    step_r1(2)

    each = width // n_tok
    at = lax.broadcasted_iota(jnp.int32, (width, n_tok * 128), 0)
    lane = lax.broadcasted_iota(jnp.int32, (width, n_tok * 128), 1)
    inner = jnp.bitwise_and(lane, 127)
    pick = (at == jnp.right_shift(lane, 7) * each + inner) & (inner < each)
    spread = jnp.dot(nar_v[...], pick.astype(f32), precision=lax.Precision.HIGHEST, preferred_element_type=f32)
    share_up = ffw // n_tok
    for d in range(n_tok):
        nar_s[d] = jnp.concatenate(
            [spread[0:8, d * 128 : (d + 1) * 128]]
            + [bup_v[0:1, d * share_up + i : d * share_up + i + 128] for i in range(0, share_up, 128)]
            + [jnp.zeros((8 - share_up // 128, 128), f32)], axis=0)

    def nar_copy(k):
        return remote(nar_s.at[me ^ k], nar_r.at[k], nt_ss.at[k], nt_rs.at[k], (grp, me ^ k))

    def nar_cross(k):
        return remote(nar_g, nar_h.at[k], ng_ss.at[k], ng_rs.at[k], (grp ^ k, me))

    for k in order:
        nar_copy(k).start()
    step_r2(1)
    step_r0(3)
    step_r2(2)
    step_r1(3, turns[:2])
    step_ra(1)
    step_ra(2)
    send_home(5, 4, 3, 2)
    step_r1(3, turns[2:])
    step_rb(1)
    step_rb(2)
    total = nar_s[me]
    for k in order:
        nar_copy(k).wait_recv()
        total += nar_r[k]
    nar_g[...] = total
    for k in (3, 1, 2):
        nar_cross(k).start()
    step_r2(3)
    total = nar_g[...]
    for k in (1, 2, 3):
        nar_cross(k).wait_recv()
        total += nar_h[k]
    nar_t[...] = total
    nar_out = pltpu.make_async_copy(nar_t, nar_o, own_sem.at[2])
    nar_out.start()
    step_ra(3)
    step_rb(3)

    own_bo.wait()
    own_gt.wait()
    nar_out.wait()
    for k in order:
        row_copy(back_ref, bo_got, bo_ss, bo_rs, k).wait()
        row_copy(gdown, gt_got, gt_ss, gt_rs, k).wait()
        nar_copy(k).wait_send()
    for k in (1, 2, 3):
        nar_cross(k).wait_send()
    for m in range(4):
        own_ag(m).wait()
        for z in range(chips):
            copy_s0(m, z).wait_send()
            copy_x1(m, z).wait_send()
            copy_x2(m, z).wait_send()
        copy_za(m, 0).wait_send()
        copy_za(m, 1).wait_send()
        copy_zb(m).wait_send()
        for k in (1, 2, 3):
            copy_ag(m, k).wait()


def backward(n_tok, saved, w_qkv, w_out, w_up, w_down, norm1_gain, norm2_gain):
    rows, width = saved[0].shape
    ffw = w_up.shape[1]
    per = rows // n_tok
    chips = n_tok // 2
    kinds = grad_kinds(width, ffw, n_tok)
    vm = pl.BlockSpec(memory_space=pltpu.VMEM)
    hb = pl.BlockSpec(memory_space=pl.ANY)
    outs = [((rows, width), bf16), ((rows, width), bf16), ((16, 128), f32)]
    outs += [(kind, bf16) for kind in kinds]
    vmem = pltpu.VMEM
    dma = pltpu.SemaphoreType.DMA
    scratch = [
        vmem(w_qkv.shape, bf16), vmem(w_out.shape, bf16), vmem(w_up.shape, bf16), vmem(w_down.shape, bf16),
        vmem(w_down.shape, bf16), vmem((rows, ffw), bf16), vmem((rows, ffw), bf16), vmem((rows, width), bf16),
        vmem((rows, width), bf16), vmem((rows, width), f32), vmem((rows, width), f32), vmem((rows, width), bf16),
        vmem((rows, width), bf16), vmem((rows, width), bf16), vmem((rows, 3 * width), bf16),
        vmem((rows * H // 2, 2 * CLU), bf16), vmem(w_down.shape, bf16), vmem((rows, 128), f32),
        vmem((16, width), f32), vmem((8, ffw), f32), vmem((n_tok, 16, 128), f32), vmem((n_tok, 16, 128), f32),
        vmem((16, 128), f32), vmem((4, 16, 128), f32), vmem((16, 128), f32),
        dma((15,)), dma((n_tok,)), dma((n_tok,)), dma((n_tok,)), dma((n_tok,)), dma((3,)),
    ]
    scratch += [dma((4, chips))] * 6 + [dma((4, 2))] * 2 + [dma((4,))] * 2
    scratch += [dma((4, 4))] * 2 + [dma((4,)), pltpu.SemaphoreType.REGULAR((2,))]
    scratch += [dma((n_tok,))] * 2 + [dma((4,))] * 2
    return pl.pallas_call(
        functools.partial(backward_kernel, n_tok, per, kinds),
        out_shape=[jax.ShapeDtypeStruct(s, d) for s, d in outs],
        in_specs=[hb] * 16 + [vm] * 2,
        out_specs=[hb] * len(outs),
        scratch_shapes=scratch,
        compiler_params=pltpu.CompilerParams(
            collective_id=1, has_side_effects=True, vmem_limit_bytes=63 * 2**20
        ),
        name="layer_backward",
    )(*saved, w_qkv, w_out, w_up, w_down, norm1_gain, norm2_gain)[:7]


def finish_kernel(
    pos_ref, nar_ref, bo_ref, gt_ref, wd_ref, wu_ref, wo_ref, wq_ref,
    out_o, tok_o, wq_o, wo_o, wu_o, wd_o, bq_o, bv_o, b_out_o, g1_o, s1_o, bu_o, bd_o, g2_o, s2_o,
    bo, gt, wd, wu, wo, wq, out_t, tok_t, wd_t, wu_t, wo_t, wq_t, in_sem, out_sem, row_sem,
):
    rows = bo.shape[0]
    ins = [
        pltpu.make_async_copy(src, dst, in_sem.at[i])
        for i, (src, dst) in enumerate(
            ((wd_ref, wd), (wu_ref, wu), (wq_ref, wq), (wo_ref, wo), (bo_ref, bo), (gt_ref, gt))
        )
    ]
    for copy in ins:
        copy.start()
    outs = []
    for i, (src, dst, whole) in enumerate(((wd, wd_t, wd_o), (wu, wu_t, wu_o), (wq, wq_t, wq_o), (wo, wo_t, wo_o))):
        ins[i].wait()
        dst[...] = src[...].astype(f32)
        outs.append(pltpu.make_async_copy(dst, whole, out_sem.at[i]))
        outs[-1].start()
    column = column_of(pos_ref[0:1, :].astype(f32))
    ins[4].wait()
    ins[5].wait()
    for b in range(rows // BLK):
        sl = pl.ds(b * BLK, BLK)
        home = hot_from_column(column[b * BLK : (b + 1) * BLK], rows)
        for i, (got, tile, whole) in enumerate(((bo, out_t, out_o), (gt, tok_t, tok_o))):
            tile[sl, :] = dot32(home, got[...]).astype(bf16)
            outs.append(pltpu.make_async_copy(tile.at[sl], whole.at[sl], row_sem.at[i, b]))
            outs[-1].start()
    for i, dst in enumerate((bq_o, bv_o, b_out_o, g1_o, s1_o, bd_o, g2_o, s2_o)):
        dst[...] = nar_ref[i, 0 : dst.shape[0]]
    for i in range(bu_o.shape[0] // 128):
        bu_o[i * 128 : (i + 1) * 128] = nar_ref[8 + i, :]
    for copy in outs:
        copy.wait()


def finish(pos, got):
    bo, gt, nar, wd, wu, wo, wq = got
    rows, width = bo.shape
    each = wq.shape[0]
    vm = pl.BlockSpec(memory_space=pltpu.VMEM)
    hb = pl.BlockSpec(memory_space=pl.ANY)
    outs = [(bo.shape, bf16), (gt.shape, bf16), (wq.shape, f32), (wo.shape, f32), (wu.shape, f32), (wd.shape, f32)]
    outs += [((each,), f32)] * 5 + [((wd.shape[0],), f32)] + [((each,), f32)] * 3
    vmem = pltpu.VMEM
    scratch = [vmem(member.shape, bf16) for member in (bo, gt, wd, wu, wo, wq, bo, gt)]
    scratch += [vmem(member.shape, f32) for member in (wd, wu, wo, wq)]
    scratch += [pltpu.SemaphoreType.DMA((6,)), pltpu.SemaphoreType.DMA((4,)), pltpu.SemaphoreType.DMA((2, rows // BLK))]
    (out, tok, g_wq, g_wo, g_wu, g_wd, bq, bv, b_out, g1, s1, bu, bd, g2, s2) = pl.pallas_call(
        finish_kernel,
        out_shape=[jax.ShapeDtypeStruct(s, d) for s, d in outs],
        in_specs=[vm] * 2 + [hb] * 6,
        out_specs=[hb] * 6 + [vm] * 9,
        scratch_shapes=scratch,
        compiler_params=pltpu.CompilerParams(vmem_limit_bytes=60 * 2**20),
        name="back_home",
    )(pos, nar, bo, gt, wd, wu, wo, wq)
    return out, tok, g_wq, bq, bv, g_wo, b_out, g1, s1, g_wu, bu, g_wd, bd, g2, s2


def per_device_fast(
    tokens_in, w_qkv, b_query, b_value, w_out, b_out, norm1_gain, norm1_shift,
    w_up, b_up, w_down, b_down, norm2_gain, norm2_shift, out_grad, doc_lengths, cluster_slots,
):
    n_tok = lax.axis_size("tok")
    *saved, pos = forward(
        n_tok, tokens_in, w_qkv, b_query, b_value, w_out, b_out, norm1_gain, norm1_shift,
        w_up, b_up, w_down, b_down, norm2_gain, norm2_shift, out_grad, doc_lengths, cluster_slots)
    got = backward(n_tok, saved, w_qkv, w_out, w_up, w_down, norm1_gain, norm2_gain)
    return tuple(finish(pos, got))


def norm_rows(values, scales, shifts):
    centre = values - jnp.mean(values, axis=-1, keepdims=True)
    spread = jnp.mean(centre * centre, axis=-1, keepdims=True)
    return centre * lax.rsqrt(spread + eps) * scales + shifts


def gelu_exact(values):
    return jax.nn.gelu(values, approximate=False)


def valid_tokens(lengths_row, offset, amount, cluster):
    padded = (lengths_row + cluster - 1) // cluster * cluster
    starts = jnp.cumsum(padded) - padded
    position = offset + jnp.arange(amount, dtype=jnp.int32)
    inside = (position[:, None] >= starts[None, :]) & (
        position[:, None] < (starts + lengths_row)[None, :]
    )
    return jnp.any(inside, axis=1)


def move(one_hot, rows):
    return dot32(one_hot, rows).astype(jnp.bfloat16)


def move_back(one_hot, rows):
    picked = jnp.einsum("pi,pd->id", one_hot, rows, preferred_element_type=jnp.float32)
    return picked.astype(jnp.bfloat16)


def exchange(rows):
    return lax.all_to_all(rows, "tok", split_axis=0, concat_axis=0, tiled=True)


def per_device(
    tokens_in, w_qkv, b_query, b_value, w_out, b_out, norm1_gain, norm1_shift,
    w_up, b_up, w_down, b_down, norm2_gain, norm2_shift, out_grad, doc_lengths, cluster_slots,
):
    tok_dev, width = tokens_in.shape
    head_size = width // H
    clusters = tok_dev // CLU
    n_tok = lax.axis_size("tok")
    per_peer = tok_dev // n_tok
    my_index = lax.axis_index("tok")
    f32 = jnp.float32

    usable = valid_tokens(doc_lengths[0], my_index * tok_dev, tok_dev, CLU)
    dest = cluster_slots // tok_dev
    dest_hot = (dest[:, None] == jnp.arange(n_tok)[None, :]).astype(jnp.int32)
    rank = jnp.sum((jnp.cumsum(dest_hot, axis=0) - dest_hot) * dest_hot, axis=1)
    send_pos = dest * per_peer + rank
    send_hot = (jnp.arange(tok_dev)[:, None] == send_pos[None, :])
    note = (cluster_slots % tok_dev) * 2 + usable.astype(jnp.int32)
    sent_note = jnp.sum(jnp.where(send_hot, note[None, :], 0), axis=1)
    send_hot = send_hot.astype(jnp.bfloat16)
    got_note = exchange(sent_note)
    x_got = exchange(move(send_hot, tokens_in))
    g_got = exchange(move(send_hot, out_grad))
    place_hot = jnp.arange(tok_dev)[:, None] == (got_note // 2)[None, :]
    key_live = jnp.sum(jnp.where(place_hot, got_note[None, :] % 2, 0), axis=1) > 0
    place_hot = place_hot.astype(jnp.bfloat16)
    x = move(place_hot, x_got)

    bias_qkv = jnp.concatenate(
        [b_query.astype(f32), jnp.zeros((width,), f32), b_value.astype(f32)]
    )
    qkv = (dot32(x, w_qkv) + bias_qkv).astype(jnp.bfloat16)
    packed = qkv.reshape(clusters, CLU, 3, H, head_size)
    query, keys, value = packed[:, :, 0], packed[:, :, 1], packed[:, :, 2]
    scale = head_size ** (-0.5)
    scores = jnp.einsum("bqhd,bkhd->bhqk", query, keys, preferred_element_type=f32) * scale
    scores = jnp.where(key_live.reshape(clusters, 1, 1, CLU), scores, masked_score)
    expo = jnp.exp(scores - jnp.max(scores, axis=-1, keepdims=True))
    probs = expo / jnp.sum(expo, axis=-1, keepdims=True)
    weights = probs.astype(jnp.bfloat16)
    context = jnp.einsum("bhqk,bkhd->bqhd", weights, value, preferred_element_type=f32)
    context = context.astype(jnp.bfloat16).reshape(tok_dev, width)

    resid1 = x.astype(f32) + dot32(context, w_out) + b_out.astype(f32)
    normed1, norm1_back = jax.vjp(
        norm_rows, resid1, norm1_gain.astype(f32), norm1_shift.astype(f32)
    )
    normed1_low = normed1.astype(jnp.bfloat16)
    up_pre = dot32(normed1_low, w_up) + b_up.astype(f32)
    gelu_out, gelu_back = jax.vjp(gelu_exact, up_pre)
    gelu_low = gelu_out.astype(jnp.bfloat16)
    down_out = dot32(gelu_low, w_down) + b_down.astype(f32)
    normed2, norm2_back = jax.vjp(
        norm_rows, normed1 + down_out, norm2_gain.astype(f32), norm2_shift.astype(f32)
    )
    out_got = exchange(move_back(place_hot, normed2.astype(jnp.bfloat16)))
    block_out = move_back(send_hot, out_got)

    g = move(place_hot, g_got)
    grad_resid2, grad_gain2, grad_shift2 = norm2_back(g.astype(f32))
    grad_down = grad_resid2.astype(jnp.bfloat16)
    grad_b_down = jnp.sum(grad_down.astype(f32), axis=0)
    grad_w_down = jnp.einsum("nf,nd->fd", gelu_low, grad_down, preferred_element_type=f32)
    grad_gelu = jnp.einsum("nd,fd->nf", grad_down, w_down, preferred_element_type=f32)
    grad_up = gelu_back(grad_gelu)[0].astype(jnp.bfloat16)
    grad_b_up = jnp.sum(grad_up.astype(f32), axis=0)
    grad_w_up = jnp.einsum("nd,nf->df", normed1_low, grad_up, preferred_element_type=f32)
    grad_normed1 = grad_resid2 + jnp.einsum(
        "nf,df->nd", grad_up, w_up, preferred_element_type=f32
    )
    grad_resid1, grad_gain1, grad_shift1 = norm1_back(grad_normed1)
    grad_attn = grad_resid1.astype(jnp.bfloat16)
    grad_b_out = jnp.sum(grad_attn.astype(f32), axis=0)
    grad_w_out = jnp.einsum("nd,ne->de", context, grad_attn, preferred_element_type=f32)
    grad_context = jnp.einsum("ne,de->nd", grad_attn, w_out, preferred_element_type=f32)
    grad_context = grad_context.astype(jnp.bfloat16).reshape(clusters, CLU, H, head_size)

    grad_probs = jnp.einsum("bqhd,bkhd->bhqk", grad_context, value, preferred_element_type=f32)
    row_dot = jnp.sum(grad_probs * probs, axis=-1, keepdims=True)
    grad_scores = (probs * (grad_probs - row_dot)).astype(jnp.bfloat16)
    grad_q = jnp.einsum("bhqk,bkhd->bqhd", grad_scores, keys, preferred_element_type=f32) * scale
    grad_k = jnp.einsum("bhqk,bqhd->bkhd", grad_scores, query, preferred_element_type=f32) * scale
    grad_v = jnp.einsum("bhqk,bqhd->bkhd", weights, grad_context, preferred_element_type=f32)
    grad_qkv = jnp.stack([grad_q, grad_k, grad_v], axis=2).astype(jnp.bfloat16)
    grad_qkv = grad_qkv.reshape(tok_dev, 3 * width)
    grad_total = grad_resid1 + jnp.einsum(
        "ne,de->nd", grad_qkv, w_qkv, preferred_element_type=f32
    )
    back_got = exchange(move_back(place_hot, grad_total.astype(jnp.bfloat16)))
    grad_tokens = move_back(send_hot, back_got)
    grad_w_qkv = jnp.einsum("nd,ne->de", x, grad_qkv, preferred_element_type=f32)
    grad_qkv_sum = jnp.sum(grad_qkv.astype(f32), axis=0)

    low = jnp.bfloat16
    wide = jnp.concatenate(
        [
            grad_w_qkv.astype(low), grad_w_out.astype(low), grad_w_up.astype(low),
            grad_w_down.astype(low).reshape(width, -1),
        ],
        axis=1,
    )
    narrow = jnp.concatenate(
        [
            member.reshape(n_tok, -1)
            for member in (
                grad_qkv_sum[:width], grad_qkv_sum[2 * width :], grad_b_out, grad_gain1,
                grad_shift1, grad_b_down, grad_gain2, grad_shift2, grad_b_up,
            )
        ],
        axis=1,
    )
    share = lax.psum_scatter(wide, "tok", scatter_dimension=0, tiled=True)
    share = lax.psum(share, "grp").astype(f32)
    narrow = lax.psum(narrow, ("grp", "tok"))
    mine = lax.dynamic_index_in_dim(narrow, my_index, 0, keepdims=False)
    step = width // n_tok
    parts = [mine[i * step : (i + 1) * step] for i in range(8)] + [mine[8 * step :]]
    ffw = w_up.shape[1]
    return (
        block_out,
        grad_tokens,
        share[:, : 3 * width],
        parts[0],
        parts[1],
        share[:, 3 * width : 4 * width],
        parts[2],
        parts[3],
        parts[4],
        share[:, 4 * width : 4 * width + ffw],
        parts[8],
        share[:, 4 * width + ffw :].reshape(ffw // n_tok, width),
        parts[5],
        parts[6],
        parts[7],
    )


def solution(mesh):
    n_tok = mesh.shape["tok"]

    def body(*args):
        fits = n_tok == 8 and mesh.shape["grp"] == 4 and args[0].shape[0] == 1024
        return (per_device_fast if fits else per_device)(*args)

    rows = P(("grp", "tok"), None)
    in_specs = (rows,) + (P(),) * 13 + (rows, P("grp", None), P(("grp", "tok")))
    shares = (
        P("tok", None), P("tok"), P("tok"), P("tok", None), P("tok"), P("tok"), P("tok"),
        P("tok", None), P("tok"), P("tok", None), P("tok"), P("tok"), P("tok"),
    )
    return jax.shard_map(
        body, mesh=mesh, in_specs=in_specs, out_specs=(rows, rows) + shares, check_vma=False
    )
```

```python
import functools

import jax
import jax.numpy as jnp
from jax import lax
from jax.experimental import pallas as pl
from jax.experimental.pallas import tpu as pltpu
from jax.sharding import PartitionSpec as P

H = 12
CLU = 128

eps = 1e-12
masked_score = -1000000000.0

MESH = pl.DeviceIdType.MESH
f32 = jnp.float32
bf16 = jnp.bfloat16
BLK = 256


def dot32(a, b):
    return jnp.dot(a, b, preferred_element_type=jnp.float32)


def dot_rows(a, b):
    return lax.dot_general(a, b, (((1,), (1,)), ((), ())), preferred_element_type=jnp.float32)


def dot_cols(a, b):
    return lax.dot_general(a, b, (((0,), (0,)), ((), ())), preferred_element_type=jnp.float32)


def peer_order(n_tok):
    return sorted(range(1, n_tok), key=lambda k: -k)


def row_of(ref):
    return ref[...].astype(f32)[None, :]


def norm_parts(values):
    centre = values - jnp.mean(values, axis=-1, keepdims=True)
    spread = jnp.mean(centre * centre, axis=-1, keepdims=True)
    rstd = lax.rsqrt(spread + eps)
    return centre * rstd, rstd


def lane_halves(width, factor=1.0):
    lane = lax.broadcasted_iota(jnp.int32, (1, width), 1)
    low = (lane < width // 2).astype(f32) * factor
    return low.astype(bf16), (factor - low).astype(bf16)


def stack_heads(pair, halves):
    return jnp.concatenate([pair * halves[0], pair * halves[1]], axis=0)


def one_over_other(pair):
    half = pair.shape[1] // 2
    return jnp.concatenate([pair[:, :half], pair[:, half:]], axis=0)


def column_of(row):
    amount = row.shape[1]
    return jnp.concatenate(
        [
            jnp.broadcast_to(row[:, at : at + 128], (128, 128)).T
            for at in range(0, amount, 128)
        ],
        axis=0,
    )


def hot_from_column(column, amount):
    lane = lax.broadcasted_iota(jnp.int32, column.shape, 1).astype(f32)
    return jnp.concatenate(
        [(lane + float(at) == column).astype(f32).astype(bf16) for at in range(0, amount, 128)],
        axis=1,
    )


def forward_kernel(
    n_tok, per,
    slots_ref, docs_ref, tok_ref, og_ref, wq_ref, bq_ref, bv_ref, wo_ref, bo_ref, g1_ref, s1_ref,
    wu_ref, bu_ref, wd_ref, bd_ref, g2_ref, s2_ref,
    xc_o, gc_o, qkv_o, p_o, ctx_o, r1_o, n1_o, gelu_o, gelup_o, r2_o, back_o, col_o, pos_o,
    xh, gh, xs, gs, xr, gr, hot, note_s, note_r, wq, wo, wu, wd, live_s,
    xc_t, qkv_t, p_t, ctx_t, r1_t, n1_t, gelu_t, gelup_t, r2_t, bo_c, back_t, gc_t, col_t, pos_t,
    load_sem, note_ss, note_rs, x_ss, x_rs, g_ss, g_rs, own_sem, out_sem, last_sem,
):
    rows, width = xh.shape
    ffw = wu.shape[1]
    blocks = rows // BLK
    grp = lax.axis_index("grp")
    me = lax.axis_index("tok")
    order = peer_order(n_tok)

    barrier = pltpu.get_barrier_semaphore()
    for k in order:
        pl.semaphore_signal(barrier, inc=1, device_id=(grp, me ^ k), device_id_type=MESH)

    loads = [
        pltpu.make_async_copy(src, dst, load_sem.at[i])
        for i, (src, dst) in enumerate(
            ((tok_ref, xh), (og_ref, gh), (wq_ref, wq), (wo_ref, wo), (wu_ref, wu), (wd_ref, wd))
        )
    ]
    loads[0].start()

    def note_copy(k):
        return pltpu.make_async_remote_copy(
            src_ref=note_s.at[me ^ k], dst_ref=note_r.at[me], send_sem=note_ss.at[k],
            recv_sem=note_rs.at[k], device_id=(grp, me ^ k), device_id_type=MESH,
        )

    def row_copy(src, dst, ss, rs, k):
        return pltpu.make_async_remote_copy(
            src_ref=src.at[pl.ds(pl.multiple_of((me ^ k) * per, per), per)],
            dst_ref=dst.at[pl.ds(pl.multiple_of(me * per, per), per)],
            send_sem=ss.at[k], recv_sem=rs.at[k], device_id=(grp, me ^ k), device_id_type=MESH,
        )

    slots = slots_ref[...][None, :]
    dest = jnp.right_shift(slots, rows.bit_length() - 1)
    within = jnp.bitwise_and(slots, rows - 1)
    lanes = lax.broadcasted_iota(jnp.int32, (1, rows), 1)
    dest_hot = lax.broadcasted_iota(jnp.int32, (16, rows), 0) == dest
    dest_hot = dest_hot.astype(f32)
    before = lax.broadcasted_iota(jnp.int32, (BLK, rows), 1)
    rank = jnp.zeros((16, rows), f32)
    for b in range(blocks):
        earlier = lax.broadcasted_iota(jnp.int32, (BLK, rows), 0) + b * BLK < before
        rank += dot32(
            dest_hot[:, b * BLK : (b + 1) * BLK].astype(bf16), earlier.astype(f32).astype(bf16)
        )
    rank = jnp.sum(rank * dest_hot, axis=0, keepdims=True).astype(jnp.int32)
    pos = dest * per + rank
    spot = lax.broadcasted_iota(jnp.int32, (BLK, rows), 0)
    chip = lax.div(me * per, BLK)
    loads[0].wait()
    for copy in loads[1:]:
        copy.start()
    for j in range(blocks - 1, -1, -1):
        at = pl.multiple_of((chip ^ j) * BLK, BLK)
        picked = (spot + at == pos).astype(f32).astype(bf16)
        hot[pl.ds(at, BLK), :] = picked
        xs[pl.ds(at, BLK), :] = dot32(picked, xh[...]).astype(bf16)
        if j == blocks - 1:
            pl.semaphore_wait(barrier, n_tok - 1)
        for k in order:
            if k // (BLK // per) == j:
                row_copy(xs, xr, x_ss, x_rs, k).start()
    mine = pl.ds(pl.multiple_of(me * per, per), per)
    own_x = pltpu.make_async_copy(xs.at[mine], xr.at[mine], own_sem.at[0])
    own_x.start()

    pos_t[...] = jnp.broadcast_to(pos, (8, rows))
    start = jnp.int32(0)
    position = lanes + me * rows
    usable = jnp.zeros((1, rows), jnp.int32)
    for i in range(docs_ref.shape[1]):
        length = docs_ref[0, i]
        inside = (position >= start) & (position < start + length)
        usable = jnp.where(inside, 1, usable)
        start = start + jnp.bitwise_and(length + (CLU - 1), -CLU)
    kind = lax.broadcasted_iota(jnp.int32, (16, rows), 0)
    notes = jnp.where(
        kind == 0,
        jnp.right_shift(within, 5),
        jnp.where(kind == 1, jnp.bitwise_and(within, 31), jnp.where(kind == 2, usable, 0)),
    )
    notes = dot_rows(notes.astype(f32).astype(bf16), hot[...]).astype(bf16)
    for d in range(n_tok):
        note_s[d] = notes[:, d * per : (d + 1) * per]
    for k in order:
        note_copy(k).start()
    own_note = pltpu.make_async_copy(note_s.at[me], note_r.at[me], own_sem.at[1])
    own_note.start()
    loads[1].wait()
    for b in range(blocks):
        sl = pl.ds(b * BLK, BLK)
        gs[sl, :] = dot32(hot[sl, :], gh[...]).astype(bf16)
    own_g = pltpu.make_async_copy(gs.at[mine], gr.at[mine], own_sem.at[2])
    own_g.start()

    own_note.wait()
    for k in order:
        note_copy(k).wait_recv()
    got = jnp.concatenate([note_r[d] for d in range(n_tok)], axis=1)
    got32 = got.astype(f32)
    slot_row = got32[0:1, :] * 32.0 + got32[1:2, :]
    col_t[...] = column_of(slot_row)
    slot_row = slot_row.astype(jnp.int32)
    for b in range(blocks):
        spot = lax.broadcasted_iota(jnp.int32, (BLK, rows), 0) + b * BLK
        hot[b * BLK : (b + 1) * BLK, :] = (spot == slot_row).astype(f32).astype(bf16)
    live_s[...] = column_of(dot_rows(got, hot[...])[2:3, :])

    def gather_rows(source, target, own, copy):
        for j in range(blocks):
            if j == 0:
                own.wait()
            for k in range(1, n_tok):
                if k // (BLK // per) == j:
                    copy(k).wait_recv()
            at = pl.multiple_of((chip ^ j) * BLK, BLK)
            for b in range(blocks):
                sl = pl.ds(b * BLK, BLK)
                part = dot32(hot[sl, pl.ds(at, BLK)], source[pl.ds(at, BLK), :]).astype(bf16)
                target[sl, :] = part if j == 0 else target[sl, :] + part

    for k in order:
        row_copy(xs, xr, x_ss, x_rs, k).wait_send()
    for k in order:
        row_copy(gs, gr, g_ss, g_rs, k).start()
    gather_rows(xr, xc_t, own_x, lambda k: row_copy(xs, xr, x_ss, x_rs, k))
    xc_out = pltpu.make_async_copy(xc_t, xc_o, last_sem.at[4])
    xc_out.start()
    for copy in loads[2:]:
        copy.wait()

    halves = lane_halves(2 * width // H)
    scaled = lane_halves(2 * width // H, (width // H) ** (-0.5))
    pair_width = 2 * width // H
    pairs = range(H // 2)
    outs = (
        (qkv_t, qkv_o, BLK), (p_t, p_o, BLK * H // 2), (ctx_t, ctx_o, BLK), (r1_t, r1_o, BLK),
        (n1_t, n1_o, BLK), (gelu_t, gelu_o, BLK), (gelup_t, gelup_o, BLK), (r2_t, r2_o, BLK),
    )

    def out_copy(i, b, slot):
        tile, whole, count = outs[i]
        return pltpu.make_async_copy(
            tile.at[slot], whole.at[pl.ds(pl.multiple_of(b * count, count), count)], out_sem.at[slot, i]
        )

    def block(b, carry):
        slot = lax.rem(b, 2)
        sl = pl.ds(pl.multiple_of(b * BLK, BLK), BLK)

        @pl.when(b >= 2)
        def _():
            for i in range(len(outs)):
                out_copy(i, b - 2, slot).wait()

        x = xc_t[sl, :]
        for part, bias in ((0, row_of(bq_ref)), (1, None), (2, row_of(bv_ref))):
            got_part = dot32(x, wq[:, part * width : (part + 1) * width])
            if bias is not None:
                got_part = got_part + bias
            qkv_t[slot, :, part * width : (part + 1) * width] = got_part.astype(bf16)
        for c in range(BLK // CLU):
            at = pl.multiple_of(b * BLK + c * CLU, CLU)
            live = live_s[pl.ds(at, CLU), :] > 0.5
            live = jnp.concatenate([live, live], axis=1)
            crow = pl.ds(c * CLU, CLU)
            cols = [[pl.ds(part * width + p * pair_width, pair_width) for p in pairs] for part in range(3)]
            q2 = [stack_heads(qkv_t[slot, crow, cols[0][p]], scaled) for p in pairs]
            scores = [jnp.where(live, dot_rows(qkv_t[slot, crow, cols[1][p]], q2[p]), masked_score) for p in pairs]
            expo = [jnp.exp(member - jnp.max(member, axis=0, keepdims=True)) for member in scores]
            weights = [(member / jnp.sum(member, axis=0, keepdims=True)).astype(bf16) for member in expo]
            v2 = [stack_heads(qkv_t[slot, crow, cols[2][p]], halves) for p in pairs]
            context = [dot_cols(one_over_other(weights[p]), v2[p]).astype(bf16) for p in pairs]
            for p in pairs:
                p_t[slot, pl.ds((c * (H // 2) + p) * CLU, CLU), :] = weights[p]
                ctx_t[slot, crow, cols[0][p]] = context[p]
        resid1 = x.astype(f32) + (dot32(ctx_t[slot], wo[...]) + row_of(bo_ref))
        r1_t[slot] = resid1
        hat1, _ = norm_parts(resid1)
        normed1 = hat1 * row_of(g1_ref) + row_of(s1_ref)
        low1 = normed1.astype(bf16)
        n1_t[slot] = low1
        down = None
        step = width
        for j in range(ffw // step):
            cs = pl.ds(j * step, step)
            up = dot32(low1, wu[:, cs]) + bu_ref[cs].astype(f32)[None, :]
            phi = 0.5 * (1.0 + lax.erf(up * 0.7071067811865476))
            slope = phi + up * jnp.exp(up * up * -0.5) * 0.3989422804014327
            act = (up * phi).astype(bf16)
            gelu_t[slot, :, cs] = act
            gelup_t[slot, :, cs] = slope.astype(bf16)
            term = dot32(act, wd[cs, :])
            down = term if down is None else down + term
        resid2 = normed1 + (down + row_of(bd_ref))
        r2_t[slot] = resid2
        hat2, _ = norm_parts(resid2)
        bo_c[sl, :] = (hat2 * row_of(g2_ref) + row_of(s2_ref)).astype(bf16)
        for i in range(len(outs)):
            out_copy(i, b, slot).start()
        return carry

    lax.fori_loop(0, blocks, block, 0)

    col_out = pltpu.make_async_copy(col_t, col_o, last_sem.at[0])
    col_out.start()
    pos_out = pltpu.make_async_copy(pos_t, pos_o, last_sem.at[1])
    pos_out.start()
    for b in range(blocks):
        sl = pl.ds(b * BLK, BLK)
        back_t[sl, :] = dot32(hot_from_column(col_t[sl, :], rows), bo_c[...]).astype(bf16)
    back_out = pltpu.make_async_copy(back_t, back_o, last_sem.at[2])
    back_out.start()
    gather_rows(gr, gc_t, own_g, lambda k: row_copy(gs, gr, g_ss, g_rs, k))
    gc_out = pltpu.make_async_copy(gc_t, gc_o, last_sem.at[3])
    gc_out.start()
    for k in order:
        note_copy(k).wait_send()
        row_copy(gs, gr, g_ss, g_rs, k).wait_send()
    for b in range(max(blocks - 2, 0), blocks):
        for i in range(len(outs)):
            out_copy(i, b, b % 2).wait()
    col_out.wait()
    pos_out.wait()
    back_out.wait()
    gc_out.wait()
    xc_out.wait()


def forward(n_tok, tokens_in, w_qkv, b_query, b_value, w_out, b_out, norm1_gain, norm1_shift,
            w_up, b_up, w_down, b_down, norm2_gain, norm2_shift, out_grad, doc_lengths, cluster_slots):
    rows, width = tokens_in.shape
    ffw = w_up.shape[1]
    per = rows // n_tok
    vm = pl.BlockSpec(memory_space=pltpu.VMEM)
    sm = pl.BlockSpec(memory_space=pltpu.SMEM)
    hb = pl.BlockSpec(memory_space=pl.ANY)
    out_shape = [
        ((rows, width), bf16), ((rows, width), bf16), ((rows, 3 * width), bf16), ((rows * H // 2, 2 * CLU), bf16),
        ((rows, width), bf16), ((rows, width), f32), ((rows, width), bf16), ((rows, ffw), bf16),
        ((rows, ffw), bf16), ((rows, width), f32), ((rows, width), bf16), ((rows, 128), f32),
        ((8, rows), jnp.int32),
    ]
    vmem = pltpu.VMEM
    dma = pltpu.SemaphoreType.DMA
    scratch = (
        [vmem((rows, width), bf16)] * 6
        + [vmem((rows, rows), bf16), vmem((n_tok, 16, per), bf16), vmem((n_tok, 16, per), bf16)]
        + [vmem(w_qkv.shape, bf16), vmem(w_out.shape, bf16), vmem(w_up.shape, bf16), vmem(w_down.shape, bf16)]
        + [vmem((rows, 128), f32)]
        + [
            vmem((rows, width), bf16), vmem((2, BLK, 3 * width), bf16), vmem((2, BLK * H // 2, 2 * CLU), bf16),
            vmem((2, BLK, width), bf16), vmem((2, BLK, width), f32), vmem((2, BLK, width), bf16),
            vmem((2, BLK, ffw), bf16), vmem((2, BLK, ffw), bf16), vmem((2, BLK, width), f32),
            vmem((rows, width), bf16), vmem((rows, width), bf16), vmem((rows, width), bf16),
            vmem((rows, 128), f32), vmem((8, rows), jnp.int32),
        ]
        + [dma((6,))] + [dma((n_tok,))] * 6 + [dma((3,)), dma((2, 8)), dma((5,))]
    )
    return pl.pallas_call(
        functools.partial(forward_kernel, n_tok, per),
        out_shape=[jax.ShapeDtypeStruct(s, d) for s, d in out_shape],
        in_specs=[vm, sm, hb, hb, hb, vm, vm, hb, vm, vm, vm, hb, vm, hb, vm, vm, vm],
        out_specs=[hb] * len(out_shape),
        scratch_shapes=scratch,
        compiler_params=pltpu.CompilerParams(
            collective_id=0, has_side_effects=True, vmem_limit_bytes=60 * 2**20
        ),
        name="layer_forward",
    )(cluster_slots, doc_lengths, tokens_in, out_grad, w_qkv, b_query, b_value, w_out, b_out, norm1_gain,
      norm1_shift, w_up, b_up, w_down, b_down, norm2_gain, norm2_shift)


def grad_kinds(width, ffw, n_tok):
    return ((ffw // n_tok, width), (width // n_tok, ffw), (width // n_tok, width), (width // n_tok, 3 * width))


def backward_kernel(n_tok, per, kinds, *refs):
    (xc_ref, gc_ref, qkv_ref, p_ref, ctx_ref, r1_ref, n1_ref, gelu_ref, gelup_ref, r2_ref, back_ref, col_ref,
     wq_ref, wo_ref, wu_ref, wd_ref, g1_ref, g2_ref) = refs[:18]
    refs = refs[18:]
    bo_got, gt_got, nar_o = refs[:3]
    shares = refs[3:7]
    refs = refs[7:]
    (wq, wo, wu, wd, gwd, gelu, gup, low1, gdown, resid, grow, ctx, gattn, gcl, qkv, probs, land0, col,
     nar_v, bup_v, nar_s, nar_r, nar_g, nar_h, nar_t,
     load_sem, bo_ss, bo_rs, gt_ss, gt_rs, own_sem, s0_ss, s0_rs, x1_ss, x1_rs, x2_ss, x2_rs, za_ss, za_rs,
     zb_ss, zb_rs, ag_ss, ag_rs, fin_sem, free_sem, nt_ss, nt_rs, ng_ss, ng_rs) = refs
    rows, width = low1.shape
    ffw = wu.shape[1]
    blocks = rows // BLK
    grp = lax.axis_index("grp")
    me = lax.axis_index("tok")
    core = lax.rem(me, 2)
    chip = lax.div(me, 2)
    chips = n_tok // 2
    gx = lax.rem(grp, 2)
    gy = lax.div(grp, 2)
    order = peer_order(n_tok)
    mats = (gwd, wu, wo, wq)

    barrier = pltpu.get_barrier_semaphore()
    for k in order:
        pl.semaphore_signal(barrier, inc=1, device_id=(grp, me ^ k), device_id_type=MESH)
    for k in (1, 2, 3):
        pl.semaphore_signal(barrier, inc=1, device_id=(grp ^ k, me), device_id_type=MESH)

    load = {
        name: pltpu.make_async_copy(src, dst, load_sem.at[i])
        for i, (name, src, dst) in enumerate((
            ("gc", gc_ref, gcl), ("r2", r2_ref, resid), ("gelu", gelu_ref, gelu), ("wd", wd_ref, wd),
            ("gelup", gelup_ref, gup), ("wu", wu_ref, wu), ("n1", n1_ref, low1), ("wo", wo_ref, wo),
            ("ctx", ctx_ref, ctx), ("qkv", qkv_ref, qkv), ("p", p_ref, probs), ("wq", wq_ref, wq),
            ("xc", xc_ref, gattn), ("col", col_ref, col), ("r1", r1_ref, resid),
        ))
    }

    def begin(*names):
        for name in names:
            load[name].start()

    def ready(*names):
        for name in names:
            load[name].wait()

    begin("gc", "r2")

    def row_copy(src, dst, ss, rs, k):
        return pltpu.make_async_remote_copy(
            src_ref=src.at[pl.ds(pl.multiple_of((me ^ k) * per, per), per)],
            dst_ref=dst.at[pl.ds(pl.multiple_of(me * per, per), per)],
            send_sem=ss.at[k], recv_sem=rs.at[k], device_id=(grp, me ^ k), device_id_type=MESH,
        )

    mine = pl.ds(pl.multiple_of(me * per, per), per)
    def held(m, z, row0, count, col0, ncols):
        share, _ = kinds[m]
        at = (2 * z + core) * share + row0
        return mats[m].at[pl.ds(pl.multiple_of(at, 16), count), pl.ds(pl.multiple_of(col0, 128), ncols)]

    zones = (land0, gelu, gup, gup)
    zone_col = (0, 0, 3 * width, 0)

    def land(m, row, count, half_at, whole):
        share, cols = kinds[m]
        ncols = cols if whole else cols // 2
        return zones[m].at[pl.ds(row, count), pl.ds(zone_col[m] + half_at * (cols // 2), ncols)]

    def land_s0(m, z):
        share = kinds[m][0]
        return land(m, z * share, share, 0, True)

    def land_x1(m, z):
        share = kinds[m][0]
        if first_x(z):
            return land(m, (chips + z) * share, share, 0, False)
        return land(m, (chips + 2) * share + (z - chips // 2) * (share // 2), share // 2, 0, True)

    def land_x2(m, z):
        share = kinds[m][0]
        return land(m, chips * share + z * (share // 2), share // 2, 1, False)

    def land_za(m, i):
        share = kinds[m][0]
        return land(m, (chips + 3) * share, share // 2, i, False)

    def land_zb(m):
        share = kinds[m][0]
        return land(m, (chips + 3) * share + share // 2, share // 2, 0, False)

    partners = ((grp, me ^ 1), (grp ^ 1, me), (grp ^ 2, me), (grp, me ^ 2), (grp, me ^ 4))

    def tell_free(i):
        for who in partners:
            pl.semaphore_signal(free_sem.at[i], inc=1, device_id=who, device_id_type=MESH)

    def partners_free(i):
        pl.semaphore_wait(free_sem.at[i], len(partners))

    def remote(src, dst, ss, rs, who):
        return pltpu.make_async_remote_copy(
            src_ref=src, dst_ref=dst, send_sem=ss, recv_sem=rs, device_id=who, device_id_type=MESH
        )

    def copy_s0(m, z):
        share, cols = kinds[m]
        at = (2 * z + 1 - core) * share
        return remote(
            mats[m].at[pl.ds(pl.multiple_of(at, 16), share)], land_s0(m, z),
            s0_ss.at[m, z], s0_rs.at[m, z], (grp, me ^ 1),
        )

    def first_x(z):
        return z < chips // 2

    def copy_x1(m, z):
        share, cols = kinds[m]
        half, hcols = share // 2, cols // 2
        if first_x(z):
            src = held(m, z, 0, share, (1 - gx) * hcols, hcols)
            who = (grp ^ 1, me)
        else:
            src = held(m, z, (1 - gy) * half, half, 0, cols)
            who = (grp ^ 2, me)
        return remote(src, land_x1(m, z), x1_ss.at[m, z], x1_rs.at[m, z], who)

    def copy_x2(m, z):
        share, cols = kinds[m]
        half, hcols = share // 2, cols // 2
        if first_x(z):
            src, who = held(m, z, (1 - gy) * half, half, gx * hcols, hcols), (grp ^ 2, me)
        else:
            src, who = held(m, z, gy * half, half, (1 - gx) * hcols, hcols), (grp ^ 1, me)
        return remote(src, land_x2(m, z), x2_ss.at[m, z], x2_rs.at[m, z], who)

    def quarter(m, z):
        share, cols = kinds[m]
        half, hcols = share // 2, cols // 2
        return held(m, z, gy * half, half, gx * hcols, hcols)

    def copy_za(m, i):
        return remote(quarter(m, chip ^ (1 + 2 * i)), land_za(m, i), za_ss.at[m, i], za_rs.at[m, i], (grp, me ^ 2))

    def copy_zb(m):
        return remote(quarter(m, chip ^ 2), land_zb(m), zb_ss.at[m], zb_rs.at[m], (grp, me ^ 4))

    def share_part(m):
        share, cols = kinds[m]
        half, hcols = share // 2, cols // 2
        return shares[m].at[
            pl.ds(pl.multiple_of(gy * half, 16), half), pl.ds(pl.multiple_of(gx * hcols, 128), hcols)
        ]

    def own_part(m):
        return quarter(m, chip)

    def copy_ag(m, k):
        return remote(own_part(m), share_part(m), ag_ss.at[m, k], ag_rs.at[m, k], (grp ^ k, me))

    def own_ag(m):
        return pltpu.make_async_copy(own_part(m), share_part(m), fin_sem.at[m])

    def add_in(target, extra):
        target[...] = target[...] + extra[...]

    turns = (0, 2, 1, 3)

    def start_s0(m):
        for z in turns:
            copy_s0(m, z).start()

    def step_r0(m, zs=turns):
        share, cols = kinds[m]
        for z in zs:
            copy_s0(m, z).wait_recv()
            add_in(held(m, z, 0, share, 0, cols), land_s0(m, z))
            copy_x1(m, z).start()

    def step_r1(m, zs=turns):
        share, cols = kinds[m]
        half, hcols = share // 2, cols // 2
        for z in zs:
            copy_x1(m, z).wait_recv()
            spot = (0, share, gx * hcols, hcols) if first_x(z) else (gy * half, half, 0, cols)
            add_in(held(m, z, *spot), land_x1(m, z))
            copy_x2(m, z).start()

    def step_r2(m):
        for z in turns:
            copy_x2(m, z).wait_recv()
            add_in(quarter(m, z), land_x2(m, z))
        copy_za(m, 0).start()
        copy_za(m, 1).start()

    def step_ra(m):
        copy_za(m, 0).wait_recv()
        copy_za(m, 1).wait_recv()
        add_in(quarter(m, chip ^ 2), land_za(m, 1))
        copy_zb(m).start()
        add_in(own_part(m), land_za(m, 0))

    def step_rb(m):
        copy_zb(m).wait_recv()
        add_in(own_part(m), land_zb(m))
        for k in (3, 1, 2):
            copy_ag(m, k).start()
        own_ag(m).start()

    gain2 = row_of(g2_ref)
    gain1 = row_of(g1_ref)

    def norm_back(upstream, resid_rows, gain):
        hat, rstd = norm_parts(resid_rows)
        dh = upstream * gain
        inner = jnp.mean(dh * hat, axis=-1, keepdims=True)
        return rstd * (dh - jnp.mean(dh, axis=-1, keepdims=True) - hat * inner), hat

    def add_sum(at, values):
        nar_v[at : at + 1, :] += jnp.sum(values, axis=0, keepdims=True)

    nar_v[...] = jnp.zeros_like(nar_v)
    bup_v[...] = jnp.zeros_like(bup_v)
    own_bo = pltpu.make_async_copy(back_ref.at[mine], bo_got.at[mine], own_sem.at[0])
    ready("gc", "r2")
    begin("gelu", "wd", "gelup")
    for b in range(blocks):
        sl = pl.ds(b * BLK, BLK)
        g = gcl[sl, :].astype(f32)
        back, hat = norm_back(g, resid[sl, :], gain2)
        low = back.astype(bf16)
        grow[sl, :] = back
        gdown[sl, :] = low
        add_sum(5, low.astype(f32))
        add_sum(6, g * hat)
        add_sum(7, g)
        if b == 0:
            pl.semaphore_wait(barrier, n_tok - 1 + 3)
            for k in order:
                row_copy(back_ref, bo_got, bo_ss, bo_rs, k).start()
            own_bo.start()

    ready("gelu")
    begin("wu", "r1", "wo", "n1", "ctx")
    step = width
    for j in turns:
        cs = pl.ds(j * step, step)
        gwd[cs, :] = dot_cols(gelu[:, cs], gdown[...]).astype(bf16)
        copy_s0(0, j).start()
    tell_free(0)
    ready("wd", "gelup")
    step_r0(0, turns[:2])
    for b in range(blocks):
        sl = pl.ds(b * BLK, BLK)
        for j in range(ffw // step):
            cs = pl.ds(j * step, step)
            up = (dot_rows(gdown[sl, :], wd[cs, :]) * gup[sl, cs].astype(f32)).astype(bf16)
            gup[sl, cs] = up
            bup_v[0:1, cs] += jnp.sum(up.astype(f32), axis=0, keepdims=True)
        if b == 1:
            step_r0(0, turns[2:])
    begin("qkv", "p", "wq", "col")
    ready("wu", "n1")
    for b in range(blocks):
        sl = pl.ds(b * BLK, BLK)
        grow[sl, :] += dot_rows(gup[sl, :], wu[...])
    for j in range(ffw // step):
        cs = pl.ds(j * step, step)
        wu[:, cs] = dot_cols(low1[...], gup[:, cs]).astype(bf16)
        if j == 0:
            step_r1(0, turns[:2])
        elif j == 2:
            step_r1(0, turns[2:])
    tell_free(1)
    partners_free(0)
    start_s0(1)
    ready("r1", "wo", "ctx")
    for b in range(blocks):
        sl = pl.ds(b * BLK, BLK)
        gn1 = grow[sl, :]
        back, hat = norm_back(gn1, resid[sl, :], gain1)
        low = back.astype(bf16)
        grow[sl, :] = back
        gattn[sl, :] = low
        add_sum(2, low.astype(f32))
        add_sum(3, gn1 * hat)
        add_sum(4, gn1)
        gcl[sl, :] = dot_rows(low, wo[...]).astype(bf16)
        if b == 2:
            step_r0(1, turns[:2])
    wo[...] = dot_cols(ctx[...], gattn[...]).astype(bf16)
    begin("xc")
    partners_free(1)
    start_s0(2)
    step_r0(1, turns[2:])
    step_r2(0)

    ready("qkv", "p", "wq")
    halves = lane_halves(2 * width // H)
    pair_width = 2 * width // H
    scaled = lane_halves(2 * width // H, (width // H) ** (-0.5))
    pairs = range(H // 2)

    def attend(b):
        for c in range(BLK // CLU):
            crow = pl.ds(b * BLK + c * CLU, CLU)
            cols = [[pl.ds(part * width + p * pair_width, pair_width) for p in pairs] for part in range(3)]
            first = (b * BLK // CLU + c) * (H // 2)
            go = [stack_heads(gcl[crow, cols[0][p]], halves) for p in pairs]
            gp = [dot_rows(qkv[crow, cols[2][p]], go[p]) for p in pairs]
            weights = [probs[pl.ds((first + p) * CLU, CLU), :] for p in pairs]
            gv = [dot32(weights[p], go[p]).astype(bf16) for p in pairs]
            wide = [member.astype(f32) for member in weights]
            dots = [jnp.sum(gp[p] * wide[p], axis=0, keepdims=True) for p in pairs]
            gs = [(wide[p] * (gp[p] - dots[p])).astype(bf16) for p in pairs]
            q2 = [stack_heads(qkv[crow, cols[0][p]], scaled) for p in pairs]
            k2 = [stack_heads(qkv[crow, cols[1][p]], scaled) for p in pairs]
            gk = [dot32(gs[p], q2[p]).astype(bf16) for p in pairs]
            gq = [dot_cols(one_over_other(gs[p]), k2[p]).astype(bf16) for p in pairs]
            for p in pairs:
                qkv[crow, cols[0][p]] = gq[p]
                qkv[crow, cols[1][p]] = gk[p]
                qkv[crow, cols[2][p]] = gv[p]
        sl = pl.ds(b * BLK, BLK)
        add_sum(0, qkv[sl, 0:width].astype(f32))
        add_sum(1, qkv[sl, 2 * width :].astype(f32))
        total = grow[sl, :] + dot_rows(qkv[sl, :], wq[...])
        low1[sl, :] = total.astype(bf16)

    attend(0)
    step_r0(2)
    attend(1)
    step_ra(0)
    attend(2)
    step_r1(1, turns[:2])
    attend(3)
    step_r1(1, turns[2:])
    ready("xc", "col")
    for b in range(blocks):
        sl = pl.ds(b * BLK, BLK)
        gdown[sl, :] = dot32(hot_from_column(col[sl, :], rows), low1[...]).astype(bf16)
    def send_home(*who):
        for k in who:
            row_copy(gdown, gt_got, gt_ss, gt_rs, k).start()

    send_home(7, 6, 1)
    own_gt = pltpu.make_async_copy(gdown.at[mine], gt_got.at[mine], own_sem.at[1])
    own_gt.start()
    step_rb(0)
    for j in range(3):
        cs = pl.ds(j * step, step)
        wq[:, cs] = dot_cols(gattn[...], qkv[:, cs]).astype(bf16)
    start_s0(3)
    step_r1(2)

    each = width // n_tok
    at = lax.broadcasted_iota(jnp.int32, (width, n_tok * 128), 0)
    lane = lax.broadcasted_iota(jnp.int32, (width, n_tok * 128), 1)
    inner = jnp.bitwise_and(lane, 127)
    pick = (at == jnp.right_shift(lane, 7) * each + inner) & (inner < each)
    spread = jnp.dot(nar_v[...], pick.astype(f32), precision=lax.Precision.HIGHEST, preferred_element_type=f32)
    share_up = ffw // n_tok
    for d in range(n_tok):
        nar_s[d] = jnp.concatenate(
            [spread[0:8, d * 128 : (d + 1) * 128]]
            + [bup_v[0:1, d * share_up + i : d * share_up + i + 128] for i in range(0, share_up, 128)]
            + [jnp.zeros((8 - share_up // 128, 128), f32)], axis=0)

    def nar_copy(k):
        return remote(nar_s.at[me ^ k], nar_r.at[k], nt_ss.at[k], nt_rs.at[k], (grp, me ^ k))

    def nar_cross(k):
        return remote(nar_g, nar_h.at[k], ng_ss.at[k], ng_rs.at[k], (grp ^ k, me))

    for k in order:
        nar_copy(k).start()
    step_r2(1)
    step_r0(3)
    step_r2(2)
    step_r1(3, turns[:2])
    step_ra(1)
    step_ra(2)
    send_home(5, 3, 2)
    step_r1(3, turns[2:])
    step_rb(1)
    step_rb(2)
    total = nar_s[me]
    for k in order:
        nar_copy(k).wait_recv()
        total += nar_r[k]
    nar_g[...] = total
    for k in (3, 1, 2):
        nar_cross(k).start()
    step_r2(3)
    total = nar_g[...]
    for k in (1, 2, 3):
        nar_cross(k).wait_recv()
        total += nar_h[k]
    nar_t[...] = total
    nar_out = pltpu.make_async_copy(nar_t, nar_o, own_sem.at[2])
    nar_out.start()
    step_ra(3)
    send_home(4,)
    step_rb(3)

    own_bo.wait()
    own_gt.wait()
    nar_out.wait()
    for k in order:
        row_copy(back_ref, bo_got, bo_ss, bo_rs, k).wait()
        row_copy(gdown, gt_got, gt_ss, gt_rs, k).wait()
        nar_copy(k).wait_send()
    for k in (1, 2, 3):
        nar_cross(k).wait_send()
    for m in range(4):
        own_ag(m).wait()
        for z in range(chips):
            copy_s0(m, z).wait_send()
            copy_x1(m, z).wait_send()
            copy_x2(m, z).wait_send()
        copy_za(m, 0).wait_send()
        copy_za(m, 1).wait_send()
        copy_zb(m).wait_send()
        for k in (1, 2, 3):
            copy_ag(m, k).wait()


def backward(n_tok, saved, w_qkv, w_out, w_up, w_down, norm1_gain, norm2_gain):
    rows, width = saved[0].shape
    ffw = w_up.shape[1]
    per = rows // n_tok
    chips = n_tok // 2
    kinds = grad_kinds(width, ffw, n_tok)
    vm = pl.BlockSpec(memory_space=pltpu.VMEM)
    hb = pl.BlockSpec(memory_space=pl.ANY)
    outs = [((rows, width), bf16), ((rows, width), bf16), ((16, 128), f32)]
    outs += [(kind, bf16) for kind in kinds]
    vmem = pltpu.VMEM
    dma = pltpu.SemaphoreType.DMA
    scratch = [
        vmem(w_qkv.shape, bf16), vmem(w_out.shape, bf16), vmem(w_up.shape, bf16), vmem(w_down.shape, bf16),
        vmem(w_down.shape, bf16), vmem((rows, ffw), bf16), vmem((rows, ffw), bf16), vmem((rows, width), bf16),
        vmem((rows, width), bf16), vmem((rows, width), f32), vmem((rows, width), f32), vmem((rows, width), bf16),
        vmem((rows, width), bf16), vmem((rows, width), bf16), vmem((rows, 3 * width), bf16),
        vmem((rows * H // 2, 2 * CLU), bf16), vmem(w_down.shape, bf16), vmem((rows, 128), f32),
        vmem((16, width), f32), vmem((8, ffw), f32), vmem((n_tok, 16, 128), f32), vmem((n_tok, 16, 128), f32),
        vmem((16, 128), f32), vmem((4, 16, 128), f32), vmem((16, 128), f32),
        dma((15,)), dma((n_tok,)), dma((n_tok,)), dma((n_tok,)), dma((n_tok,)), dma((3,)),
    ]
    scratch += [dma((4, chips))] * 6 + [dma((4, 2))] * 2 + [dma((4,))] * 2
    scratch += [dma((4, 4))] * 2 + [dma((4,)), pltpu.SemaphoreType.REGULAR((2,))]
    scratch += [dma((n_tok,))] * 2 + [dma((4,))] * 2
    return pl.pallas_call(
        functools.partial(backward_kernel, n_tok, per, kinds),
        out_shape=[jax.ShapeDtypeStruct(s, d) for s, d in outs],
        in_specs=[hb] * 16 + [vm] * 2,
        out_specs=[hb] * len(outs),
        scratch_shapes=scratch,
        compiler_params=pltpu.CompilerParams(
            collective_id=1, has_side_effects=True, vmem_limit_bytes=63 * 2**20
        ),
        name="layer_backward",
    )(*saved, w_qkv, w_out, w_up, w_down, norm1_gain, norm2_gain)[:7]


def finish_kernel(
    pos_ref, nar_ref, bo_ref, gt_ref, wd_ref, wu_ref, wo_ref, wq_ref,
    out_o, tok_o, wq_o, wo_o, wu_o, wd_o, bq_o, bv_o, b_out_o, g1_o, s1_o, bu_o, bd_o, g2_o, s2_o,
    bo, gt, wd, wu, wo, wq, out_t, tok_t, wd_t, wu_t, wo_t, wq_t, in_sem, out_sem, row_sem,
):
    rows = bo.shape[0]
    ins = [
        pltpu.make_async_copy(src, dst, in_sem.at[i])
        for i, (src, dst) in enumerate(
            ((bo_ref, bo), (gt_ref, gt), (wd_ref, wd), (wu_ref, wu), (wq_ref, wq), (wo_ref, wo))
        )
    ]
    for copy in ins:
        copy.start()
    outs = []
    column = column_of(pos_ref[0:1, :].astype(f32))
    home = [hot_from_column(column[b * BLK : (b + 1) * BLK], rows) for b in range(rows // BLK)]

    def widen(i, src, dst, whole):
        ins[i].wait()
        dst[...] = src[...].astype(f32)
        outs.append(pltpu.make_async_copy(dst, whole, out_sem.at[i - 2]))
        outs[-1].start()

    def bring(i, got, tile, whole):
        ins[i].wait()
        for b in range(rows // BLK):
            sl = pl.ds(b * BLK, BLK)
            tile[sl, :] = dot32(home[b], got[...]).astype(bf16)
            outs.append(pltpu.make_async_copy(tile.at[sl], whole.at[sl], row_sem.at[i, b]))
            outs[-1].start()

    bring(0, bo, out_t, out_o)
    widen(2, wd, wd_t, wd_o)
    widen(3, wu, wu_t, wu_o)
    widen(4, wq, wq_t, wq_o)
    widen(5, wo, wo_t, wo_o)
    bring(1, gt, tok_t, tok_o)
    for i, dst in enumerate((bq_o, bv_o, b_out_o, g1_o, s1_o, bd_o, g2_o, s2_o)):
        dst[...] = nar_ref[i, 0 : dst.shape[0]]
    for i in range(bu_o.shape[0] // 128):
        bu_o[i * 128 : (i + 1) * 128] = nar_ref[8 + i, :]
    for copy in outs:
        copy.wait()


def finish(pos, got):
    bo, gt, nar, wd, wu, wo, wq = got
    rows, width = bo.shape
    each = wq.shape[0]
    vm = pl.BlockSpec(memory_space=pltpu.VMEM)
    hb = pl.BlockSpec(memory_space=pl.ANY)
    outs = [(bo.shape, bf16), (gt.shape, bf16), (wq.shape, f32), (wo.shape, f32), (wu.shape, f32), (wd.shape, f32)]
    outs += [((each,), f32)] * 5 + [((wd.shape[0],), f32)] + [((each,), f32)] * 3
    vmem = pltpu.VMEM
    scratch = [vmem(member.shape, bf16) for member in (bo, gt, wd, wu, wo, wq, bo, gt)]
    scratch += [vmem(member.shape, f32) for member in (wd, wu, wo, wq)]
    scratch += [pltpu.SemaphoreType.DMA((6,)), pltpu.SemaphoreType.DMA((4,)), pltpu.SemaphoreType.DMA((2, rows // BLK))]
    (out, tok, g_wq, g_wo, g_wu, g_wd, bq, bv, b_out, g1, s1, bu, bd, g2, s2) = pl.pallas_call(
        finish_kernel,
        out_shape=[jax.ShapeDtypeStruct(s, d) for s, d in outs],
        in_specs=[vm] * 2 + [hb] * 6,
        out_specs=[hb] * 6 + [vm] * 9,
        scratch_shapes=scratch,
        compiler_params=pltpu.CompilerParams(vmem_limit_bytes=60 * 2**20),
        name="back_home",
    )(pos, nar, bo, gt, wd, wu, wo, wq)
    return out, tok, g_wq, bq, bv, g_wo, b_out, g1, s1, g_wu, bu, g_wd, bd, g2, s2


def per_device_fast(
    tokens_in, w_qkv, b_query, b_value, w_out, b_out, norm1_gain, norm1_shift,
    w_up, b_up, w_down, b_down, norm2_gain, norm2_shift, out_grad, doc_lengths, cluster_slots,
):
    n_tok = lax.axis_size("tok")
    *saved, pos = forward(
        n_tok, tokens_in, w_qkv, b_query, b_value, w_out, b_out, norm1_gain, norm1_shift,
        w_up, b_up, w_down, b_down, norm2_gain, norm2_shift, out_grad, doc_lengths, cluster_slots)
    got = backward(n_tok, saved, w_qkv, w_out, w_up, w_down, norm1_gain, norm2_gain)
    return tuple(finish(pos, got))


def norm_rows(values, scales, shifts):
    centre = values - jnp.mean(values, axis=-1, keepdims=True)
    spread = jnp.mean(centre * centre, axis=-1, keepdims=True)
    return centre * lax.rsqrt(spread + eps) * scales + shifts


def gelu_exact(values):
    return jax.nn.gelu(values, approximate=False)


def valid_tokens(lengths_row, offset, amount, cluster):
    padded = (lengths_row + cluster - 1) // cluster * cluster
    starts = jnp.cumsum(padded) - padded
    position = offset + jnp.arange(amount, dtype=jnp.int32)
    inside = (position[:, None] >= starts[None, :]) & (
        position[:, None] < (starts + lengths_row)[None, :]
    )
    return jnp.any(inside, axis=1)


def move(one_hot, rows):
    return dot32(one_hot, rows).astype(jnp.bfloat16)


def move_back(one_hot, rows):
    picked = jnp.einsum("pi,pd->id", one_hot, rows, preferred_element_type=jnp.float32)
    return picked.astype(jnp.bfloat16)


def exchange(rows):
    return lax.all_to_all(rows, "tok", split_axis=0, concat_axis=0, tiled=True)


def per_device(
    tokens_in, w_qkv, b_query, b_value, w_out, b_out, norm1_gain, norm1_shift,
    w_up, b_up, w_down, b_down, norm2_gain, norm2_shift, out_grad, doc_lengths, cluster_slots,
):
    tok_dev, width = tokens_in.shape
    head_size = width // H
    clusters = tok_dev // CLU
    n_tok = lax.axis_size("tok")
    per_peer = tok_dev // n_tok
    my_index = lax.axis_index("tok")
    f32 = jnp.float32

    usable = valid_tokens(doc_lengths[0], my_index * tok_dev, tok_dev, CLU)
    dest = cluster_slots // tok_dev
    dest_hot = (dest[:, None] == jnp.arange(n_tok)[None, :]).astype(jnp.int32)
    rank = jnp.sum((jnp.cumsum(dest_hot, axis=0) - dest_hot) * dest_hot, axis=1)
    send_pos = dest * per_peer + rank
    send_hot = (jnp.arange(tok_dev)[:, None] == send_pos[None, :])
    note = (cluster_slots % tok_dev) * 2 + usable.astype(jnp.int32)
    sent_note = jnp.sum(jnp.where(send_hot, note[None, :], 0), axis=1)
    send_hot = send_hot.astype(jnp.bfloat16)
    got_note = exchange(sent_note)
    x_got = exchange(move(send_hot, tokens_in))
    g_got = exchange(move(send_hot, out_grad))
    place_hot = jnp.arange(tok_dev)[:, None] == (got_note // 2)[None, :]
    key_live = jnp.sum(jnp.where(place_hot, got_note[None, :] % 2, 0), axis=1) > 0
    place_hot = place_hot.astype(jnp.bfloat16)
    x = move(place_hot, x_got)

    bias_qkv = jnp.concatenate(
        [b_query.astype(f32), jnp.zeros((width,), f32), b_value.astype(f32)]
    )
    qkv = (dot32(x, w_qkv) + bias_qkv).astype(jnp.bfloat16)
    packed = qkv.reshape(clusters, CLU, 3, H, head_size)
    query, keys, value = packed[:, :, 0], packed[:, :, 1], packed[:, :, 2]
    scale = head_size ** (-0.5)
    scores = jnp.einsum("bqhd,bkhd->bhqk", query, keys, preferred_element_type=f32) * scale
    scores = jnp.where(key_live.reshape(clusters, 1, 1, CLU), scores, masked_score)
    expo = jnp.exp(scores - jnp.max(scores, axis=-1, keepdims=True))
    probs = expo / jnp.sum(expo, axis=-1, keepdims=True)
    weights = probs.astype(jnp.bfloat16)
    context = jnp.einsum("bhqk,bkhd->bqhd", weights, value, preferred_element_type=f32)
    context = context.astype(jnp.bfloat16).reshape(tok_dev, width)

    resid1 = x.astype(f32) + dot32(context, w_out) + b_out.astype(f32)
    normed1, norm1_back = jax.vjp(
        norm_rows, resid1, norm1_gain.astype(f32), norm1_shift.astype(f32)
    )
    normed1_low = normed1.astype(jnp.bfloat16)
    up_pre = dot32(normed1_low, w_up) + b_up.astype(f32)
    gelu_out, gelu_back = jax.vjp(gelu_exact, up_pre)
    gelu_low = gelu_out.astype(jnp.bfloat16)
    down_out = dot32(gelu_low, w_down) + b_down.astype(f32)
    normed2, norm2_back = jax.vjp(
        norm_rows, normed1 + down_out, norm2_gain.astype(f32), norm2_shift.astype(f32)
    )
    out_got = exchange(move_back(place_hot, normed2.astype(jnp.bfloat16)))
    block_out = move_back(send_hot, out_got)

    g = move(place_hot, g_got)
    grad_resid2, grad_gain2, grad_shift2 = norm2_back(g.astype(f32))
    grad_down = grad_resid2.astype(jnp.bfloat16)
    grad_b_down = jnp.sum(grad_down.astype(f32), axis=0)
    grad_w_down = jnp.einsum("nf,nd->fd", gelu_low, grad_down, preferred_element_type=f32)
    grad_gelu = jnp.einsum("nd,fd->nf", grad_down, w_down, preferred_element_type=f32)
    grad_up = gelu_back(grad_gelu)[0].astype(jnp.bfloat16)
    grad_b_up = jnp.sum(grad_up.astype(f32), axis=0)
    grad_w_up = jnp.einsum("nd,nf->df", normed1_low, grad_up, preferred_element_type=f32)
    grad_normed1 = grad_resid2 + jnp.einsum(
        "nf,df->nd", grad_up, w_up, preferred_element_type=f32
    )
    grad_resid1, grad_gain1, grad_shift1 = norm1_back(grad_normed1)
    grad_attn = grad_resid1.astype(jnp.bfloat16)
    grad_b_out = jnp.sum(grad_attn.astype(f32), axis=0)
    grad_w_out = jnp.einsum("nd,ne->de", context, grad_attn, preferred_element_type=f32)
    grad_context = jnp.einsum("ne,de->nd", grad_attn, w_out, preferred_element_type=f32)
    grad_context = grad_context.astype(jnp.bfloat16).reshape(clusters, CLU, H, head_size)

    grad_probs = jnp.einsum("bqhd,bkhd->bhqk", grad_context, value, preferred_element_type=f32)
    row_dot = jnp.sum(grad_probs * probs, axis=-1, keepdims=True)
    grad_scores = (probs * (grad_probs - row_dot)).astype(jnp.bfloat16)
    grad_q = jnp.einsum("bhqk,bkhd->bqhd", grad_scores, keys, preferred_element_type=f32) * scale
    grad_k = jnp.einsum("bhqk,bqhd->bkhd", grad_scores, query, preferred_element_type=f32) * scale
    grad_v = jnp.einsum("bhqk,bqhd->bkhd", weights, grad_context, preferred_element_type=f32)
    grad_qkv = jnp.stack([grad_q, grad_k, grad_v], axis=2).astype(jnp.bfloat16)
    grad_qkv = grad_qkv.reshape(tok_dev, 3 * width)
    grad_total = grad_resid1 + jnp.einsum(
        "ne,de->nd", grad_qkv, w_qkv, preferred_element_type=f32
    )
    back_got = exchange(move_back(place_hot, grad_total.astype(jnp.bfloat16)))
    grad_tokens = move_back(send_hot, back_got)
    grad_w_qkv = jnp.einsum("nd,ne->de", x, grad_qkv, preferred_element_type=f32)
    grad_qkv_sum = jnp.sum(grad_qkv.astype(f32), axis=0)

    low = jnp.bfloat16
    wide = jnp.concatenate(
        [
            grad_w_qkv.astype(low), grad_w_out.astype(low), grad_w_up.astype(low),
            grad_w_down.astype(low).reshape(width, -1),
        ],
        axis=1,
    )
    narrow = jnp.concatenate(
        [
            member.reshape(n_tok, -1)
            for member in (
                grad_qkv_sum[:width], grad_qkv_sum[2 * width :], grad_b_out, grad_gain1,
                grad_shift1, grad_b_down, grad_gain2, grad_shift2, grad_b_up,
            )
        ],
        axis=1,
    )
    share = lax.psum_scatter(wide, "tok", scatter_dimension=0, tiled=True)
    share = lax.psum(share, "grp").astype(f32)
    narrow = lax.psum(narrow, ("grp", "tok"))
    mine = lax.dynamic_index_in_dim(narrow, my_index, 0, keepdims=False)
    step = width // n_tok
    parts = [mine[i * step : (i + 1) * step] for i in range(8)] + [mine[8 * step :]]
    ffw = w_up.shape[1]
    return (
        block_out,
        grad_tokens,
        share[:, : 3 * width],
        parts[0],
        parts[1],
        share[:, 3 * width : 4 * width],
        parts[2],
        parts[3],
        parts[4],
        share[:, 4 * width : 4 * width + ffw],
        parts[8],
        share[:, 4 * width + ffw :].reshape(ffw // n_tok, width),
        parts[5],
        parts[6],
        parts[7],
    )


def solution(mesh):
    n_tok = mesh.shape["tok"]

    def body(*args):
        fits = n_tok == 8 and mesh.shape["grp"] == 4 and args[0].shape[0] == 1024
        return (per_device_fast if fits else per_device)(*args)

    rows = P(("grp", "tok"), None)
    in_specs = (rows,) + (P(),) * 13 + (rows, P("grp", None), P(("grp", "tok")))
    shares = (
        P("tok", None), P("tok"), P("tok"), P("tok", None), P("tok"), P("tok"), P("tok"),
        P("tok", None), P("tok"), P("tok", None), P("tok"), P("tok"), P("tok"),
    )
    return jax.shard_map(
        body, mesh=mesh, in_specs=in_specs, out_specs=(rows, rows) + shares, check_vma=False
    )
```
